32 devices in a mesh: section: 2 (over core), ctx: 4 (over y, x), fsdp: 4 (over z).
Axes of the slice: x: 2, y: 2, z: 4, core: 2. Of those that a mesh axis runs over, the one named last changes fastest.
Arguments:
- stream_in: bfloat16 [2, 4, 2, 512, 1024], P('section', 'fsdp', None, 'ctx'), may hold values from -6 to 6
- lengths: int32 [4, 2, 3], P('fsdp'), may hold values from 1 to 256, 512 in all within a row
- dealing: int32 [4, 2, 512], P('fsdp'), may hold values from 0 to 511, each once within a row
- attention_gain: float32 [2, 1024], P('section', 'fsdp'), may hold values from 0.25 to 1.75
- query_weight: float32 [2, 1024, 2048], P('section', 'fsdp'), may hold values from -0.1875 to 0.1875
- key_weight: float32 [2, 1024, 1024], P('section', 'fsdp'), may hold values from -0.1875 to 0.1875
- value_weight: float32 [2, 1024, 1024], P('section', 'fsdp'), may hold values from -0.1875 to 0.1875
- query_gain: float32 [2, 128], P('section', 'fsdp'), may hold values from 0.25 to 1.75
- key_gain: float32 [2, 128], P('section', 'fsdp'), may hold values from 0.25 to 1.75
- out_weight: float32 [2, 2048, 1024], P('section', 'fsdp'), may hold values from -1 to 1
- mlp_gain: float32 [2, 1024], P('section', 'fsdp'), may hold values from 0.25 to 1.75
- gate_weight: float32 [2, 1024, 3072], P('section', 'fsdp'), may hold values from -0.1875 to 0.1875
- up_weight: float32 [2, 1024, 3072], P('section', 'fsdp'), may hold values from -0.1875 to 0.1875
- down_weight: float32 [2, 3072, 1024], P('section', 'fsdp'), may hold values from -0.109375 to 0.109375
Outputs:
- boundary: bfloat16 [2, 4, 2, 512, 1024], P('section', 'fsdp', None, 'ctx')
- grad_attention_gain: float32 [2, 1024], P('section', 'fsdp')
- grad_query: float32 [2, 1024, 2048], P('section', 'fsdp')
- grad_key: float32 [2, 1024, 1024], P('section', 'fsdp')
- grad_value: float32 [2, 1024, 1024], P('section', 'fsdp')
- grad_query_gain: float32 [2, 128], P('section', 'fsdp')
- grad_key_gain: float32 [2, 128], P('section', 'fsdp')
- grad_out: float32 [2, 2048, 1024], P('section', 'fsdp')
- grad_mlp_gain: float32 [2, 1024], P('section', 'fsdp')
- grad_gate: float32 [2, 1024, 3072], P('section', 'fsdp')
- grad_up: float32 [2, 1024, 3072], P('section', 'fsdp')
- grad_down: float32 [2, 3072, 1024], P('section', 'fsdp')
The draws below stay inside these ranges and needn't reach their ends.
Inputs may be any that keep to these rules, and one draw needn't show every extreme that they name: Each row holds the lengths of 3 sequences packed in order that fill the 512 tokens of one micro-batch; the longest is exactly 256. `dealing`: each row is a permutation of the 512 natural indices of a micro-batch.
All inputs are finite; a program needn't handle non-finite values.
Results may differ from the reference program's by a relative error of at most 0.028.
Values may be sent and summed in bfloat16 or wider, within the bound.
No kernel may reach another device: no remote copies, remote signals or barrier semaphores. Data moves between devices by JAX's collectives and lax.ppermute only.
A program may use at most 192 MiB of HBM per device.

```python
import math
from functools import partial
import jax
import jax.numpy as jnp
import numpy as np
from jax import lax

D = 1024
HEADS = 16
KV_HEADS = 8
HEAD_DIM = 128
FF = 3072
MICRO = 2
SEQS = 3
SECTIONS = 2
GROUPS = 4
PACK = 512
LONGEST = 256


def levels(key, dims, split, least, top_value):
    level = 1.0
    for axis_at, parts in split:
        steps = jax.random.uniform(jax.random.fold_in(jax.random.fold_in(key, 6), axis_at), (parts,), jnp.float32, least / len(split), top_value / len(split))
        level = level * jnp.repeat(jnp.exp(steps), dims[axis_at] // parts).reshape((-1,) + (1,) * (len(dims) - 1 - axis_at))
    return level


def split_up(number_of, total, reach, lean):
    weights = [(1 << 20) // math.isqrt(standing ** lean) + 1 for standing in range(2, number_of + 1)]
    rest, counts = total - reach - (number_of - 1), [1] * (number_of - 1)
    while rest > 0:
        candidates = [i for i in range(number_of - 1) if counts[i] < reach]
        mass, left = sum([weights[i] for i in candidates]), rest
        for i in candidates:
            more = min(reach - counts[i], max(1, left * weights[i] // mass), rest)
            counts[i] = counts[i] + more
            rest = rest - more
    return np.array([reach] + counts)


def uneven(key, amount, total, limit, slope):
    if amount == 2:
        one = jax.random.randint(key, (), max(1, total - limit), min(limit, total - 1) + 1)
        return jnp.stack([one, total - one])
    tallies = jnp.asarray(split_up(amount, total, limit, slope), jnp.int32)
    twos = (amount - 1) // 2
    giver, taker = tallies[1:1 + 2 * twos:2], tallies[2:2 + 2 * twos:2]
    margin = jnp.minimum(giver - 1, limit - taker)
    moved = jax.random.randint(jax.random.fold_in(key, 1), (twos,), 0, 1 << 20) % (margin + 1)
    tallies = tallies.at[1:1 + 2 * twos:2].set(giver - moved).at[2:2 + 2 * twos:2].set(taker + moved)
    return tallies[jax.random.permutation(jax.random.fold_in(key, 2), amount)]


def scatter_about(rng, extent, scale, most, cuts=(), held_as=jnp.bfloat16):
    level = levels(rng, extent, cuts, -0.22, 0.18) if cuts else 1.0
    result = jax.random.normal(rng, extent, jnp.float32) * scale * level
    return jnp.minimum(jnp.maximum(result, -most), most).astype(held_as)


def setup_inputs(seed: int = 0) -> dict:
    seeds = jax.random.split(jax.random.key(seed), 15)
    return {
        "stream_in": scatter_about(seeds[0], (2, GROUPS, MICRO, PACK, D), 1.0, 6.0, ((0, 2), (1, 4), (3, 4))),
        "lengths": jax.vmap(lambda own: uneven(own, SEQS, PACK, LONGEST, 2))(jax.random.split(seeds[1], GROUPS * MICRO)).reshape((GROUPS, MICRO, SEQS)).astype(jnp.int32),
        "dealing": jax.vmap(lambda own: jax.random.permutation(own, PACK))(jax.random.split(seeds[2], GROUPS * MICRO)).reshape((GROUPS, MICRO, PACK)).astype(jnp.int32),
        "attention_gain": jnp.clip(1.0 + 0.15 * jax.random.normal(seeds[3], (SECTIONS, D), jnp.float32), 0.25, 1.75),
        "query_weight": scatter_about(seeds[4], (SECTIONS, D, HEADS * HEAD_DIM), D ** -0.5, 0.1875, ((0, 2), (1, 4)), jnp.float32),
        "key_weight": scatter_about(seeds[5], (SECTIONS, D, KV_HEADS * HEAD_DIM), D ** -0.5, 0.1875, ((0, 2), (1, 4)), jnp.float32),
        "value_weight": scatter_about(seeds[6], (SECTIONS, D, KV_HEADS * HEAD_DIM), D ** -0.5, 0.1875, ((0, 2), (1, 4)), jnp.float32),
        "query_gain": jnp.clip(1.0 + 0.15 * jax.random.normal(seeds[7], (SECTIONS, HEAD_DIM), jnp.float32), 0.25, 1.75),
        "key_gain": jnp.clip(1.0 + 0.15 * jax.random.normal(seeds[8], (SECTIONS, HEAD_DIM), jnp.float32), 0.25, 1.75),
        "out_weight": scatter_about(seeds[9], (SECTIONS, HEADS * HEAD_DIM, D), (max(HEADS * HEAD_DIM // 64, 1)) ** -0.5, 1.0, ((0, 2), (1, 4)), jnp.float32),
        "mlp_gain": jnp.clip(1.0 + 0.15 * jax.random.normal(seeds[10], (SECTIONS, D), jnp.float32), 0.25, 1.75),
        "gate_weight": scatter_about(seeds[11], (SECTIONS, D, FF), D ** -0.5, 0.1875, ((0, 2), (1, 4)), jnp.float32),
        "up_weight": scatter_about(seeds[12], (SECTIONS, D, FF), D ** -0.5, 0.1875, ((0, 2), (1, 4)), jnp.float32),
        "down_weight": scatter_about(seeds[13], (SECTIONS, FF, D), FF ** -0.5, 0.109375, ((0, 2), (1, 4)), jnp.float32),
    }


@jax.custom_vjp
def low(v):
    return lax.optimization_barrier(v.astype(jnp.bfloat16)).astype(jnp.float32)

@jax.custom_vjp
def low_back(v):
    return v

def low_keep(v):
    return (low(v), None)

def low_pass(kept, grad):
    return (grad,)

def back_keep(v):
    return (v, None)

def back_low(kept, grad):
    return (low(grad),)
low.defvjp(low_keep, low_pass)
low_back.defvjp(back_keep, back_low)
epsilon = 1e-06
rope_base = 1000000.0

def matmul_high(left, right):
    return jnp.dot(left, right, precision=lax.Precision.HIGHEST, preferred_element_type=jnp.float32)

def rms_scale(values, gain):
    scale = lax.rsqrt(lax.optimization_barrier(jnp.mean(values * values, axis=-1, keepdims=True)) + epsilon)
    return values * scale * gain

def rotate(values, cosine, sine):
    half = values.shape[-1] // 2
    turned = jnp.concatenate([-values[..., half:], values[..., :half]], axis=-1)
    return values * cosine + turned * sine

def angles(position, width):
    half = width // 2
    rates = jnp.power(rope_base, jnp.arange(half, dtype=jnp.float32) * (-2.0 / width))
    phase = position.astype(jnp.float32)[..., None] * rates
    phase = jnp.concatenate([phase, phase], axis=-1)
    return (jnp.cos(phase)[..., None, :], jnp.sin(phase)[..., None, :])

def layout(lengths_row, natural):
    bounds = jnp.cumsum(lengths_row, axis=-1).astype(jnp.int32)
    passed = (bounds[..., None, :] <= natural[..., :, None]).astype(jnp.int32)
    sequence = lax.optimization_barrier(jnp.sum(passed, axis=-1)).astype(jnp.int32)
    position = (natural - lax.optimization_barrier(jnp.sum(passed * lengths_row[..., None, :], axis=-1))).astype(jnp.int32)
    return (sequence, position)

def swiglu(gate, lifted):
    return gate * jax.nn.sigmoid(gate) * lifted

def attend(queries, key_rows, value_rows, sequence, natural):
    group = queries.shape[1] // key_rows.shape[1]
    key_rows = jnp.repeat(key_rows, group, axis=1)
    value_rows = jnp.repeat(value_rows, group, axis=1)
    scores = jnp.einsum('qhd,khd->hqk', queries, key_rows, precision=lax.Precision.HIGHEST) * queries.shape[-1] ** (-0.5)
    scores = low_back(scores)
    visible = (sequence[None, :] == sequence[:, None]) & (natural[None, :] <= natural[:, None])
    scores = jnp.where(visible[None], scores, -1e+30)
    top = lax.optimization_barrier(jnp.max(scores, axis=-1, keepdims=True))
    raised = jnp.exp(scores - top)
    probs = raised / lax.optimization_barrier(jnp.sum(raised, axis=-1, keepdims=True))
    return jnp.einsum('hqk,khd->qhd', low(probs), value_rows, precision=lax.Precision.HIGHEST)

def layer(hidden_in, params, sequence, natural, cosine, sine):
    attention_gain, query_weight, key_weight, value_weight, query_gain, key_gain, out_weight, mlp_gain, gate_weight, up_weight, down_weight = params
    rows = hidden_in.shape[0]
    head_dim = query_gain.shape[0]
    normed = low(rms_scale(hidden_in, attention_gain))
    query_raw = low_back(matmul_high(normed, query_weight)).reshape(rows, -1, head_dim)
    key_raw = low_back(matmul_high(normed, key_weight)).reshape(rows, -1, head_dim)
    value_rows = low_back(low(matmul_high(normed, value_weight))).reshape(rows, -1, head_dim)
    queries = low(rotate(rms_scale(query_raw, query_gain), cosine, sine))
    key_rows = low(rotate(rms_scale(key_raw, key_gain), cosine, sine))
    mixed = attend(queries, key_rows, value_rows, sequence, natural)
    mixed = low_back(low(mixed)).reshape(rows, -1)
    middle = hidden_in + low_back(matmul_high(mixed, out_weight))
    normed_mlp = low(rms_scale(middle, mlp_gain))
    gate = low_back(matmul_high(normed_mlp, gate_weight))
    lifted = low_back(matmul_high(normed_mlp, up_weight))
    product = low(swiglu(gate, lifted))
    return middle + low_back(matmul_high(product, down_weight))

def one_batch(first, second, item):
    rows_in, length_row = item
    natural = jnp.arange(rows_in.shape[0], dtype=jnp.int32)
    sequence, position = layout(length_row, natural)
    cosine, sine = angles(position, HEAD_DIM)
    middle = layer(rows_in, first, sequence, natural, cosine, sine)
    middle = low_back(low(middle))
    return layer(middle, second, sequence, natural, cosine, sine)

def reference(stream_in, lengths, dealing, attention_gain, query_weight, key_weight, value_weight, query_gain, key_gain, out_weight, mlp_gain, gate_weight, up_weight, down_weight):
    masters = (attention_gain, query_weight, key_weight, value_weight, query_gain, key_gain, out_weight, mlp_gain, gate_weight, up_weight, down_weight)
    batches = GROUPS * MICRO
    inputs = stream_in[0].astype(jnp.float32).reshape(batches, PACK, D)
    cotangent = stream_in[1].astype(jnp.float32).reshape(batches, PACK, D)
    length_rows = lengths.reshape(batches, SEQS)

    def forward(rows_all, weights):
        rounded = tuple((low(weight) for weight in weights))
        first = tuple((weight[0] for weight in rounded))
        second = tuple((weight[1] for weight in rounded))
        stepper = jax.checkpoint(partial(one_batch, first, second))
        return lax.map(stepper, (rows_all, length_rows))
    output, pull = jax.vjp(forward, inputs, masters)
    grad_input, grads = pull(cotangent)
    order = dealing.reshape(batches, PACK)
    first_end = jnp.take_along_axis(grad_input, order[:, :, None], axis=1)
    second_end = jnp.take_along_axis(output, order[:, :, None], axis=1)
    boundary = jnp.stack([first_end, second_end]).astype(jnp.bfloat16).reshape(2, GROUPS, MICRO, PACK, D)
    return (boundary, grads[0], grads[1], grads[2], grads[3], grads[4], grads[5], grads[6], grads[7], grads[8], grads[9], grads[10])
```

```python
import jax
import jax.numpy as jnp
from jax import lax
from jax.sharding import PartitionSpec as P

HEAD_DIM = 128
GAIN_ROWS = 16
epsilon = 1e-06
rope_base = 1000000.0
low = jnp.bfloat16
f32 = jnp.float32


def swap(value):
    return lax.ppermute(value, "section", [(0, 1), (1, 0)])


def hop(value, step):
    count = lax.axis_size("ctx")
    return lax.ppermute(value, "ctx", [(i, i ^ step) for i in range(count)])


def gather_rows(own):
    return jnp.concatenate([own] + [hop(own, k) for k in range(1, lax.axis_size("ctx"))], axis=0)


def scatter_rows(partial):
    count = lax.axis_size("ctx")
    pieces = partial.astype(low).reshape(count, -1, partial.shape[-1])
    total = pieces[0].astype(f32)
    for k in range(1, count):
        total = total + hop(pieces[k], k).astype(f32)
    return total


def rms_scale(values, gain):
    scale = lax.rsqrt(jnp.mean(values * values, axis=-1, keepdims=True) + epsilon)
    return values * scale * gain


def rotate(values, cosine, sine):
    half = values.shape[-1] // 2
    turned = jnp.concatenate([-values[..., half:], values[..., :half]], axis=-1)
    return values * cosine + turned * sine


def head_prepare(raw, gain, cosine, sine):
    shape = (1,) * (raw.ndim - 2)
    cosine = cosine.reshape(cosine.shape[:1] + shape + cosine.shape[1:])
    sine = sine.reshape(sine.shape[:1] + shape + sine.shape[1:])
    return rotate(rms_scale(raw, gain), cosine, sine)


def swiglu(gate, lifted):
    return gate * jax.nn.sigmoid(gate) * lifted


def dot(left, right):
    return jnp.dot(left, right, preferred_element_type=f32)


def dot_rows(left, right):
    return lax.dot_general(left, right, (((0,), (0,)), ((), ())), preferred_element_type=f32)


def dot_cols(left, right):
    return lax.dot_general(left, right, (((1,), (1,)), ((), ())), preferred_element_type=f32)


def es(text, left, right):
    return jnp.einsum(text, left, right, preferred_element_type=f32)


def layer_forward(hidden, weights, context):
    attention_gain, mlp_gain, query_gain, key_gain, qkv, out, lift, down = weights
    cosine, sine, visible = context
    normed = gather_rows(rms_scale(hidden, attention_gain).astype(low))
    tokens = normed.shape[0]
    raw = dot(normed, qkv).reshape(tokens, 2, -1, HEAD_DIM)
    group = raw.shape[2] - 2
    query_raw, key_raw, value_rows = raw[:, :, :group], raw[:, :, group], raw[:, :, group + 1]
    value_rows = value_rows.astype(low)
    queries = head_prepare(query_raw, query_gain, cosine, sine).astype(low)
    key_rows = head_prepare(key_raw, key_gain, cosine, sine).astype(low)
    scores = es("tvgd,uvd->vgtu", queries, key_rows) * HEAD_DIM ** (-0.5)
    scores = jnp.where(visible, scores, -1e30)
    raised = jnp.exp(scores - jnp.max(scores, axis=-1, keepdims=True))
    probs = raised / jnp.sum(raised, axis=-1, keepdims=True)
    mixed = es("vgtu,uvd->tvgd", probs.astype(low), value_rows).astype(low).reshape(tokens, -1)
    middle = hidden + scatter_rows(dot(mixed, out))
    normed_mlp = gather_rows(rms_scale(middle, mlp_gain).astype(low))
    both = dot(normed_mlp, lift).reshape(tokens, 2, 2, -1)
    gate, lifted = both[:, :, 0], both[:, :, 1]
    product = swiglu(gate, lifted).astype(low).reshape(tokens, -1)
    result = middle + scatter_rows(dot(product, down))
    kept = (hidden, normed, query_raw, key_raw, value_rows, queries, key_rows, probs, mixed)
    return result, kept + (middle, normed_mlp, gate, lifted, product)


def layer_backward(upstream, kept, weights, context):
    attention_gain, mlp_gain, query_gain, key_gain, qkv, out, lift, down = weights
    hidden, normed, query_raw, key_raw, value_rows, queries, key_rows, probs, mixed = kept[:9]
    middle, normed_mlp, gate, lifted, product = kept[9:]
    cosine, sine, visible = context
    scale = HEAD_DIM ** (-0.5)
    tokens = normed.shape[0]
    branch = gather_rows(upstream.astype(low))
    grad_down = dot_rows(product, branch)
    grad_product = dot_cols(branch, down).reshape(gate.shape)
    unused, pull = jax.vjp(swiglu, gate, lifted)
    grad_gate, grad_lifted = pull(grad_product)
    grad_both = jnp.stack([grad_gate.astype(low), grad_lifted.astype(low)], axis=2)
    grad_both = grad_both.reshape(tokens, -1)
    grad_lift = dot_rows(normed_mlp, grad_both)
    grad_normed_mlp = scatter_rows(dot_cols(grad_both, lift))
    unused, pull = jax.vjp(rms_scale, middle, mlp_gain)
    grad_middle, grad_mlp_gain = pull(grad_normed_mlp)
    grad_middle = upstream + grad_middle
    branch = gather_rows(grad_middle.astype(low))
    grad_out = dot_rows(mixed, branch)
    grad_mixed = dot_cols(branch, out).astype(low).reshape(queries.shape)
    probs_low = probs.astype(low)
    grad_probs = es("tvgd,uvd->vgtu", grad_mixed, value_rows)
    weighted = jnp.sum(probs * grad_probs, axis=-1, keepdims=True)
    grad_scores = (probs * (grad_probs - weighted)).astype(low)
    grad_queries = es("vgtu,uvd->tvgd", grad_scores, key_rows) * scale
    grad_keys = es("vgtu,tvgd->uvd", grad_scores, queries) * scale
    grad_values = es("vgtu,tvgd->uvd", probs_low, grad_mixed).astype(low)

    def prepare(raw, gain):
        return head_prepare(raw, gain, cosine, sine)

    unused, pull = jax.vjp(prepare, query_raw, query_gain)
    grad_query_raw, grad_query_gain = pull(grad_queries)
    unused, pull = jax.vjp(prepare, key_raw, key_gain)
    grad_key_raw, grad_key_gain = pull(grad_keys)
    grad_raw = jnp.concatenate(
        [grad_query_raw.astype(low), grad_key_raw.astype(low)[:, :, None], grad_values[:, :, None]],
        axis=2,
    ).reshape(tokens, -1)
    grad_qkv = dot_rows(normed, grad_raw)
    grad_normed = scatter_rows(dot_cols(grad_raw, qkv))
    unused, pull = jax.vjp(rms_scale, hidden, attention_gain)
    grad_hidden, grad_attention_gain = pull(grad_normed)
    gains = (grad_attention_gain, grad_mlp_gain, grad_query_gain, grad_key_gain)
    return grad_middle + grad_hidden, (gains, grad_qkv, grad_out, grad_lift, grad_down)


def shards(
    stream_in,
    lengths,
    dealing,
    attention_gain,
    query_weight,
    key_weight,
    value_weight,
    query_gain,
    key_gain,
    out_weight,
    mlp_gain,
    gate_weight,
    up_weight,
    down_weight,
):
    core = lax.axis_index("section")
    piece = lax.axis_index("ctx")
    count = lax.axis_size("ctx")
    depth = lax.axis_size("fsdp")
    rows, width = stream_in.shape[3], stream_in.shape[4]
    tokens = rows * count
    first = core == 0
    query_half = query_weight.shape[2] // (2 * count)
    key_half = key_weight.shape[2] // (2 * count)
    hidden_half = gate_weight.shape[2] // (2 * count)
    part = query_weight.shape[1]
    aligned = depth == count

    def ordered(own, other, axis=0):
        pair = jnp.where(first, jnp.stack([own, other]), jnp.stack([other, own]))
        return jnp.moveaxis(pair, 0, axis)

    def columns(weight, half, size):
        start = (piece * 2 + half) * size
        return lax.dynamic_slice_in_dim(weight[0], start, size, 1).astype(low)

    def quarter(weight, half, size):
        share = size // count
        return lax.dynamic_slice_in_dim(weight[0], half * size + piece * share, share, 0).astype(low)

    gains = (attention_gain[0], mlp_gain[0], query_gain[0], key_gain[0])
    sizes = [gain.shape[0] for gain in gains]
    block_width = query_half + 2 * key_half
    gain_block = jnp.concatenate(gains).astype(low)
    gain_block = jnp.pad(gain_block, (0, GAIN_ROWS * block_width - gain_block.shape[0]))
    gain_block = gain_block.reshape(GAIN_ROWS, block_width)

    def attention_block(half):
        block = [columns(query_weight, half, query_half), columns(key_weight, half, key_half)]
        block = jnp.concatenate(block + [columns(value_weight, half, key_half)], axis=1)
        return jnp.concatenate([block, gain_block], axis=0)

    def lift_block(half):
        block = [columns(gate_weight, half, hidden_half), columns(up_weight, half, hidden_half)]
        return jnp.concatenate(block, axis=1)

    def row_block(half):
        return jnp.concatenate(
            [quarter(out_weight, half, query_half), quarter(down_weight, half, hidden_half)], axis=0
        )

    def by_layer(make):
        mine = make(core)
        other = swap(make(1 - core))
        return jnp.where(first, mine, other), jnp.where(first, other, mine)

    def both_halves(own):
        return own, swap(own)

    blocks = by_layer(attention_block), by_layer(lift_block)
    row_blocks = by_layer(row_block) if aligned else None
    out_share, down_share = query_half // count, hidden_half // count
    if not aligned:
        whole = []
        for weight, size in ((out_weight, query_half), (down_weight, hidden_half)):
            full = lax.all_gather(weight[0].astype(low), "fsdp", axis=0, tiled=True)
            full = lax.dynamic_slice_in_dim(full, piece * 2 * size, 2 * size, 0)
            other = swap(full)
            layers = jnp.where(first, full, other), jnp.where(first, other, full)
            own = [lax.dynamic_slice_in_dim(v, core * size, size, 0) for v in layers]
            far = [lax.dynamic_slice_in_dim(v, (1 - core) * size, size, 0) for v in layers]
            whole.append([jnp.concatenate(pair, axis=0) for pair in zip(own, far)])

    def layer_weights(layer):
        own = lax.all_gather(blocks[0][layer], "fsdp", axis=0, tiled=False)
        packed = own[:, part:].reshape(depth, -1)
        split = []
        at = 0
        for size in sizes:
            split.append(packed[:, at : at + size].reshape(-1).astype(f32))
            at += size
        qkv = jnp.concatenate(both_halves(own[:, :part].reshape(width, block_width)), axis=1)
        if aligned:
            own = lax.all_gather(row_blocks[layer], "fsdp", axis=0, tiled=False)
            own = lax.all_to_all(own, "ctx", 0, 0, tiled=True)
            far = swap(own)
            out = [half[:, :out_share].reshape(query_half, width) for half in (own, far)]
            down = [half[:, out_share:].reshape(hidden_half, width) for half in (own, far)]
            out, down = jnp.concatenate(out, axis=0), jnp.concatenate(down, axis=0)
        else:
            out, down = whole[0][layer], whole[1][layer]
        own = lax.all_gather(blocks[1][layer], "fsdp", axis=0, tiled=True)
        lift = jnp.concatenate(both_halves(own), axis=1)
        return (*split, qkv, out, lift, down)

    lens = lax.dynamic_index_in_dim(lengths[0], core, 0, keepdims=False)
    slots = lax.dynamic_index_in_dim(dealing[0], core, 0, keepdims=False)
    index = jnp.arange(tokens, dtype=jnp.int32)
    natural = ((index // rows) ^ piece) * rows + index % rows
    bounds = jnp.cumsum(lens)
    passed = (bounds[None, :] <= natural[:, None]).astype(jnp.int32)
    sequence = jnp.sum(passed, axis=1)
    position = natural - jnp.sum(passed * lens[None, :], axis=1)
    half = HEAD_DIM // 2
    rates = jnp.power(rope_base, jnp.arange(half, dtype=f32) * (-2.0 / HEAD_DIM))
    phase = position.astype(f32)[:, None] * rates
    phase = jnp.concatenate([phase, phase], axis=-1)
    visible = (sequence[None, :] == sequence[:, None]) & (natural[None, :] <= natural[:, None])
    context = (jnp.cos(phase), jnp.sin(phase), visible)

    own = lax.dynamic_index_in_dim(stream_in[0, 0], core, 0, keepdims=False)
    other = swap(lax.dynamic_index_in_dim(stream_in[0, 0], 1 - core, 0, keepdims=False))
    hidden = jnp.where(first, own, other)
    cotangent = jnp.where(first, other, own)

    layers = [layer_weights(0), layer_weights(1)]
    result, kept_first = layer_forward(hidden.astype(f32), layers[0], context)
    middle = result.astype(low)
    result, kept_last = layer_forward(middle.astype(f32), layers[1], context)
    last = result.astype(low)
    grad, grads_last = layer_backward(cotangent.astype(f32), kept_last, layers[1], context)
    grad = grad.astype(low)
    grad, grads_first = layer_backward(grad.astype(f32), kept_first, layers[0], context)
    grad = grad.astype(low)

    wanted = lax.dynamic_slice_in_dim(slots, piece * rows, rows, 0)
    wanted = ((wanted // rows) ^ piece) * rows + wanted % rows
    chosen = (wanted[:, None] == index[None, :]).astype(low)

    def dealt(value):
        return dot(chosen, gather_rows(value)).astype(low)

    last, grad = dealt(last), dealt(grad)
    own = jnp.where(first, grad, last)
    other = swap(jnp.where(first, last, grad))
    boundary = ordered(own, other)

    def meet(grad_own, grad_other):
        return grad_own + swap(grad_other.astype(low)).astype(f32)

    def reduced(grads):
        gains, grad_qkv, grad_out, grad_lift, grad_down = grads
        total = meet(grad_qkv[:, :block_width], grad_qkv[:, block_width:])
        split = [gain.reshape(depth, -1) for gain in gains]
        packed = jnp.concatenate(split, axis=1)
        packed = meet(packed, packed)
        packed = jnp.pad(packed, ((0, 0), (0, GAIN_ROWS * block_width - packed.shape[1])))
        packed = packed.reshape(depth, GAIN_ROWS, block_width)
        total = jnp.concatenate([total.reshape(depth, part, block_width), packed], axis=1)
        total = lax.psum_scatter(total.astype(low), "fsdp", scatter_dimension=0, tiled=False)
        attention = lax.all_gather(total, "ctx", axis=0, tiled=False)
        total = meet(grad_lift[:, : 2 * hidden_half], grad_lift[:, 2 * hidden_half :])
        total = lax.psum_scatter(total.astype(low), "fsdp", scatter_dimension=0, tiled=True)
        lift = lax.all_gather(total, "ctx", axis=0, tiled=False)
        out = meet(grad_out[:query_half], grad_out[query_half:])
        down = meet(grad_down[:hidden_half], grad_down[hidden_half:])
        if aligned:
            total = [out.reshape(count, out_share, width), down.reshape(count, down_share, width)]
            total = jnp.concatenate(total, axis=1).astype(low)
            total = lax.all_to_all(total, "ctx", 0, 0, tiled=True)
            total = lax.psum_scatter(total, "fsdp", scatter_dimension=0, tiled=False)
            rest = (lax.all_gather(total, "ctx", axis=0, tiled=False),)
        else:
            rest = []
            for grad, size in ((out, query_half), (down, hidden_half)):
                full = jnp.zeros((2 * count * size, width), low)
                at = (piece * 2 + core) * size
                full = lax.dynamic_update_slice_in_dim(full, grad.astype(low), at, 0)
                full = lax.psum_scatter(full, "fsdp", scatter_dimension=0, tiled=True)
                rest.append(lax.psum(full, "ctx"))
        return (attention, lift, *rest)

    pairs = []
    for from_first, from_last in zip(reduced(grads_first), reduced(grads_last)):
        own = jnp.where(first, from_first, from_last)
        pairs.append((own, swap(jnp.where(first, from_last, from_first))))

    def side(own, other, start, stop):
        both = ordered(own[..., start:stop], other[..., start:stop], axis=1)
        return jnp.moveaxis(both, 2, 0).reshape(1, own.shape[1], -1).astype(f32)

    own, other = pairs[0]
    middle_at = query_half + key_half
    grad_query = side(own[:, :part], other[:, :part], 0, query_half)
    grad_key = side(own[:, :part], other[:, :part], query_half, middle_at)
    grad_value = side(own[:, :part], other[:, :part], middle_at, block_width)
    packed = jnp.sum(own[:, part:].reshape(count, -1).astype(f32), axis=0)
    packed_gains = []
    at = 0
    for size in sizes:
        packed_gains.append(packed[None, at : at + size])
        at += size
    own, other = pairs[1]
    grad_gate = side(own, other, 0, hidden_half)
    grad_up = side(own, other, hidden_half, 2 * hidden_half)
    if aligned:
        own, other = pairs[2]

        def stacked(start, stop):
            both = ordered(own[:, start:stop], other[:, start:stop])
            return both.reshape(1, -1, width).astype(f32)

        grad_out = stacked(0, out_share)
        grad_down = stacked(out_share, out_share + down_share)
    else:
        grad_out, grad_down = [(own.astype(f32) + other.astype(f32))[None] for own, other in pairs[2:]]
    return (
        boundary[None, None],
        packed_gains[0],
        grad_query,
        grad_key,
        grad_value,
        packed_gains[2],
        packed_gains[3],
        grad_out,
        packed_gains[1],
        grad_gate,
        grad_up,
        grad_down,
    )


def solution(mesh):
    weight, gain, row = P("section", "fsdp", None), P("section", "fsdp"), P("fsdp", None, None)
    stream = P("section", "fsdp", None, "ctx", None)
    masters = (gain, weight, weight, weight, gain, gain, weight, gain, weight, weight, weight)
    return jax.shard_map(
        shards,
        mesh=mesh,
        in_specs=(stream, row, row) + masters,
        out_specs=(stream,) + masters,
        check_vma=False,
    )
```

```python
import functools

import jax
import jax.numpy as jnp
from jax import lax
from jax.experimental import pallas as pl
from jax.experimental.pallas import tpu as pltpu
from jax.sharding import PartitionSpec as P

HEAD_DIM = 128
GAIN_ROWS = 16
LANES = 256
VMEM_LIMIT = 56 * 1024 * 1024
FLOPS_PER_US = 1.15e9
SCALE = HEAD_DIM ** (-0.5)
epsilon = 1e-06
rope_base = 1000000.0
low = jnp.bfloat16
f32 = jnp.float32


def swap(value):
    return lax.ppermute(value, "section", [(0, 1), (1, 0)])


def hop(value, step):
    count = lax.axis_size("ctx")
    return lax.ppermute(value, "ctx", [(i, i ^ step) for i in range(count)])


def hops(own):
    return [own] + [hop(own, k) for k in range(1, lax.axis_size("ctx"))]


def met(parts):
    return [parts[0]] + [hop(parts[k], k) for k in range(1, len(parts))]


def beside(results, others):
    return lax.optimization_barrier((results, others))


def tie(value, other):
    return lax.optimization_barrier((value, other))[0]


def xored(pieces, index):
    for bit in range(len(pieces).bit_length() - 1):
        turned = ((index >> bit) & 1) == 1
        pieces = [jnp.where(turned, pieces[j ^ (1 << bit)], v) for j, v in enumerate(pieces)]
    return pieces


def dot(left, right):
    return jnp.dot(left, right, preferred_element_type=f32)


def dot_rows(left, right):
    return lax.dot_general(left, right, (((0,), (0,)), ((), ())), preferred_element_type=f32)


def dot_cols(left, right):
    return lax.dot_general(left, right, (((1,), (1,)), ((), ())), preferred_element_type=f32)


def rms_scale(values, gain):
    scale = lax.rsqrt(jnp.mean(values * values, axis=-1, keepdims=True) + epsilon)
    return values * scale * gain


def rms_back(values, gain, grad):
    scale = lax.rsqrt(jnp.mean(values * values, axis=-1, keepdims=True) + epsilon)
    unit = values * scale
    lifted = grad * gain
    grad_values = (lifted - unit * jnp.mean(lifted * unit, axis=-1, keepdims=True)) * scale
    return grad_values, jnp.sum(grad * unit, axis=0, keepdims=True)


def turn(values, cosine, sine):
    return values * cosine + pltpu.roll(values, HEAD_DIM // 2, 1) * sine


def turn_back(grad, cosine, sine):
    return grad * cosine + pltpu.roll(grad * sine, HEAD_DIM // 2, 1)


def chunk(j, size):
    return pl.ds(pl.multiple_of(j * size, size), size)


def span(j, size):
    return slice(j * size, (j + 1) * size)


def join(pieces, target):
    rows = pieces[0].shape[0]
    for i, piece in enumerate(pieces):
        target[span(i, rows), :] = piece[...]


def deal_out(parts, block, value):
    rows = parts[0].shape[0]
    for i, part in enumerate(parts):
        part[:, block] = value[span(i, rows)].astype(part.dtype)


def call(kernel, operands, outputs, took, scratch=(), scalars=(), after=()):
    vmem = pl.BlockSpec(memory_space=pltpu.VMEM)
    smem = pl.BlockSpec(memory_space=pltpu.SMEM)
    anywhere = pl.BlockSpec(memory_space=pl.ANY)
    shapes = [jax.ShapeDtypeStruct(shape, dtype) for shape, dtype in outputs]
    moved = sum(v.size * v.dtype.itemsize for v in [*operands, *shapes])
    skipped, used = len(after), len(scalars)

    def body(*refs):
        kernel(*refs[skipped:])

    return pl.pallas_call(
        body,
        out_shape=shapes,
        in_specs=[anywhere] * skipped + [smem] * used + [vmem] * len(operands),
        out_specs=[vmem] * len(shapes),
        scratch_shapes=[pltpu.VMEM(shape, dtype) for shape, dtype in scratch],
        compiler_params=pltpu.CompilerParams(vmem_limit_bytes=VMEM_LIMIT),
        cost_estimate=pl.CostEstimate(
            flops=int(took * FLOPS_PER_US), bytes_accessed=moved, transcendentals=0
        ),
    )(*after, *scalars, *operands)


def add_kernel(count, rounded, *refs):
    parts, (residual, gain, total, normed) = refs[:count], refs[count:]
    value = residual[...].astype(f32)
    for part in parts:
        value = value + part[...].astype(f32)
    if rounded:
        value = value.astype(low).astype(f32)
    total[...] = value
    normed[...] = rms_scale(value, gain[...]).astype(low)


def add_back_kernel(count, rounded, *refs):
    parts, (upstream, middle, gain, total, sent, grad_gain) = refs[:count], refs[count:]
    grad = parts[0][...].astype(f32)
    for part in parts[1:]:
        grad = grad + part[...].astype(f32)
    grad, gains = rms_back(middle[...].astype(f32), gain[...], grad)
    grad = upstream[...].astype(f32) + grad
    sent[...] = grad.astype(low)
    total[...] = grad.astype(low).astype(f32) if rounded else grad
    grad_gain[...] = gains


def attention_forward_kernel(count, part, raw_rows, *refs):
    pieces, refs = refs[:count], refs[count:]
    if raw_rows:
        gain, *refs = refs
    own_weight, far_weight, cosine, sine, query_gain, key_gain, start, place, place_row, *refs = refs
    normed, raw, queries, keys, mixed, spread, values = refs
    tokens = normed.shape[0]
    rows = pieces[0].shape[0]
    depth = own_weight.shape[0]
    halves = keys.shape[1] // HEAD_DIM
    group = queries.shape[1] // keys.shape[1]
    step = (group + 2) * HEAD_DIM
    if raw_rows:
        for i, piece in enumerate(pieces):
            normed[span(i, rows), :] = rms_scale(piece[...].astype(f32), gain[...]).astype(low)
    else:
        join(pieces, normed)
    for half, weight in enumerate((own_weight, far_weight)):
        for j, at in enumerate((0, part + GAIN_ROWS)):
            total = None
            for z in range(depth):
                term = dot(normed[:, span(z, part)], weight[z, at : at + part, :])
                total = term if total is None else total + term
            raw[:, span(2 * half + j, LANES)] = total

    for half in range(halves):
        base = half * step
        at = base + group * HEAD_DIM
        own = span(half, HEAD_DIM)
        unit = rms_scale(raw[:, at : at + HEAD_DIM], key_gain[...])
        keys[:, own] = turn(unit, cosine[...], sine[...]).astype(low)
        values[:, own] = raw[:, at + HEAD_DIM : at + 2 * HEAD_DIM].astype(low)
        for g in range(group):
            unit = rms_scale(raw[:, base + g * HEAD_DIM : base + (g + 1) * HEAD_DIM], query_gain[...])
            unit = turn(unit, cosine[...], sine[...])
            queries[:, span(half * group + g, HEAD_DIM)] = unit.astype(low)

    @pl.loop(0, tokens // rows)
    def _(i):
        block = chunk(i, rows)
        visible = (place_row[...] >= start[block, :]) & (place_row[...] <= place[block, :])
        for head in range(halves * group):
            own, at = span(head // group, HEAD_DIM), span(head, HEAD_DIM)
            scores = dot_cols(queries[block, at], keys[:, own]) * SCALE
            scores = jnp.where(visible, scores, -1e30)
            top = jnp.max(scores, axis=-1, keepdims=True)
            raised = jnp.exp(scores - top)
            total = jnp.sum(raised, axis=-1, keepdims=True)
            probs = (raised * (1.0 / total)).astype(low)
            mixed[block, at] = dot(probs, values[:, own]).astype(low)
            spread[block, head : head + 1] = top + jnp.log(total)


def rows_kernel(count, ordered, *refs):
    index, left, own, far, *refs = refs
    parts, whole = refs[:count], refs[count]
    if ordered:
        whole[...] = own[...]
    else:
        size = whole.shape[0] // 2
        share = size // count
        for half, value in enumerate((own, far)):
            for k in range(count):
                to = half * size + (index[0] ^ k) * share
                to = pl.ds(pl.multiple_of(to, share), share)
                for j in range(whole.shape[1] // LANES):
                    whole[to, span(j, LANES)] = value[k, span(j, share), :]

    @pl.loop(0, whole.shape[1] // LANES)
    def _(j):
        block = chunk(j, LANES)
        deal_out(parts, block, dot(left[...], whole[:, block]))


def lift_kernel(count, part, *refs):
    pieces, (own_weight, far_weight, normed, gate, lifted, product) = refs[:count], refs[count:]
    half_size = product.shape[1] // 2
    depth = own_weight.shape[0]
    join(pieces, normed)
    for half, weight in enumerate((own_weight, far_weight)):
        both = []
        for j in range(2 * half_size // LANES):
            total = None
            for z in range(depth):
                term = dot(normed[:, span(z, part)], weight[z, span(j, part), :])
                total = term if total is None else total + term
            both.append(total)
        both = jnp.concatenate(both, axis=1)
        one, two = both[:, :half_size], both[:, half_size:]
        at = span(half, half_size)
        gate[:, at] = one
        lifted[:, at] = two
        product[:, at] = (one * jax.nn.sigmoid(one) * two).astype(low)


def mlp_backward_kernel(count, part, *refs):
    pieces, refs = refs[:count], refs[count:]
    own_weight, far_weight, down, gate, lifted, *refs = refs
    parts, (branch, grad_both) = refs[:count], refs[count:]
    size = gate.shape[1] // 2
    depth = own_weight.shape[0]
    join(pieces, branch)
    for half in range(2):
        at = span(half, size)
        grad = dot_cols(branch[...], down[at, :])
        one, two = gate[:, at], lifted[:, at]
        sigmoid = jax.nn.sigmoid(one)
        grad_gate = grad * two * sigmoid * (1.0 + one * (1.0 - sigmoid))
        grad_both[:, span(2 * half, size)] = grad_gate.astype(low)
        grad_both[:, span(2 * half + 1, size)] = (grad * one * sigmoid).astype(low)
    for z in range(depth):
        total = None
        for half, weight in enumerate((own_weight, far_weight)):
            for j in range(2 * size // LANES):
                at = 2 * half * size + j * LANES
                term = dot_cols(grad_both[:, at : at + LANES], weight[z, span(j, part), :])
                total = term if total is None else total + term
        deal_out(parts, span(z, part), total)


def attention_backward_kernel(count, part, *refs):
    pieces, refs = refs[:count], refs[count:]
    own_weight, far_weight, out, *refs = refs
    cosine, sine, query_gain, key_gain, start, place, place_row, *refs = refs
    raw, queries, keys, spread, *refs = refs
    parts, refs = refs[:count], refs[count:]
    branch, grad_raw, grad_query_gain, grad_key_gain, *refs = refs
    grad_mixed, values, grad_queries, grad_keys, grad_values = refs
    tokens, width = branch.shape
    rows = pieces[0].shape[0]
    depth = own_weight.shape[0]
    halves = keys.shape[1] // HEAD_DIM
    group = queries.shape[1] // keys.shape[1]
    step = (group + 2) * HEAD_DIM
    join(pieces, branch)

    @pl.loop(0, grad_mixed.shape[1] // LANES)
    def _(j):
        block = chunk(j, LANES)
        grad_mixed[:, block] = dot_cols(branch[...], out[block, :]).astype(low)

    for half in range(halves):
        at = half * step + (group + 1) * HEAD_DIM
        values[:, span(half, HEAD_DIM)] = raw[:, at : at + HEAD_DIM].astype(low)
    grad_keys[...] = jnp.zeros_like(grad_keys)
    grad_values[...] = jnp.zeros_like(grad_values)

    @pl.loop(0, tokens // rows)
    def _(i):
        block = chunk(i, rows)
        visible = (place_row[...] >= start[block, :]) & (place_row[...] <= place[block, :])
        for head in range(halves * group):
            own, at = span(head // group, HEAD_DIM), span(head, HEAD_DIM)
            query, grad = queries[block, at], grad_mixed[block, at]
            scores = dot_cols(query, keys[:, own]) * SCALE
            scores = jnp.where(visible, scores, -1e30)
            probs = jnp.exp(scores - spread[block, head : head + 1])
            grad_probs = dot_cols(grad, values[:, own])
            weighted = jnp.sum(probs * grad_probs, axis=-1, keepdims=True)
            grad_scores = (probs * (grad_probs - weighted)).astype(low)
            grad_queries[block, at] = dot(grad_scores, keys[:, own]) * SCALE
            grad_keys[:, own] += dot_rows(grad_scores, query) * SCALE
            grad_values[:, own] += dot_rows(probs.astype(low), grad)

    total_query = jnp.zeros((1, HEAD_DIM), f32)
    total_key = jnp.zeros((1, HEAD_DIM), f32)
    for half in range(halves):
        base = half * step
        own = span(half, HEAD_DIM)
        for g in range(group + 1):
            at = slice(base + g * HEAD_DIM, base + (g + 1) * HEAD_DIM)
            if g < group:
                grad, gain = grad_queries[:, span(half * group + g, HEAD_DIM)], query_gain[...]
            else:
                grad, gain = grad_keys[:, own], key_gain[...]
            grad = turn_back(grad, cosine[...], sine[...])
            grad, grad_gain = rms_back(raw[:, at], gain, grad)
            grad_raw[:, at] = grad.astype(low)
            if g < group:
                total_query += grad_gain
            else:
                total_key += grad_gain
        at = base + (group + 1) * HEAD_DIM
        grad_raw[:, at : at + HEAD_DIM] = grad_values[:, own].astype(low)
    grad_query_gain[...] = total_query
    grad_key_gain[...] = total_key
    for z in range(depth):
        total = None
        for half, weight in enumerate((own_weight, far_weight)):
            for j, at in enumerate((0, part + GAIN_ROWS)):
                grad = grad_raw[:, span(2 * half + j, LANES)]
                term = dot_cols(grad, weight[z, at : at + part, :])
                total = term if total is None else total + term
        deal_out(parts, span(z, part), total)


def weight_grads_kernel(part, left, grads, inner, branch, own, far, own_rows, far_rows, turned):
    depth, count = own.shape[0], own_rows.shape[0]
    chunks = grads.shape[1] // (2 * LANES)
    size = inner.shape[1] // 2
    share = size // count
    for z in range(depth):
        turned[span(z, part), :] = left[:, span(z, part)].T
    for half, target in enumerate((own, far)):
        for j in range(chunks):
            total = dot(turned[...], grads[:, span(half * chunks + j, LANES)])
            for z in range(depth):
                target[z, span(j, part), :] = total[span(z, part)].astype(target.dtype)
    for half, target in enumerate((own_rows, far_rows)):
        rows = inner[:, span(half, size)].T
        for j in range(branch.shape[1] // LANES):
            total = dot(rows, branch[:, span(j, LANES)])
            for k in range(count):
                target[k, span(j, share), :] = total[span(k, share)].astype(target.dtype)


def meet_kernel(index, own, recv, own_rows, recv_rows, total, *rows):
    total[...] = (own[...] + recv[...].astype(f32)).astype(low)
    for k, row in enumerate(rows):
        at = index[0] ^ k
        row[...] = (own_rows[at] + recv_rows[at].astype(f32)).astype(low)


def layout_kernel(part, mid, index, *refs):
    total, *refs = refs
    refs = list(refs)
    gains = refs.pop(0) if mid else None
    *rows, out = refs
    depth = out.shape[0]
    size = total.shape[1]
    extra = GAIN_ROWS if mid else 0
    for z in range(depth):
        out[z, :part, :] = total[z, :part, :]
        if mid:
            out[z, part : part + extra, :] = gains[z]
        out[z, part + extra : size + extra, :] = total[z, part:, :]
    for k, row in enumerate(rows):
        out[index[0] ^ k, size + extra :, :] = row[...]


def shards(
    stream_in,
    lengths,
    dealing,
    attention_gain,
    query_weight,
    key_weight,
    value_weight,
    query_gain,
    key_gain,
    out_weight,
    mlp_gain,
    gate_weight,
    up_weight,
    down_weight,
):
    core = lax.axis_index("section")
    piece = lax.axis_index("ctx")
    count = lax.axis_size("ctx")
    depth = lax.axis_size("fsdp")
    rows, width = stream_in.shape[3], stream_in.shape[4]
    tokens = rows * count
    first = core == 0
    query_half = query_weight.shape[2] // (2 * count)
    key_half = key_weight.shape[2] // (2 * count)
    hidden_half = gate_weight.shape[2] // (2 * count)
    part = query_weight.shape[1]
    aligned = depth == count
    out_share, down_share = query_half // count, hidden_half // count
    index = piece.astype(jnp.int32).reshape(1)
    chunks = width // LANES
    qkv_rows = 2 * part + GAIN_ROWS
    lift_rows = 2 * hidden_half // LANES * part

    where = jnp.stack([piece, core]).astype(jnp.int32)

    def cut(kernel, weights, constants, size):
        def half(i, where):
            return jnp.where(i == 0, 1 - where[1], where[1])

        def columns(i, where):
            return 0, 0, where[0] * 2 + half(i, where)

        def shares(i, where):
            return 0, half(i, where) * count + where[0], 0

        in_specs = [
            pl.BlockSpec((1, height, breadth), shares if by_rows else columns)
            for _, height, breadth, by_rows in weights
        ]
        in_specs += [pl.BlockSpec(v.shape, lambda i, where: (0, 0)) for v in constants]
        return pl.pallas_call(
            kernel,
            grid_spec=pltpu.PrefetchScalarGridSpec(
                num_scalar_prefetch=1,
                grid=(2,),
                in_specs=in_specs,
                out_specs=pl.BlockSpec((1, size, LANES), lambda i, where: (i, 0, 0)),
            ),
            out_shape=jax.ShapeDtypeStruct((2, size, LANES), low),
            compiler_params=pltpu.CompilerParams(vmem_limit_bytes=VMEM_LIMIT),
            cost_estimate=pl.CostEstimate(
                flops=int(3 * FLOPS_PER_US), bytes_accessed=12 * size * LANES, transcendentals=0
            ),
        )(where, *[weight for weight, *_ in weights], *constants)

    def place_shares(weight, out, at):
        share = weight.shape[1]
        for j in range(chunks):
            out[0, at + j * share : at + (j + 1) * share, :] = weight[0, :, span(j, LANES)].astype(low)

    def qkv_cut_kernel(where, query, key, value, *refs):
        *rest, gains, out = refs
        out[0, :part, :] = query[0].astype(low)
        out[0, part : part + GAIN_ROWS, :] = gains[...]
        at = slice(part + GAIN_ROWS, qkv_rows)
        out[0, at, :key_half] = key[0].astype(low)
        out[0, at, key_half:] = value[0].astype(low)
        if aligned:
            place_shares(rest[0], out, qkv_rows)

    def mlp_cut_kernel(where, gate, up, *refs):
        *rest, out = refs
        both = jnp.concatenate([gate[0].astype(low), up[0].astype(low)], axis=1)
        for j in range(2 * hidden_half // LANES):
            out[0, span(j, part), :] = both[:, span(j, LANES)]
        if aligned:
            place_shares(rest[0], out, lift_rows)

    gains = (attention_gain[0], mlp_gain[0], query_gain[0], key_gain[0])
    sizes = [gain.shape[0] for gain in gains]
    gain_block = jnp.concatenate(gains).astype(low)
    gain_block = jnp.pad(gain_block, (0, GAIN_ROWS * LANES - gain_block.shape[0]))
    gain_block = gain_block.reshape(GAIN_ROWS, LANES)

    def by_layer(cuts):
        mine, other = cuts[1], swap(cuts[0])
        return jnp.where(first, mine, other), jnp.where(first, other, mine)

    weights = [(query_weight, part, query_half, False), (key_weight, part, key_half, False)]
    weights += [(value_weight, part, key_half, False)]
    weights += [(out_weight, out_share, width, True)] if aligned else []
    size = qkv_rows + (chunks * out_share if aligned else 0)
    attention_blocks = by_layer(cut(qkv_cut_kernel, weights, [gain_block], size))
    weights = [(gate_weight, part, hidden_half, False), (up_weight, part, hidden_half, False)]
    weights += [(down_weight, down_share, width, True)] if aligned else []
    size = lift_rows + (chunks * down_share if aligned else 0)
    mlp_blocks = by_layer(cut(mlp_cut_kernel, weights, [], size))

    def gathered(block):
        return lax.all_gather(block, "fsdp", axis=0, tiled=False)

    def gathered_direct(block):
        pieces = [block]
        for k in range(1, depth):
            pieces.append(lax.ppermute(block, "fsdp", [(i, i ^ k) for i in range(depth)]))
        return jnp.stack(xored(pieces, lax.axis_index("fsdp")))

    def whole_rows(weight, size):
        full = lax.all_gather(weight[0].astype(low), "fsdp", axis=0, tiled=True)
        full = lax.dynamic_slice_in_dim(full, piece * 2 * size, 2 * size, 0)
        other = swap(full)
        layers = jnp.where(first, full, other), jnp.where(first, other, full)
        own = [lax.dynamic_slice_in_dim(v, core * size, size, 0) for v in layers]
        far = [lax.dynamic_slice_in_dim(v, (1 - core) * size, size, 0) for v in layers]
        return [jnp.concatenate(pair, axis=0) for pair in zip(own, far)]

    def shared_rows(value):
        sent = [lax.dynamic_index_in_dim(value, piece ^ k, 0, keepdims=False) for k in range(count)]
        own = jnp.stack(met(sent))
        return own, swap(own)

    def split_gains(own):
        found, at = [], 0
        flat = own[:, part : part + GAIN_ROWS].reshape(depth, -1)
        for size in sizes:
            found.append(flat[:, at : at + size].reshape(1, -1).astype(f32))
            at += size
        return found

    lens = lax.dynamic_index_in_dim(lengths[0], core, 0, keepdims=False)
    slots = lax.dynamic_index_in_dim(dealing[0], core, 0, keepdims=False)
    order = jnp.arange(tokens, dtype=jnp.int32)
    natural = ((order // rows) ^ piece) * rows + order % rows
    bounds = jnp.cumsum(lens)
    passed = (bounds[None, :] <= natural[:, None]).astype(jnp.int32)
    start = jnp.sum(passed * lens[None, :], axis=1)
    position = natural - start
    rates = jnp.power(rope_base, jnp.arange(HEAD_DIM // 2, dtype=f32) * (-2.0 / HEAD_DIM))
    phase = position.astype(f32)[:, None] * rates
    cosine, sine = jnp.cos(phase), jnp.sin(phase)
    cosine = jnp.concatenate([cosine, cosine], axis=-1)
    sine = jnp.concatenate([-sine, sine], axis=-1)
    places = [start[:, None], natural[:, None], natural[None, :]]

    own = lax.dynamic_index_in_dim(stream_in[0, 0], core, 0, keepdims=False)
    other = swap(lax.dynamic_index_in_dim(stream_in[0, 0], 1 - core, 0, keepdims=False))
    entering = jnp.where(first, own, other)
    cotangent = jnp.where(first, other, own)

    wide, half_wide = (rows, width), (tokens, width)
    heads_wide, hidden_wide = 2 * query_half, 2 * hidden_half

    def add(parts, residual, gain, rounded, after=()):
        kernel = functools.partial(add_kernel, count, rounded)
        outputs = [(wide, f32), (wide, low)]
        return call(kernel, [*parts, residual, gain], outputs, 2, after=after)

    def add_back(parts, upstream, middle, gain, rounded, after=()):
        kernel = functools.partial(add_back_kernel, count, rounded)
        outputs = [(wide, f32), (wide, low), ((1, width), f32)]
        return call(kernel, [*parts, upstream, middle, gain], outputs, 2, after=after)

    def attention_forward(pieces, weights, found, raw_rows, after=()):
        kernel = functools.partial(attention_forward_kernel, count, part, raw_rows)
        outputs = [(half_wide, low), ((tokens, 2 * (query_half + 2 * key_half)), f32)]
        outputs += [((tokens, heads_wide), low), ((tokens, 2 * key_half), low)]
        outputs += [((tokens, heads_wide), low), ((tokens, heads_wide // HEAD_DIM), f32)]
        operands = [*pieces] + ([found[0]] if raw_rows else [])
        operands += [*weights, cosine, sine, found[2], found[3], *places]
        return call(kernel, operands, outputs, 12, [((tokens, 2 * key_half), low)], after=after)

    def rows_product(left, shares, after=()):
        kernel = functools.partial(rows_kernel, count, not aligned)
        outputs = [(wide, low)] * count + [((left.shape[1], width), low)]
        *parts, whole = call(kernel, [left, *shares], outputs, 4, scalars=[index], after=after)
        return parts, whole

    def lift_forward(pieces, weights, after=()):
        kernel = functools.partial(lift_kernel, count, part)
        outputs = [(half_wide, low)] + [((tokens, hidden_wide), f32)] * 2
        outputs += [((tokens, hidden_wide), low)]
        return call(kernel, [*pieces, *weights], outputs, 6, after=after)

    def mlp_backward(pieces, weights, down, kept, after=()):
        kernel = functools.partial(mlp_backward_kernel, count, part)
        outputs = [(wide, low)] * count + [(half_wide, low), ((tokens, 2 * hidden_wide), low)]
        operands = [*pieces, *weights, down, kept[1], kept[2]]
        *parts, branch, both = call(kernel, operands, outputs, 9, after=after)
        return parts, branch, both

    def attention_backward(pieces, weights, out, found, kept, after=()):
        kernel = functools.partial(attention_backward_kernel, count, part)
        normed, raw, queries, keys, mixed, spread = kept
        outputs = [(wide, low)] * count + [(half_wide, low), (raw.shape, low)]
        outputs += [((1, HEAD_DIM), f32)] * 2
        scratch = [(queries.shape, low), (keys.shape, low), (queries.shape, f32)]
        scratch += [(keys.shape, f32)] * 2
        operands = [*pieces, *weights, out, cosine, sine, found[2], found[3], *places]
        operands += [raw, queries, keys, spread]
        *parts, branch, grad_raw, query, key = call(
            kernel, operands, outputs, 18, scratch, after=after
        )
        return parts, branch, grad_raw, (query, key)

    def weight_grads(left, grads, inner, branch, after=()):
        kernel = functools.partial(weight_grads_kernel, part)
        shape = (depth, grads.shape[1] // (2 * LANES) * part, LANES)
        row_shape = (count, inner.shape[1] // (2 * count) * chunks, LANES)
        outputs = [(shape, f32), (shape, low), (row_shape, f32), (row_shape, low)]
        operands = [left, grads, inner, branch]
        return call(kernel, operands, outputs, 6, [((width, tokens), low)], after=after)

    own = gathered_direct(attention_blocks[0])
    pieces = hops(tie(entering, attention_blocks[0]))
    own = tie(own, pieces)
    qkv_first = [own, swap(own)]
    found_first = split_gains(own)
    if aligned:
        out_first = shared_rows(own[:, qkv_rows:])
    else:
        outs, downs = whole_rows(out_weight, query_half), whole_rows(down_weight, hidden_half)
        out_first = [outs[0], outs[0]]
    kept_attention_first = attention_forward(pieces, qkv_first, found_first, True)
    kept_attention_first, out_first = beside(kept_attention_first, out_first)
    parts, out_first = rows_product(kept_attention_first[4], out_first)
    middle_first, normed = add(met(parts), entering, found_first[1], False)
    own = tie(gathered(tie(mlp_blocks[0], own)), normed)
    lift_first = [own, swap(own)]
    down_first = shared_rows(own[:, lift_rows:]) if aligned else [downs[0], downs[0]]
    kept_mlp_first = lift_forward(hops(normed), lift_first)
    kept_mlp_first, down_first = beside(kept_mlp_first, down_first)
    parts, down_first = rows_product(kept_mlp_first[3], down_first)

    own = tie(gathered(attention_blocks[1]), kept_mlp_first[3])
    qkv_last = [own, swap(own)]
    found_last = split_gains(own)
    out_last = shared_rows(own[:, qkv_rows:]) if aligned else [outs[1], outs[1]]
    hidden_last, normed = add(met(parts), middle_first, found_last[0], True)
    kept_attention_last = attention_forward(
        hops(normed), qkv_last, found_last, False, after=[out_last[1]]
    )
    parts, out_last = rows_product(kept_attention_last[4], out_last)
    middle_last, normed = add(met(parts), hidden_last, found_last[1], False)
    own = tie(gathered(mlp_blocks[1]), normed)
    lift_last = [own, swap(own)]
    down_last = shared_rows(own[:, lift_rows:]) if aligned else [downs[1], downs[1]]
    kept_mlp_last = lift_forward(hops(normed), lift_last)
    kept_mlp_last, down_last = beside(kept_mlp_last, down_last)
    last_parts, down_last = rows_product(kept_mlp_last[3], down_last)

    def meet(grads, swapped):
        own, far, own_rows, far_rows = grads
        if not aligned:
            total = (own + swapped[0].astype(f32)).astype(low)
            return total, [own_rows + swapped[1].astype(f32)]
        outputs = [(own.shape, low)] + [(own_rows.shape[1:], low)] * count
        operands = [own, swapped[0], own_rows, swapped[1]]
        total, *rows_by = call(meet_kernel, operands, outputs, 4, scalars=[index])
        return total, rows_by

    def met_gains(gains):
        split = jnp.concatenate([gain.reshape(depth, -1) for gain in gains], axis=1)
        split = split + swap(split.astype(low)).astype(f32)
        split = jnp.pad(split, ((0, 0), (0, GAIN_ROWS * LANES - split.shape[1])))
        return split.reshape(depth, GAIN_ROWS, LANES).astype(low)

    def laid_out(total, rows_by, gains=None):
        operands = [total] + ([] if gains is None else [gains])
        size = total.shape[1] + (0 if gains is None else GAIN_ROWS)
        if aligned:
            operands += rows_by
            size += rows_by[0].shape[0]
        kernel = functools.partial(layout_kernel, part, gains is not None)
        outputs = [((depth, size, LANES), low)]
        return call(kernel, operands, outputs, 3, scalars=[index])[0]

    def scattered(operand):
        return lax.psum_scatter(operand, "fsdp", scatter_dimension=0, tiled=False)

    def rows_fallback(rest):
        (rest,) = rest
        share = rest.shape[1] // chunks
        rest = rest.reshape(count, chunks, share, LANES).swapaxes(1, 2).reshape(-1, width)
        full = jnp.zeros((2 * count * rest.shape[0], width), low)
        at = (piece * 2 + core) * rest.shape[0]
        full = lax.dynamic_update_slice_in_dim(full, rest.astype(low), at, 0)
        return lax.psum(lax.psum_scatter(full, "fsdp", scatter_dimension=0, tiled=True), "ctx")

    wanted = lax.dynamic_slice_in_dim(slots, piece * rows, rows, 0)
    wanted = ((wanted // rows) ^ piece) * rows + wanted % rows
    chosen = (wanted[:, None] == order[None, :]).astype(low)

    def dealt(pieces):
        return dot(chosen, jnp.concatenate(pieces, axis=0)).astype(low)

    def returned(pieces, layer):
        own = jnp.stack(pieces)
        return own, lax.ppermute(own, "section", [(1 - layer, layer)])

    pieces = hops(cotangent)
    parts, branch, both = mlp_backward(pieces, lift_last, down_last, kept_mlp_last)
    parts = met(parts)
    mlp_grads = weight_grads(kept_mlp_last[0], both, kept_mlp_last[3], branch)
    grad, sent, mlp_gain = add_back(
        parts, cotangent, middle_last, found_last[1], False, after=[mlp_grads[1]]
    )
    swapped = swap(mlp_grads[1]), swap(mlp_grads[3])
    pieces = hops(sent)
    mlp_total, mlp_rows = meet(mlp_grads, swapped)
    results = attention_backward(
        pieces, qkv_last, out_last, found_last, kept_attention_last, after=[mlp_total]
    )
    results, last_parts = beside(results, met(tie(last_parts, pieces[1])))
    parts, branch, grad_raw, head_gains = results
    last = middle_last
    for value in last_parts:
        last = last + value.astype(f32)
    last = last.astype(low)
    mlp_rows = met(mlp_rows)
    parts = met(parts)
    attention_grads = weight_grads(
        kept_attention_last[0], grad_raw, kept_attention_last[4], branch
    )
    mlp_operand = laid_out(mlp_total, mlp_rows)
    mlp_last = scattered(mlp_operand)
    grad, sent, gain = add_back(
        parts, grad, hidden_last, found_last[0], True, after=[attention_grads[1], mlp_operand]
    )
    gains = (gain, mlp_gain, *head_gains)
    down_grad_last = None if aligned else rows_fallback(mlp_rows)

    swapped = swap(attention_grads[1]), swap(attention_grads[3])
    pieces = hops(sent)
    attention_total, attention_rows = meet(attention_grads, swapped)
    results = mlp_backward(
        pieces, lift_first, down_first, kept_mlp_first, after=[attention_total]
    )
    results, last = beside(results, hops(tie(last, pieces[1])))
    parts, branch, both = results
    last = dealt(last)
    attention_rows = met(attention_rows)
    gains = met_gains(gains)
    parts = met(parts)
    attention_operand = laid_out(attention_total, attention_rows, gains)
    mlp_grads = weight_grads(kept_mlp_first[0], both, kept_mlp_first[3], branch)
    attention_last = scattered(attention_operand)
    out_grad_last = None if aligned else rows_fallback(attention_rows)
    grad, sent, mlp_gain = add_back(
        parts,
        grad,
        middle_first,
        found_first[1],
        False,
        after=[mlp_grads[1], attention_operand, mlp_last],
    )
    swapped = swap(mlp_grads[1]), swap(mlp_grads[3])
    pieces = hops(sent)
    mlp_total, mlp_rows = meet(mlp_grads, swapped)
    results = attention_backward(
        pieces, qkv_first, out_first, found_first, kept_attention_first, after=[mlp_total]
    )
    results, mlp_last = beside(results, hops(tie(mlp_last, pieces[1])))
    parts, branch, grad_raw, head_gains = results
    mlp_rows = met(mlp_rows)
    parts = met(parts)
    mlp_operand = laid_out(mlp_total, mlp_rows)
    attention_grads = weight_grads(
        kept_attention_first[0], grad_raw, kept_attention_first[4], branch
    )
    mlp_first = scattered(mlp_operand)
    swapped = swap(attention_grads[1]), swap(attention_grads[3])
    attention_total, attention_rows = meet(attention_grads, swapped)
    attention_rows = met(attention_rows)
    down_grad_first = None if aligned else rows_fallback(mlp_rows)
    grad, sent, gain = add_back(
        parts, grad, entering, found_first[0], True, after=[attention_grads[1], mlp_operand]
    )
    gains = met_gains((gain, mlp_gain, *head_gains))
    attention_operand = laid_out(attention_total, attention_rows, gains)
    attention_first = scattered(attention_operand)
    out_grad_first = None if aligned else rows_fallback(attention_rows)
    attention_last = hops(tie(attention_last, sent))
    mlp_first = hops(tie(mlp_first, attention_last[1]))
    grad = dealt(hops(tie(sent, mlp_first[1])))
    mlp_last, attention_last = returned(mlp_last, 1), returned(attention_last, 1)
    mlp_first = returned(mlp_first, 0)

    def settle(kernel, from_first, from_last, outputs):
        size = from_first[0].shape[1]

        def block_of(layer):
            def at(i, where):
                return jnp.where(where[1] == layer, i ^ where[0], 0), 0, 0

            return pl.BlockSpec((1, size, LANES), at)

        return pl.pallas_call(
            kernel,
            grid_spec=pltpu.PrefetchScalarGridSpec(
                num_scalar_prefetch=1,
                grid=(count,),
                in_specs=[block_of(0), block_of(0), block_of(1), block_of(1)],
                out_specs=[
                    pl.BlockSpec(block, functools.partial(lambda at, i, where: at(i), at))
                    for _, block, at in outputs
                ],
            ),
            out_shape=[jax.ShapeDtypeStruct(shape, f32) for shape, _, _ in outputs],
            compiler_params=pltpu.CompilerParams(vmem_limit_bytes=VMEM_LIMIT),
            cost_estimate=pl.CostEstimate(
                flops=0, bytes_accessed=12 * count * size * LANES, transcendentals=0
            ),
        )(where, *from_first, *from_last)

    def halves_of(where, blocks, body):
        @pl.when(where[1] == 0)
        def _():
            body(0, blocks[0])
            body(1, blocks[1])

        @pl.when(where[1] == 1)
        def _():
            body(1, blocks[2])
            body(0, blocks[3])

    def place_rows(block, at, half, out):
        share = out.shape[1]
        for j in range(chunks):
            out[half, :, span(j, LANES)] = block[0, at + j * share : at + (j + 1) * share, :].astype(f32)

    def mlp_settle_kernel(where, *refs):
        blocks, (gate, up, *down) = refs[:4], refs[4:]

        def body(half, block):
            both = [block[0, span(j, part), :].astype(f32) for j in range(2 * hidden_half // LANES)]
            both = jnp.concatenate(both, axis=1)
            gate[:, span(half, hidden_half)] = both[:, :hidden_half]
            up[:, span(half, hidden_half)] = both[:, hidden_half:]
            if aligned:
                place_rows(block, lift_rows, half, down[0])

        halves_of(where, blocks, body)

    def attention_settle_kernel(where, *refs):
        blocks, (query, key, value, sums, *out) = refs[:4], refs[4:]

        @pl.when(pl.program_id(0) == 0)
        def _():
            sums[...] = jnp.zeros_like(sums)

        def body(half, block):
            query[:, span(half, query_half)] = block[0, :part, :].astype(f32)
            both = block[0, part + GAIN_ROWS : qkv_rows, :].astype(f32)
            key[:, span(half, key_half)] = both[:, :key_half]
            value[:, span(half, key_half)] = both[:, key_half:]
            if half == 0:
                sums[...] += block[0, part : part + GAIN_ROWS, :].astype(f32)
            if aligned:
                place_rows(block, qkv_rows, half, out[0])

        halves_of(where, blocks, body)

    def column_output(size):
        return ((part, 2 * count * size), (part, 2 * size), lambda i: (0, i))

    def row_output(size):
        return ((2, size, width), (2, size // count, width), lambda i: (0, i, 0))

    outputs = [column_output(hidden_half)] * 2 + ([row_output(hidden_half)] if aligned else [])
    grad_gate, grad_up, *grad_down = settle(
        mlp_settle_kernel, mlp_first, mlp_last, outputs
    )
    attention_first = returned(hops(tie(attention_first, grad_gate)), 0)
    outputs = [column_output(query_half)] + [column_output(key_half)] * 2
    outputs += [((GAIN_ROWS, LANES), (GAIN_ROWS, LANES), lambda i: (0, 0))]
    outputs += [row_output(query_half)] if aligned else []
    grad_query, grad_key, grad_value, sums, *grad_out = settle(
        attention_settle_kernel, attention_first, attention_last, outputs
    )
    if aligned:
        grad_out, grad_down = grad_out[0].reshape(-1, width), grad_down[0].reshape(-1, width)
    else:
        pair = []
        for one, two in ((out_grad_first, out_grad_last), (down_grad_first, down_grad_last)):
            own = jnp.where(first, one, two).astype(f32)
            pair.append(own + swap(jnp.where(first, two, one)).astype(f32))
        grad_out, grad_down = pair
    sums = sums.reshape(1, -1)
    split, at = [], 0
    for size in sizes:
        split.append(sums[:, at : at + size])
        at += size

    own = jnp.where(first, grad, last)
    other = swap(jnp.where(first, last, grad))
    boundary = jnp.where(first, jnp.stack([own, other]), jnp.stack([other, own]))
    return (
        boundary[None, None],
        split[0],
        grad_query[None],
        grad_key[None],
        grad_value[None],
        split[2],
        split[3],
        grad_out[None],
        split[1],
        grad_gate[None],
        grad_up[None],
        grad_down[None],
    )


def solution(mesh):
    weight, gain, row = P("section", "fsdp", None), P("section", "fsdp"), P("fsdp", None, None)
    stream = P("section", "fsdp", None, "ctx", None)
    masters = (gain, weight, weight, weight, gain, gain, weight, gain, weight, weight, weight)
    return jax.shard_map(
        shards,
        mesh=mesh,
        in_specs=(stream, row, row) + masters,
        out_specs=(stream,) + masters,
        check_vma=False,
    )
```

```python
import functools

import jax
import jax.numpy as jnp
from jax import lax
from jax.experimental import pallas as pl
from jax.experimental.pallas import tpu as pltpu
from jax.sharding import PartitionSpec as P

HEAD_DIM = 128
GAIN_ROWS = 16
LANES = 256
VMEM_LIMIT = 56 * 1024 * 1024
VMEM_SLACK = 6 * 1024 * 1024
FLOPS_PER_US = 1.15e9
SCALE = HEAD_DIM ** (-0.5)
epsilon = 1e-06
rope_base = 1000000.0
low = jnp.bfloat16
f32 = jnp.float32


def swap(value):
    return lax.ppermute(value, "section", [(0, 1), (1, 0)])


def hop(value, step):
    count = lax.axis_size("ctx")
    return lax.ppermute(value, "ctx", [(i, i ^ step) for i in range(count)])


def hops(own):
    return [own] + [hop(own, k) for k in range(1, lax.axis_size("ctx"))]


def hops_split(own):
    if lax.axis_size("ctx") != 4:
        return hops(own)
    one, two = own[: own.shape[0] // 2], own[own.shape[0] // 2 :]
    one_near, two_near = hop(one, 1), hop(two, 2)
    near = jnp.concatenate([one_near, hop(two, 1)]), jnp.concatenate([hop(one, 2), two_near])
    return [own, *near, jnp.concatenate([hop(one_near, 2), hop(two_near, 1)])]


def met(parts):
    return [parts[0]] + [hop(parts[k], k) for k in range(1, len(parts))]


def beside(results, others):
    return lax.optimization_barrier((results, others))


def tie(value, other):
    return lax.optimization_barrier((value, other))[0]


def xored(pieces, index):
    for bit in range(len(pieces).bit_length() - 1):
        turned = ((index >> bit) & 1) == 1
        pieces = [jnp.where(turned, pieces[j ^ (1 << bit)], v) for j, v in enumerate(pieces)]
    return pieces


def dot(left, right):
    return jnp.dot(left, right, preferred_element_type=f32)


def dot_rows(left, right):
    return lax.dot_general(left, right, (((0,), (0,)), ((), ())), preferred_element_type=f32)


def dot_cols(left, right):
    return lax.dot_general(left, right, (((1,), (1,)), ((), ())), preferred_element_type=f32)


def rms_scale(values, gain):
    scale = lax.rsqrt(jnp.mean(values * values, axis=-1, keepdims=True) + epsilon)
    return values * scale * gain


def rms_back(values, gain, grad):
    scale = lax.rsqrt(jnp.mean(values * values, axis=-1, keepdims=True) + epsilon)
    unit = values * scale
    lifted = grad * gain
    grad_values = (lifted - unit * jnp.mean(lifted * unit, axis=-1, keepdims=True)) * scale
    return grad_values, jnp.sum(grad * unit, axis=0, keepdims=True)


def turn(values, cosine, sine):
    return values * cosine + pltpu.roll(values, HEAD_DIM // 2, 1) * sine


def turn_back(grad, cosine, sine):
    return grad * cosine + pltpu.roll(grad * sine, HEAD_DIM // 2, 1)


def chunk(j, size):
    return pl.ds(pl.multiple_of(j * size, size), size)


def span(j, size):
    return slice(j * size, (j + 1) * size)


def join(pieces, target):
    rows = pieces[0].shape[0]
    for i, piece in enumerate(pieces):
        target[span(i, rows), :] = piece[...]


def deal_out(parts, block, value):
    rows = parts[0].shape[0]
    for i, part in enumerate(parts):
        part[:, block] = value[span(i, rows)].astype(part.dtype)


def call(kernel, operands, outputs, took, scratch=(), scalars=(), after=(), limit=0):
    vmem = pl.BlockSpec(memory_space=pltpu.VMEM)
    smem = pl.BlockSpec(memory_space=pltpu.SMEM)
    anywhere = pl.BlockSpec(memory_space=pl.ANY)
    shapes = [jax.ShapeDtypeStruct(shape, dtype) for shape, dtype in outputs]
    moved = sum(v.size * v.dtype.itemsize for v in [*operands, *shapes])
    skipped, used = len(after), len(scalars)
    held = moved + sum(jnp.dtype(dtype).itemsize * shape[0] * shape[1] for shape, dtype in scratch)

    def body(*refs):
        kernel(*refs[skipped:])

    return pl.pallas_call(
        body,
        out_shape=shapes,
        in_specs=[anywhere] * skipped + [smem] * used + [vmem] * len(operands),
        out_specs=[vmem] * len(shapes),
        scratch_shapes=[pltpu.VMEM(shape, dtype) for shape, dtype in scratch],
        compiler_params=pltpu.CompilerParams(vmem_limit_bytes=limit or held + VMEM_SLACK),
        cost_estimate=pl.CostEstimate(
            flops=int(took * FLOPS_PER_US), bytes_accessed=moved, transcendentals=0
        ),
    )(*after, *scalars, *operands)


def add_kernel(count, rounded, sends_rows, *refs):
    parts, (residual, gain, total, normed) = refs[:count], refs[count:]
    value = residual[...].astype(f32)
    for part in parts:
        value = value + part[...].astype(f32)
    if rounded:
        value = value.astype(low).astype(f32)
    total[...] = value
    normed[...] = (value if sends_rows else rms_scale(value, gain[...])).astype(low)


def add_back_kernel(count, rounded, *refs):
    parts, (upstream, middle, gain, total, sent, grad_gain) = refs[:count], refs[count:]
    grad = parts[0][...].astype(f32)
    for part in parts[1:]:
        grad = grad + part[...].astype(f32)
    grad, gains = rms_back(middle[...].astype(f32), gain[...], grad)
    grad = upstream[...].astype(f32) + grad
    sent[...] = grad.astype(low)
    total[...] = grad.astype(low).astype(f32) if rounded else grad
    grad_gain[...] = gains


def attention_forward_kernel(count, part, raw_rows, *refs):
    pieces, refs = refs[:count], refs[count:]
    if raw_rows:
        gain, chosen, *refs = refs
    own_weight, far_weight, cosine, sine, query_gain, key_gain, start, place, place_row, *refs = refs
    normed, raw, queries, keys, mixed, spread, *refs = refs
    values = refs[-1]
    tokens = normed.shape[0]
    rows = pieces[0].shape[0]
    depth = own_weight.shape[0]
    halves = keys.shape[1] // HEAD_DIM
    group = queries.shape[1] // keys.shape[1]
    step = (group + 2) * HEAD_DIM
    join(pieces, normed)
    if raw_rows:
        refs[0][...] = dot(chosen[:rows, :], normed[...]).astype(low)
        normed[...] = rms_scale(normed[...].astype(f32), gain[...]).astype(low)
    for half, weight in enumerate((own_weight, far_weight)):
        for j, at in enumerate((0, part + GAIN_ROWS)):
            total = None
            for z in range(depth):
                term = dot(normed[:, span(z, part)], weight[z, at : at + part, :])
                total = term if total is None else total + term
            raw[:, span(2 * half + j, LANES)] = total

    for half in range(halves):
        base = half * step
        at = base + group * HEAD_DIM
        own = span(half, HEAD_DIM)
        unit = rms_scale(raw[:, at : at + HEAD_DIM], key_gain[...])
        keys[:, own] = turn(unit, cosine[...], sine[...]).astype(low)
        values[:, own] = raw[:, at + HEAD_DIM : at + 2 * HEAD_DIM].astype(low)
        for g in range(group):
            unit = rms_scale(raw[:, base + g * HEAD_DIM : base + (g + 1) * HEAD_DIM], query_gain[...])
            unit = turn(unit, cosine[...], sine[...])
            queries[:, span(half * group + g, HEAD_DIM)] = unit.astype(low)

    @pl.loop(0, tokens // rows)
    def _(i):
        block = chunk(i, rows)
        visible = (place_row[...] >= start[block, :]) & (place_row[...] <= place[block, :])
        for head in range(halves * group):
            own, at = span(head // group, HEAD_DIM), span(head, HEAD_DIM)
            scores = dot_cols(queries[block, at], keys[:, own]) * SCALE
            scores = jnp.where(visible, scores, -1e30)
            top = jnp.max(scores, axis=-1, keepdims=True)
            raised = jnp.exp(scores - top)
            total = jnp.sum(raised, axis=-1, keepdims=True)
            probs = (raised * (1.0 / total)).astype(low)
            mixed[block, at] = dot(probs, values[:, own]).astype(low)
            spread[block, head : head + 1] = top + jnp.log(total)


def pick_kernel(first_row, index, own, *out):
    for k, share in enumerate(out):
        share[...] = own[index[0] ^ k, first_row:, :]


def rows_kernel(count, ordered, dealt, *refs):
    index, left, *refs = refs
    if dealt:
        chosen, *refs = refs
    given = 1 if ordered else 2 * count
    shares, parts, whole = refs[:given], refs[given : given + count], refs[given + count]
    if ordered:
        whole[...] = shares[0][...]
    else:
        size = whole.shape[0] // 2
        share = size // count
        for k, value in enumerate(shares):
            to = k // count * size + (index[0] ^ (k % count)) * share
            to = pl.ds(pl.multiple_of(to, share), share)
            for j in range(whole.shape[1] // LANES):
                whole[to, span(j, LANES)] = value[span(j, share), :]

    @pl.loop(0, whole.shape[1] // LANES)
    def _(j):
        block = chunk(j, LANES)
        value = dot(left[...], whole[:, block])
        deal_out(parts, block, dot(chosen[...], value.astype(low)) if dealt else value)


def lift_kernel(count, part, raw_rows, *refs):
    pieces, refs = refs[:count], refs[count:]
    if raw_rows:
        gain, chosen, *refs = refs
    own_weight, far_weight, normed, gate, lifted, product, *refs = refs
    half_size = product.shape[1] // 2
    depth = own_weight.shape[0]
    join(pieces, normed)
    if raw_rows:
        refs[0][...] = dot(chosen[: pieces[0].shape[0], :], normed[...]).astype(low)
        normed[...] = rms_scale(normed[...].astype(f32), gain[...]).astype(low)
    for half, weight in enumerate((own_weight, far_weight)):
        both = []
        for j in range(2 * half_size // LANES):
            total = None
            for z in range(depth):
                term = dot(normed[:, span(z, part)], weight[z, span(j, part), :])
                total = term if total is None else total + term
            both.append(total)
        both = jnp.concatenate(both, axis=1)
        one, two = both[:, :half_size], both[:, half_size:]
        at = span(half, half_size)
        gate[:, at] = one
        lifted[:, at] = two
        product[:, at] = (one * jax.nn.sigmoid(one) * two).astype(low)


def mlp_backward_kernel(count, part, *refs):
    pieces, refs = refs[:count], refs[count:]
    own_weight, far_weight, down, gate, lifted, *refs = refs
    parts, (branch, grad_both) = refs[:count], refs[count:]
    size = gate.shape[1] // 2
    depth = own_weight.shape[0]
    join(pieces, branch)
    for half in range(2):
        at = span(half, size)
        grad = dot_cols(branch[...], down[at, :])
        one, two = gate[:, at], lifted[:, at]
        sigmoid = jax.nn.sigmoid(one)
        grad_gate = grad * two * sigmoid * (1.0 + one * (1.0 - sigmoid))
        grad_both[:, span(2 * half, size)] = grad_gate.astype(low)
        grad_both[:, span(2 * half + 1, size)] = (grad * one * sigmoid).astype(low)
    for z in range(depth):
        total = None
        for half, weight in enumerate((own_weight, far_weight)):
            for j in range(2 * size // LANES):
                at = 2 * half * size + j * LANES
                term = dot_cols(grad_both[:, at : at + LANES], weight[z, span(j, part), :])
                total = term if total is None else total + term
        deal_out(parts, span(z, part), total)


def attention_backward_kernel(count, part, dealt, *refs):
    pieces, refs = refs[:count], refs[count:]
    if dealt:
        chosen, *refs = refs
    own_weight, far_weight, out, *refs = refs
    cosine, sine, query_gain, key_gain, start, place, place_row, *refs = refs
    raw, queries, keys, spread, *refs = refs
    parts, refs = refs[:count], refs[count:]
    branch, grad_raw, grad_query_gain, grad_key_gain, *refs = refs
    if dealt:
        dealt_branch, *refs = refs
    grad_mixed, values, grad_queries, grad_keys, grad_values = refs
    tokens, width = branch.shape
    rows = pieces[0].shape[0]
    depth = own_weight.shape[0]
    halves = keys.shape[1] // HEAD_DIM
    group = queries.shape[1] // keys.shape[1]
    step = (group + 2) * HEAD_DIM
    join(pieces, branch)
    if dealt:
        dealt_branch[...] = dot(chosen[:rows, :], branch[...]).astype(low)

    @pl.loop(0, grad_mixed.shape[1] // LANES)
    def _(j):
        block = chunk(j, LANES)
        grad_mixed[:, block] = dot_cols(branch[...], out[block, :]).astype(low)

    for half in range(halves):
        at = half * step + (group + 1) * HEAD_DIM
        values[:, span(half, HEAD_DIM)] = raw[:, at : at + HEAD_DIM].astype(low)
    grad_keys[...] = jnp.zeros_like(grad_keys)
    grad_values[...] = jnp.zeros_like(grad_values)

    @pl.loop(0, tokens // rows)
    def _(i):
        block = chunk(i, rows)
        visible = (place_row[...] >= start[block, :]) & (place_row[...] <= place[block, :])
        for head in range(halves * group):
            own, at = span(head // group, HEAD_DIM), span(head, HEAD_DIM)
            query, grad = queries[block, at], grad_mixed[block, at]
            scores = dot_cols(query, keys[:, own]) * SCALE
            scores = jnp.where(visible, scores, -1e30)
            probs = jnp.exp(scores - spread[block, head : head + 1])
            grad_probs = dot_cols(grad, values[:, own])
            weighted = jnp.sum(probs * grad_probs, axis=-1, keepdims=True)
            grad_scores = (probs * (grad_probs - weighted)).astype(low)
            grad_queries[block, at] = dot(grad_scores, keys[:, own]) * SCALE
            grad_keys[:, own] += dot_rows(grad_scores, query) * SCALE
            grad_values[:, own] += dot_rows(probs.astype(low), grad)

    total_query = jnp.zeros((1, HEAD_DIM), f32)
    total_key = jnp.zeros((1, HEAD_DIM), f32)
    for half in range(halves):
        base = half * step
        own = span(half, HEAD_DIM)
        for g in range(group + 1):
            at = slice(base + g * HEAD_DIM, base + (g + 1) * HEAD_DIM)
            if g < group:
                grad, gain = grad_queries[:, span(half * group + g, HEAD_DIM)], query_gain[...]
            else:
                grad, gain = grad_keys[:, own], key_gain[...]
            grad = turn_back(grad, cosine[...], sine[...])
            grad, grad_gain = rms_back(raw[:, at], gain, grad)
            grad_raw[:, at] = grad.astype(low)
            if g < group:
                total_query += grad_gain
            else:
                total_key += grad_gain
        at = base + (group + 1) * HEAD_DIM
        grad_raw[:, at : at + HEAD_DIM] = grad_values[:, own].astype(low)
    grad_query_gain[...] = total_query
    grad_key_gain[...] = total_key
    for z in range(depth):
        total = None
        for half, weight in enumerate((own_weight, far_weight)):
            for j, at in enumerate((0, part + GAIN_ROWS)):
                grad = grad_raw[:, span(2 * half + j, LANES)]
                term = dot_cols(grad, weight[z, at : at + part, :])
                total = term if total is None else total + term
        if dealt:
            total = dot(chosen[...], total.astype(low))
        deal_out(parts, span(z, part), total)


def weight_grads_kernel(part, left, grads, inner, branch, own, far, own_rows, far_rows, turned):
    depth, count = own.shape[0], own_rows.shape[0]
    chunks = grads.shape[1] // (2 * LANES)
    size = inner.shape[1] // 2
    share = size // count
    for z in range(depth):
        turned[span(z, part), :] = left[:, span(z, part)].T
    for half, target in enumerate((own, far)):
        for j in range(chunks):
            total = dot(turned[...], grads[:, span(half * chunks + j, LANES)])
            for z in range(depth):
                target[z, span(j, part), :] = total[span(z, part)].astype(target.dtype)
    for half, target in enumerate((own_rows, far_rows)):
        rows = inner[:, span(half, size)].T
        for j in range(branch.shape[1] // LANES):
            total = dot(rows, branch[:, span(j, LANES)])
            for k in range(count):
                target[k, span(j, share), :] = total[span(k, share)].astype(target.dtype)


def meet_kernel(index, own, recv, own_rows, recv_rows, total, *rows):
    total[...] = (own[...] + recv[...].astype(f32)).astype(low)
    for k, row in enumerate(rows):
        at = index[0] ^ k
        row[...] = (own_rows[at] + recv_rows[at].astype(f32)).astype(low)


def layout_kernel(count, index, total, *refs):
    *rows, out = refs
    at = total.shape[1]
    out[:, :at, :] = total[...]
    while rows:
        group, rows = rows[:count], rows[count:]
        size = group[0].shape[0]
        for k, row in enumerate(group):
            out[index[0] ^ k, at : at + size, :] = row[...]
        at += size


def shards(
    stream_in,
    lengths,
    dealing,
    attention_gain,
    query_weight,
    key_weight,
    value_weight,
    query_gain,
    key_gain,
    out_weight,
    mlp_gain,
    gate_weight,
    up_weight,
    down_weight,
):
    core = lax.axis_index("section")
    piece = lax.axis_index("ctx")
    count = lax.axis_size("ctx")
    depth = lax.axis_size("fsdp")
    rows, width = stream_in.shape[3], stream_in.shape[4]
    tokens = rows * count
    first = core == 0
    query_half = query_weight.shape[2] // (2 * count)
    key_half = key_weight.shape[2] // (2 * count)
    hidden_half = gate_weight.shape[2] // (2 * count)
    part = query_weight.shape[1]
    aligned = depth == count
    out_share, down_share = query_half // count, hidden_half // count
    index = piece.astype(jnp.int32).reshape(1)
    chunks = width // LANES
    qkv_rows = 2 * part + GAIN_ROWS
    lift_rows = 2 * hidden_half // LANES * part

    where = jnp.stack([piece, core]).astype(jnp.int32)

    def cut(kernel, weights, constants, size):
        def half(i, where):
            return jnp.where(i == 0, 1 - where[1], where[1])

        def columns(i, where):
            return 0, 0, where[0] * 2 + half(i, where)

        def shares(i, where):
            return 0, half(i, where) * count + where[0], 0

        in_specs = [
            pl.BlockSpec((1, height, breadth), shares if by_rows else columns)
            for _, height, breadth, by_rows in weights
        ]
        in_specs += [pl.BlockSpec(v.shape, lambda i, where: (0, 0)) for v in constants]
        return pl.pallas_call(
            kernel,
            grid_spec=pltpu.PrefetchScalarGridSpec(
                num_scalar_prefetch=1,
                grid=(2,),
                in_specs=in_specs,
                out_specs=pl.BlockSpec((1, size, LANES), lambda i, where: (i, 0, 0)),
            ),
            out_shape=jax.ShapeDtypeStruct((2, size, LANES), low),
            compiler_params=pltpu.CompilerParams(vmem_limit_bytes=VMEM_LIMIT),
            cost_estimate=pl.CostEstimate(
                flops=int(3 * FLOPS_PER_US), bytes_accessed=12 * size * LANES, transcendentals=0
            ),
        )(where, *[weight for weight, *_ in weights], *constants)

    def place_shares(weight, out, at):
        share = weight.shape[1]
        for j in range(chunks):
            out[0, at + j * share : at + (j + 1) * share, :] = weight[0, :, span(j, LANES)].astype(low)

    def qkv_cut_kernel(where, query, key, value, *refs):
        *rest, gains, out = refs
        out[0, :part, :] = query[0].astype(low)
        out[0, part : part + GAIN_ROWS, :] = gains[...]
        at = slice(part + GAIN_ROWS, qkv_rows)
        out[0, at, :key_half] = key[0].astype(low)
        out[0, at, key_half:] = value[0].astype(low)
        if aligned:
            place_shares(rest[0], out, qkv_rows)

    def mlp_cut_kernel(where, gate, up, *refs):
        *rest, out = refs
        both = jnp.concatenate([gate[0].astype(low), up[0].astype(low)], axis=1)
        for j in range(2 * hidden_half // LANES):
            out[0, span(j, part), :] = both[:, span(j, LANES)]
        if aligned:
            place_shares(rest[0], out, lift_rows)

    gains = (attention_gain[0], mlp_gain[0], query_gain[0], key_gain[0])
    sizes = [gain.shape[0] for gain in gains]
    gain_block = jnp.concatenate(gains).astype(low)
    gain_block = jnp.pad(gain_block, (0, GAIN_ROWS * LANES - gain_block.shape[0]))
    gain_block = gain_block.reshape(GAIN_ROWS, LANES)

    def by_layer(cuts):
        mine, other = cuts[1], swap(cuts[0])
        return jnp.where(first, mine, other), jnp.where(first, other, mine)

    weights = [(query_weight, part, query_half, False), (key_weight, part, key_half, False)]
    weights += [(value_weight, part, key_half, False)]
    weights += [(out_weight, out_share, width, True)] if aligned else []
    size = qkv_rows + (chunks * out_share if aligned else 0)
    cuts = cut(qkv_cut_kernel, weights, [gain_block], size)
    attention_blocks = by_layer(cuts)
    line = jnp.arange(size, dtype=jnp.int32)[:, None]
    gain_rows = (line >= part) & (line < part + GAIN_ROWS)
    attention_blocks = jnp.where(gain_rows, cuts[1], attention_blocks[0]), attention_blocks[1]
    weights = [(gate_weight, part, hidden_half, False), (up_weight, part, hidden_half, False)]
    weights += [(down_weight, down_share, width, True)] if aligned else []
    size = lift_rows + (chunks * down_share if aligned else 0)
    mlp_blocks = by_layer(cut(mlp_cut_kernel, weights, [], size))

    def gathered(block):
        return lax.all_gather(block, "fsdp", axis=0, tiled=False)

    def whole_rows(weight, size):
        full = lax.all_gather(weight[0].astype(low), "fsdp", axis=0, tiled=True)
        full = lax.dynamic_slice_in_dim(full, piece * 2 * size, 2 * size, 0)
        other = swap(full)
        layers = jnp.where(first, full, other), jnp.where(first, other, full)
        own = [lax.dynamic_slice_in_dim(v, core * size, size, 0) for v in layers]
        far = [lax.dynamic_slice_in_dim(v, (1 - core) * size, size, 0) for v in layers]
        return [jnp.concatenate(pair, axis=0) for pair in zip(own, far)]

    def picked_rows(own, first_row):
        size = own.shape[1] - first_row
        kernel = functools.partial(pick_kernel, first_row)
        return call(kernel, [own], [((size, LANES), low)] * count, 1, scalars=[index])

    def split_gains(own):
        found, at = [], 0
        flat = own[:, part : part + GAIN_ROWS].reshape(depth, -1)
        for size in sizes:
            found.append(flat[:, at : at + size].reshape(1, -1).astype(f32))
            at += size
        return found

    lens = lax.dynamic_index_in_dim(lengths[0], core, 0, keepdims=False)
    slots = lax.dynamic_index_in_dim(dealing[0], core, 0, keepdims=False)
    order = jnp.arange(tokens, dtype=jnp.int32)
    natural = ((order // rows) ^ piece) * rows + order % rows
    bounds = jnp.cumsum(lens)
    passed = (bounds[None, :] <= natural[:, None]).astype(jnp.int32)
    start = jnp.sum(passed * lens[None, :], axis=1)
    position = natural - start
    rates = jnp.power(rope_base, jnp.arange(HEAD_DIM // 2, dtype=f32) * (-2.0 / HEAD_DIM))
    phase = position.astype(f32)[:, None] * rates
    cosine, sine = jnp.cos(phase), jnp.sin(phase)
    cosine = jnp.concatenate([cosine, cosine], axis=-1)
    sine = jnp.concatenate([-sine, sine], axis=-1)
    places = [start[:, None], natural[:, None], natural[None, :]]

    wanted = slots[natural]
    wanted = ((wanted // rows) ^ piece) * rows + wanted % rows
    chosen = (wanted[:, None] == order[None, :]).astype(low)

    own = lax.dynamic_index_in_dim(stream_in[0, 0], core, 0, keepdims=False)
    other = swap(lax.dynamic_index_in_dim(stream_in[0, 0], 1 - core, 0, keepdims=False))
    entering = jnp.where(first, own, other)
    cotangent = jnp.where(first, other, own)

    wide, half_wide = (rows, width), (tokens, width)
    heads_wide, hidden_wide = 2 * query_half, 2 * hidden_half

    def add(parts, residual, gain, rounded, sends_rows=False, after=()):
        kernel = functools.partial(add_kernel, count, rounded, sends_rows)
        outputs = [(wide, f32), (wide, low)]
        return call(kernel, [*parts, residual, gain], outputs, 2, after=after)

    def add_back(parts, upstream, middle, gain, rounded, after=()):
        kernel = functools.partial(add_back_kernel, count, rounded)
        outputs = [(wide, f32), (wide, low), ((1, width), f32)]
        return call(kernel, [*parts, upstream, middle, gain], outputs, 2, after=after)

    def attention_forward(pieces, weights, found, raw_rows, after=()):
        kernel = functools.partial(attention_forward_kernel, count, part, raw_rows)
        outputs = [(half_wide, low), ((tokens, 2 * (query_half + 2 * key_half)), f32)]
        outputs += [((tokens, heads_wide), low), ((tokens, 2 * key_half), low)]
        outputs += [((tokens, heads_wide), low), ((tokens, heads_wide // HEAD_DIM), f32)]
        operands = [*pieces] + ([found[0], chosen] if raw_rows else [])
        outputs += [(wide, low)] if raw_rows else []
        operands += [*weights, cosine, sine, found[2], found[3], *places]
        return call(kernel, operands, outputs, 12, [((tokens, 2 * key_half), low)], after=after)

    def rows_product(left, shares, dealt=False, after=()):
        kernel = functools.partial(rows_kernel, count, not aligned, dealt)
        outputs = [(wide, low)] * count + [((left.shape[1], width), low)]
        operands = [left] + ([chosen] if dealt else []) + [*shares]
        *parts, whole = call(kernel, operands, outputs, 4, scalars=[index], after=after)
        return parts, whole

    def lift_forward(pieces, weights, gain=None, after=()):
        kernel = functools.partial(lift_kernel, count, part, gain is not None)
        outputs = [(half_wide, low)] + [((tokens, hidden_wide), f32)] * 2
        outputs += [((tokens, hidden_wide), low)]
        operands = [*pieces]
        if gain is not None:
            operands += [gain, chosen]
            outputs += [(wide, low)]
        return call(kernel, [*operands, *weights], outputs, 6, after=after)

    def mlp_backward(pieces, weights, down, kept, after=()):
        kernel = functools.partial(mlp_backward_kernel, count, part)
        outputs = [(wide, low)] * count + [(half_wide, low), ((tokens, 2 * hidden_wide), low)]
        operands = [*pieces, *weights, down, kept[1], kept[2]]
        *parts, branch, both = call(kernel, operands, outputs, 9, after=after)
        return parts, branch, both

    def attention_backward(pieces, weights, out, found, kept, dealt=False, after=()):
        kernel = functools.partial(attention_backward_kernel, count, part, dealt)
        normed, raw, queries, keys, mixed, spread = kept
        outputs = [(wide, low)] * count + [(half_wide, low), (raw.shape, low)]
        outputs += [((1, HEAD_DIM), f32)] * 2
        outputs += [(wide, low)] if dealt else []
        scratch = [(queries.shape, low), (keys.shape, low), (queries.shape, f32)]
        scratch += [(keys.shape, f32)] * 2
        operands = [*pieces] + ([chosen] if dealt else [])
        operands += [*weights, out, cosine, sine, found[2], found[3], *places]
        operands += [raw, queries, keys, spread]
        results = call(
            kernel, operands, outputs, 18, scratch, after=after, limit=VMEM_LIMIT
        )
        parts, (branch, grad_raw, query, key, *rest) = results[:count], results[count:]
        return (parts, branch, grad_raw, (query, key), *rest)

    def weight_grads(left, grads, inner, branch, after=()):
        kernel = functools.partial(weight_grads_kernel, part)
        shape = (depth, grads.shape[1] // (2 * LANES) * part, LANES)
        row_shape = (count, inner.shape[1] // (2 * count) * chunks, LANES)
        outputs = [(shape, f32), (shape, low), (row_shape, f32), (row_shape, low)]
        operands = [left, grads, inner, branch]
        return call(kernel, operands, outputs, 6, [((width, tokens), low)], after=after)

    if not aligned:
        outs, downs = whole_rows(out_weight, query_half), whole_rows(down_weight, hidden_half)

    def arrived(value, pieces):
        own = tie(value, pieces)
        return [own, swap(own)]

    def moving_rows(weights, first_row, whole):
        return met(picked_rows(weights[0], first_row)) if aligned else [whole]

    def with_far(shares):
        return [*shares, *map(swap, shares)] if aligned else shares

    pieces = hops(entering)
    cotangents = hops(tie(cotangent, pieces[1]))
    qkv_first = arrived(gathered(attention_blocks[0]), (pieces, cotangents))
    found_own, found_far = split_gains(qkv_first[0]), split_gains(qkv_first[1])
    found_first = [jnp.where(first, own, far) for own, far in zip(found_own, found_far)]
    found_last = [jnp.where(first, far, own) for own, far in zip(found_own, found_far)]
    shares = moving_rows(qkv_first, qkv_rows, None if aligned else outs[0])
    kept_attention_first = attention_forward(pieces, qkv_first, found_first, True)
    kept_attention_first, shares = beside(kept_attention_first, shares)
    *kept_attention_first, dealt_entering = kept_attention_first
    parts, out_first = rows_product(kept_attention_first[4], with_far(shares))
    middle_first, normed = add(met(parts), entering, found_first[1], False)
    pieces = hops(normed)
    lift_first = arrived(gathered(mlp_blocks[0]), pieces)
    shares = moving_rows(lift_first, lift_rows, None if aligned else downs[0])
    kept_mlp_first = lift_forward(pieces, lift_first)
    kept_mlp_first, shares = beside(kept_mlp_first, shares)
    parts, down_first = rows_product(kept_mlp_first[3], with_far(shares))

    hidden_last, normed = add(met(parts), middle_first, found_last[0], True)
    pieces = hops(normed)
    qkv_last = arrived(gathered(attention_blocks[1]), pieces)
    shares = moving_rows(qkv_last, qkv_rows, None if aligned else outs[1])
    kept_attention_last = attention_forward(pieces, qkv_last, found_last, False)
    kept_attention_last, shares = beside(kept_attention_last, shares)
    parts, out_last = rows_product(kept_attention_last[4], with_far(shares))
    middle_last, sent = add(met(parts), hidden_last, found_last[1], False, True)
    pieces = hops(sent)
    lift_last = arrived(gathered(mlp_blocks[1]), pieces)
    shares = moving_rows(lift_last, lift_rows, None if aligned else downs[1])
    kept_mlp_last = lift_forward(pieces, lift_last, found_last[1])
    kept_mlp_last, shares = beside(kept_mlp_last, shares)
    *kept_mlp_last, dealt_middle = kept_mlp_last
    last_parts, down_last = rows_product(kept_mlp_last[3], with_far(shares), True)

    def meet(grads, swapped):
        own, far, own_rows, far_rows = grads
        if not aligned:
            total = (own + swapped[0].astype(f32)).astype(low)
            return total, [own_rows + swapped[1].astype(f32)]
        outputs = [(own.shape, low)] + [(own_rows.shape[1:], low)] * count
        operands = [own, swapped[0], own_rows, swapped[1]]
        total, *rows_by = call(meet_kernel, operands, outputs, 4, scalars=[index])
        return total, rows_by

    def laid_out(total, *rows_by):
        if not aligned:
            return total
        size = total.shape[1] + sum(rows[0].shape[0] for rows in rows_by)
        outputs = [((depth, size, LANES), low)]
        operands = [total] + [row for rows in rows_by for row in rows]
        kernel = functools.partial(layout_kernel, count)
        return call(kernel, operands, outputs, 3, scalars=[index])[0]

    def gains_reduced(from_first, from_last):
        def by_pack(gains):
            return jnp.concatenate([gain.reshape(depth, -1) for gain in gains], axis=1)

        one, two = by_pack(from_first), by_pack(from_last)
        total = jnp.where(first, one, two) + swap(jnp.where(first, two, one))
        pack = lax.axis_index("fsdp")
        summed = lax.dynamic_index_in_dim(total, pack, 0)
        for k in range(1, depth):
            sent = lax.dynamic_index_in_dim(total, pack ^ k, 0)
            summed = summed + lax.ppermute(sent, "fsdp", [(i, i ^ k) for i in range(depth)])
        return sum(hops(summed))

    def scattered(operand):
        return lax.psum_scatter(operand, "fsdp", scatter_dimension=0, tiled=False)

    def met_rows(rows_by):
        return met(rows_by) if aligned else rows_by

    def rows_fallback(rest):
        (rest,) = rest
        share = rest.shape[1] // chunks
        rest = rest.reshape(count, chunks, share, LANES).swapaxes(1, 2).reshape(-1, width)
        full = jnp.zeros((2 * count * rest.shape[0], width), low)
        at = (piece * 2 + core) * rest.shape[0]
        full = lax.dynamic_update_slice_in_dim(full, rest.astype(low), at, 0)
        return lax.psum(lax.psum_scatter(full, "fsdp", scatter_dimension=0, tiled=True), "ctx")

    def returned(pieces, layer):
        own = jnp.stack(pieces)
        return own, lax.ppermute(own, "section", [(1 - layer, layer)])

    def meet_beside(grads, swapped, sent):
        return beside(meet(grads, swapped), hops(sent))

    parts, branch, both = mlp_backward(cotangents, lift_last, down_last, kept_mlp_last)
    mlp_grads = weight_grads(kept_mlp_last[0], both, kept_mlp_last[3], branch)
    mlp_grads, parts = beside(mlp_grads, met(parts))
    swapped = swap(mlp_grads[1]), swap(mlp_grads[3])
    grad, sent, mlp_gain = add_back(parts, cotangent, middle_last, found_last[1], False)
    (total, down_rows), pieces = meet_beside(mlp_grads, swapped, sent)

    results = attention_backward(pieces, qkv_last, out_last, found_last, kept_attention_last, after=[total])
    moving = met(tie(last_parts, pieces[1])), met_rows(down_rows)
    results, (last_parts, moved) = beside(results, moving)
    parts, branch, grad_raw, head_gains = results
    last = dealt_middle.astype(f32)
    for value in last_parts:
        last = last + value.astype(f32)
    last = last.astype(low)
    operand = laid_out(total, moved)
    attention_grads = weight_grads(kept_attention_last[0], grad_raw, kept_attention_last[4], branch)
    (attention_grads, operand), parts = beside((attention_grads, operand), met(parts))
    mlp_last = scattered(operand)
    swapped = swap(attention_grads[1]), swap(attention_grads[3])
    grad, sent, gain = add_back(parts, grad, hidden_last, found_last[0], True)
    gains_last = (gain, mlp_gain, *head_gains)
    down_grad_last = None if aligned else rows_fallback(down_rows)
    (total, out_rows), pieces = meet_beside(attention_grads, swapped, sent)

    results = mlp_backward(pieces, lift_first, down_first, kept_mlp_first, after=[total])
    results, moved = beside(results, met_rows(out_rows))
    parts, branch, both = results
    operand = laid_out(total, moved)
    mlp_grads = weight_grads(kept_mlp_first[0], both, kept_mlp_first[3], branch)
    (mlp_grads, operand, mlp_last), parts = beside((mlp_grads, operand, mlp_last), met(parts))
    attention_last = scattered(operand)
    out_grad_last = None if aligned else rows_fallback(out_rows)
    swapped = swap(mlp_grads[1]), swap(mlp_grads[3])
    grad, sent, mlp_gain = add_back(parts, grad, middle_first, found_first[1], False)
    (total, down_rows), pieces = meet_beside(mlp_grads, swapped, sent)

    results = attention_backward(
        pieces, qkv_first, out_first, found_first, kept_attention_first, True, after=[total]
    )
    mlp_last = tie(mlp_last, pieces[1])
    near = [hop(mlp_last, k) for k in range(1, count - 1)]
    results, (near, moved) = beside(results, (near, met_rows(down_rows)))
    parts, branch, grad_raw, head_gains, dealt_branch = results
    operand = laid_out(total, moved)
    mlp_first = scattered(operand)
    attention_grads = weight_grads(kept_attention_first[0], grad_raw, kept_attention_first[4], branch)
    (attention_grads, _), parts = beside((attention_grads, operand), met(parts))
    swapped = swap(attention_grads[1]), swap(attention_grads[3])
    down_grad_first = None if aligned else rows_fallback(down_rows)
    total, out_rows = meet(attention_grads, swapped)
    moved = met_rows(out_rows)
    operand = laid_out(total, moved)
    out_grad_first = None if aligned else rows_fallback(out_rows)
    attention_last = hops_split(tie(attention_last, parts))
    unused, grad, gain = add_back(
        parts, dealt_branch, dealt_entering, found_first[0], True, after=[operand]
    )
    gains_first = (gain, mlp_gain, *head_gains)
    sums = gains_reduced(gains_first, gains_last)
    mlp_last = [mlp_last, *near, hop(tie(mlp_last, operand), count - 1)]
    mlp_first, operand = beside(mlp_first, operand)
    attention_first = scattered(operand)
    mlp_first, (grad, sums, mlp_last, attention_last) = beside(
        mlp_first, (grad, sums, mlp_last, attention_last)
    )
    mlp_first = hops_split(mlp_first)
    mlp_last, attention_last = returned(mlp_last, 1), returned(attention_last, 1)
    attention_first = hops_split(tie(attention_first, mlp_first))
    mlp_first = returned(mlp_first, 0)

    def settle(kernel, from_first, from_last, outputs):
        size = from_first[0].shape[1]

        def block_of(layer):
            def at(i, where):
                return jnp.where(where[1] == layer, i ^ where[0], 0), 0, 0

            return pl.BlockSpec((1, size, LANES), at)

        return pl.pallas_call(
            kernel,
            grid_spec=pltpu.PrefetchScalarGridSpec(
                num_scalar_prefetch=1,
                grid=(count,),
                in_specs=[block_of(0), block_of(0), block_of(1), block_of(1)],
                out_specs=[
                    pl.BlockSpec(block, functools.partial(lambda at, i, where: at(i), at))
                    for _, block, at in outputs
                ],
            ),
            out_shape=[jax.ShapeDtypeStruct(shape, f32) for shape, _, _ in outputs],
            compiler_params=pltpu.CompilerParams(vmem_limit_bytes=VMEM_LIMIT),
            cost_estimate=pl.CostEstimate(
                flops=0, bytes_accessed=12 * count * size * LANES, transcendentals=0
            ),
        )(where, *from_first, *from_last)

    def halves_of(where, blocks, body):
        @pl.when(where[1] == 0)
        def _():
            body(0, blocks[0])
            body(1, blocks[1])

        @pl.when(where[1] == 1)
        def _():
            body(1, blocks[2])
            body(0, blocks[3])

    def place_rows(block, at, half, out):
        share = out.shape[1]
        for j in range(chunks):
            out[half, :, span(j, LANES)] = block[0, at + j * share : at + (j + 1) * share, :].astype(f32)

    def mlp_settle_kernel(where, *refs):
        blocks, (gate, up, *down) = refs[:4], refs[4:]

        def body(half, block):
            both = [block[0, span(j, part), :].astype(f32) for j in range(2 * hidden_half // LANES)]
            both = jnp.concatenate(both, axis=1)
            gate[:, span(half, hidden_half)] = both[:, :hidden_half]
            up[:, span(half, hidden_half)] = both[:, hidden_half:]
            if aligned:
                place_rows(block, lift_rows, half, down[0])

        halves_of(where, blocks, body)

    def attention_settle_kernel(where, *refs):
        blocks, (query, key, value, *out) = refs[:4], refs[4:]

        def body(half, block):
            query[:, span(half, query_half)] = block[0, :part, :].astype(f32)
            both = block[0, part : 2 * part, :].astype(f32)
            key[:, span(half, key_half)] = both[:, :key_half]
            value[:, span(half, key_half)] = both[:, key_half:]
            if aligned:
                place_rows(block, 2 * part, half, out[0])

        halves_of(where, blocks, body)

    def column_output(size):
        return ((part, 2 * count * size), (part, 2 * size), lambda i: (0, i))

    def row_output(size):
        return ((2, size, width), (2, size // count, width), lambda i: (0, i, 0))

    outputs = [column_output(hidden_half)] * 2 + ([row_output(hidden_half)] if aligned else [])
    settled = settle(mlp_settle_kernel, mlp_first, mlp_last, outputs)
    (grad_gate, grad_up, *grad_down), attention_first = beside(settled, attention_first)
    outputs = [column_output(query_half)] + [column_output(key_half)] * 2
    outputs += [row_output(query_half)] if aligned else []
    grad_query, grad_key, grad_value, *grad_out = settle(
        attention_settle_kernel, returned(attention_first, 0), attention_last, outputs
    )
    if aligned:
        grad_out, grad_down = grad_out[0].reshape(-1, width), grad_down[0].reshape(-1, width)
    else:
        pair = []
        for one, two in ((out_grad_first, out_grad_last), (down_grad_first, down_grad_last)):
            own = jnp.where(first, one, two).astype(f32)
            pair.append(own + swap(jnp.where(first, two, one)).astype(f32))
        grad_out, grad_down = pair
    split, at = [], 0
    for size in sizes:
        split.append(sums[:, at : at + size])
        at += size

    own = jnp.where(first, grad, last)
    other = swap(jnp.where(first, last, grad))
    boundary = jnp.where(first, jnp.stack([own, other]), jnp.stack([other, own]))
    return (
        boundary[None, None],
        split[0],
        grad_query[None],
        grad_key[None],
        grad_value[None],
        split[2],
        split[3],
        grad_out[None],
        split[1],
        grad_gate[None],
        grad_up[None],
        grad_down[None],
    )


def solution(mesh):
    weight, gain, row = P("section", "fsdp", None), P("section", "fsdp"), P("fsdp", None, None)
    stream = P("section", "fsdp", None, "ctx", None)
    masters = (gain, weight, weight, weight, gain, gain, weight, gain, weight, weight, weight)
    return jax.shard_map(
        shards,
        mesh=mesh,
        in_specs=(stream, row, row) + masters,
        out_specs=(stream,) + masters,
        check_vma=False,
    )
```

```python
import functools

import jax
import jax.numpy as jnp
from jax import lax
from jax.experimental import pallas as pl
from jax.experimental.pallas import tpu as pltpu
from jax.sharding import PartitionSpec as P

HEAD_DIM = 128
GAIN_ROWS = 16
LANES = 256
VMEM_LIMIT = 56 * 1024 * 1024
VMEM_SLACK = 6 * 1024 * 1024
FLOPS_PER_US = 1.15e9
SCALE = HEAD_DIM ** (-0.5)
epsilon = 1e-06
rope_base = 1000000.0
low = jnp.bfloat16
f32 = jnp.float32


def swap(value):
    return lax.ppermute(value, "section", [(0, 1), (1, 0)])


def hop(value, step):
    count = lax.axis_size("ctx")
    return lax.ppermute(value, "ctx", [(i, i ^ step) for i in range(count)])


def hops(own):
    return [own] + [hop(own, k) for k in range(1, lax.axis_size("ctx"))]


def hops_split(own):
    if lax.axis_size("ctx") != 4:
        return hops(own)
    one, two = own[: own.shape[0] // 2], own[own.shape[0] // 2 :]
    one_near, two_near = hop(one, 1), hop(two, 2)
    near = jnp.concatenate([one_near, hop(two, 1)]), jnp.concatenate([hop(one, 2), two_near])
    return [own, *near, jnp.concatenate([hop(one_near, 2), hop(two_near, 1)])]


def met(parts):
    return [parts[0]] + [hop(parts[k], k) for k in range(1, len(parts))]


def beside(results, others):
    return lax.optimization_barrier((results, others))


def tie(value, other):
    return lax.optimization_barrier((value, other))[0]


def xored(pieces, index):
    for bit in range(len(pieces).bit_length() - 1):
        turned = ((index >> bit) & 1) == 1
        pieces = [jnp.where(turned, pieces[j ^ (1 << bit)], v) for j, v in enumerate(pieces)]
    return pieces


def dot(left, right):
    return jnp.dot(left, right, preferred_element_type=f32)


def dot_rows(left, right):
    return lax.dot_general(left, right, (((0,), (0,)), ((), ())), preferred_element_type=f32)


def dot_cols(left, right):
    return lax.dot_general(left, right, (((1,), (1,)), ((), ())), preferred_element_type=f32)


def rms_scale(values, gain):
    scale = lax.rsqrt(jnp.mean(values * values, axis=-1, keepdims=True) + epsilon)
    return values * scale * gain


def rms_back(values, gain, grad):
    scale = lax.rsqrt(jnp.mean(values * values, axis=-1, keepdims=True) + epsilon)
    unit = values * scale
    lifted = grad * gain
    grad_values = (lifted - unit * jnp.mean(lifted * unit, axis=-1, keepdims=True)) * scale
    return grad_values, jnp.sum(grad * unit, axis=0, keepdims=True)


def turn(values, cosine, sine):
    return values * cosine + pltpu.roll(values, HEAD_DIM // 2, 1) * sine


def turn_back(grad, cosine, sine):
    return grad * cosine + pltpu.roll(grad * sine, HEAD_DIM // 2, 1)


def chunk(j, size):
    return pl.ds(pl.multiple_of(j * size, size), size)


def span(j, size):
    return slice(j * size, (j + 1) * size)


def join(pieces, target):
    rows = pieces[0].shape[0]
    for i, piece in enumerate(pieces):
        target[span(i, rows), :] = piece[...]


def deal_out(parts, block, value):
    rows = parts[0].shape[0]
    for i, part in enumerate(parts):
        part[:, block] = value[span(i, rows)].astype(part.dtype)


def call(kernel, operands, outputs, took, scratch=(), scalars=(), after=(), limit=0):
    vmem = pl.BlockSpec(memory_space=pltpu.VMEM)
    smem = pl.BlockSpec(memory_space=pltpu.SMEM)
    anywhere = pl.BlockSpec(memory_space=pl.ANY)
    shapes = [jax.ShapeDtypeStruct(shape, dtype) for shape, dtype in outputs]
    moved = sum(v.size * v.dtype.itemsize for v in [*operands, *shapes])
    skipped, used = len(after), len(scalars)
    held = moved + sum(jnp.dtype(dtype).itemsize * shape[0] * shape[1] for shape, dtype in scratch)

    def body(*refs):
        kernel(*refs[skipped:])

    return pl.pallas_call(
        body,
        out_shape=shapes,
        in_specs=[anywhere] * skipped + [smem] * used + [vmem] * len(operands),
        out_specs=[vmem] * len(shapes),
        scratch_shapes=[pltpu.VMEM(shape, dtype) for shape, dtype in scratch],
        compiler_params=pltpu.CompilerParams(vmem_limit_bytes=limit or held + VMEM_SLACK),
        cost_estimate=pl.CostEstimate(
            flops=int(took * FLOPS_PER_US), bytes_accessed=moved, transcendentals=0
        ),
    )(*after, *scalars, *operands)


def mark_kernel(out):
    out[...] = jnp.zeros_like(out)


def mark(*values, took=200):
    return call(mark_kernel, [], [((8, 128), f32)], took, after=values)[0]


def window(values, at, size):
    base = at // 128 * 128
    block = values[:, base : base + LANES]
    return pltpu.roll(block, LANES - (at - base), 1) if at != base else block


def side_by_side(left, right, size):
    if size == LANES:
        return jnp.concatenate([left, right], axis=1)
    lane = lax.broadcasted_iota(jnp.int32, (left.shape[0], 128), 1)
    turned = pltpu.roll(right, size - 128, 1)
    middle = jnp.where(lane < size - 128, left[:, 128:], turned[:, :128])
    return jnp.concatenate([left[:, :128], middle, turned[:, 128:]], axis=1)


def add_kernel(count, rounded, sends_rows, *refs):
    parts, (residual, gain, total, normed) = refs[:count], refs[count:]
    value = residual[...].astype(f32)
    for part in parts:
        value = value + part[...].astype(f32)
    if rounded:
        value = value.astype(low).astype(f32)
    total[...] = value
    normed[...] = (value if sends_rows else rms_scale(value, gain[...])).astype(low)


def add_back_kernel(count, rounded, packs, *refs):
    parts, (upstream, middle, gain, *refs) = refs[:count], refs[count:]
    if packs:
        mlp_gains, query_gains, key_gains, *refs = refs
    total, sent, grad_gain, *packed = refs
    grad = parts[0][...].astype(f32)
    for part in parts[1:]:
        grad = grad + part[...].astype(f32)
    grad, gains = rms_back(middle[...].astype(f32), gain[...], grad)
    grad = upstream[...].astype(f32) + grad
    sent[...] = grad.astype(low)
    total[...] = grad.astype(low).astype(f32) if rounded else grad
    grad_gain[...] = gains
    if packs:
        (packed,) = packed
        packed[...] = jnp.zeros_like(packed)
        for z in range(packed.shape[0]):
            packed[z, 0:1, :] = gains[:, span(z, LANES)]
            packed[z, 1:2, :] = mlp_gains[:, span(z, LANES)]
            packed[z, 2:3, :HEAD_DIM] = query_gains[...]
            packed[z, 2:3, HEAD_DIM:] = key_gains[...]


def attention_forward_kernel(count, part, raw_rows, *refs):
    pieces, refs = refs[:count], refs[count:]
    if raw_rows:
        gain, chosen, *refs = refs
    own_weight, far_weight, cosine, sine, query_gain, key_gain, start, place, place_row, *refs = refs
    normed, raw, queries, keys, mixed, spread, *refs = refs
    values = refs[-1]
    tokens = normed.shape[0]
    rows = pieces[0].shape[0]
    depth = own_weight.shape[0]
    halves = keys.shape[1] // HEAD_DIM
    group = queries.shape[1] // keys.shape[1]
    step = (group + 2) * HEAD_DIM
    join(pieces, normed)
    if raw_rows:
        refs[0][...] = dot(chosen[:rows, :], normed[...]).astype(low)
        normed[...] = rms_scale(normed[...].astype(f32), gain[...]).astype(low)
    for half, weight in enumerate((own_weight, far_weight)):
        for j, at in enumerate((0, part + GAIN_ROWS)):
            total = None
            for z in range(depth):
                term = dot(normed[:, span(z, part)], weight[z, at : at + part, :])
                total = term if total is None else total + term
            raw[:, span(2 * half + j, LANES)] = total

    for half in range(halves):
        base = half * step
        at = base + group * HEAD_DIM
        own = span(half, HEAD_DIM)
        unit = rms_scale(raw[:, at : at + HEAD_DIM], key_gain[...])
        keys[:, own] = turn(unit, cosine[...], sine[...]).astype(low)
        values[:, own] = raw[:, at + HEAD_DIM : at + 2 * HEAD_DIM].astype(low)
        for g in range(group):
            unit = rms_scale(raw[:, base + g * HEAD_DIM : base + (g + 1) * HEAD_DIM], query_gain[...])
            unit = turn(unit, cosine[...], sine[...])
            queries[:, span(half * group + g, HEAD_DIM)] = unit.astype(low)

    @pl.loop(0, tokens // rows)
    def _(i):
        block = chunk(i, rows)
        visible = (place_row[...] >= start[block, :]) & (place_row[...] <= place[block, :])
        visible = jnp.concatenate([visible] * group, axis=0)
        for half in range(halves):
            own = span(half, HEAD_DIM)
            heads = range(half * group, (half + 1) * group)
            query = jnp.concatenate([queries[block, span(h, HEAD_DIM)] for h in heads], axis=0)
            scores = dot_cols(query, keys[:, own]) * SCALE
            scores = jnp.where(visible, scores, -1e30)
            top = jnp.max(scores, axis=-1, keepdims=True)
            raised = jnp.exp(scores - top)
            total = jnp.sum(raised, axis=-1, keepdims=True)
            probs = (raised * (1.0 / total)).astype(low)
            value = dot(probs, values[:, own]).astype(low)
            log_total = top + jnp.log(total)
            for g, head in enumerate(heads):
                mixed[block, span(head, HEAD_DIM)] = value[span(g, rows)]
                spread[block, head : head + 1] = log_total[span(g, rows)]


def pick_kernel(first_row, index, own, *out):
    for k, share in enumerate(out):
        share[...] = own[index[0] ^ k, first_row:, :]


def gather_shares(count, index, shares, whole):
    size = whole.shape[0] // 2
    share = size // count
    for k, value in enumerate(shares):
        to = k // count * size + (index[0] ^ (k % count)) * share
        to = pl.ds(pl.multiple_of(to, share), share)
        for j in range(whole.shape[1] // LANES):
            whole[to, span(j, LANES)] = value[span(j, share), :]


def gather_strided(index, own, far, whole):
    depth, core = own.shape[0], index[1]
    chunks = whole.shape[1] // LANES
    share = whole.shape[0] // depth
    half = share // 2
    at = own.shape[1] - chunks * half
    for z in range(depth):
        place = (z // (depth // 2) ^ core) * (depth // 2) + z % (depth // 2)
        for value, carried in ((own, core), (far, 1 - core)):
            to = pl.ds(pl.multiple_of(place * share + carried * half, 32), half)
            for j in range(chunks):
                whole[to, span(j, LANES)] = value[z, at + j * half : at + (j + 1) * half, :]


def gather_rows(form, count, index, given, whole):
    if form == "whole":
        whole[...] = given[0][...]
    elif form == "shares":
        gather_shares(count, index, given, whole)
    else:
        gather_strided(index, *given, whole)


def rows_kernel(count, form, dealt, index, left, *refs):
    if dealt:
        chosen, *refs = refs
    given, refs = refs[: -count - 1], refs[-count - 1 :]
    parts, whole = refs[:count], refs[count]
    gather_rows(form, count, index, given, whole)

    @pl.loop(0, whole.shape[1] // LANES)
    def _(j):
        block = chunk(j, LANES)
        value = dot(left[...], whole[:, block])
        deal_out(parts, block, dot(chosen[...], value.astype(low)) if dealt else value)


def lift_kernel(count, part, raw_rows, *refs):
    pieces, refs = refs[:count], refs[count:]
    if raw_rows:
        gain, chosen, *refs = refs
    own_weight, far_weight, normed, gate, lifted, product, *refs = refs
    half_size = product.shape[1] // 2
    depth = own_weight.shape[0]
    join(pieces, normed)
    if raw_rows:
        refs[0][...] = dot(chosen[: pieces[0].shape[0], :], normed[...]).astype(low)
        normed[...] = rms_scale(normed[...].astype(f32), gain[...]).astype(low)
    for half, weight in enumerate((own_weight, far_weight)):
        both = []
        for j in range(2 * half_size // LANES):
            total = None
            for z in range(depth):
                term = dot(normed[:, span(z, part)], weight[z, span(j, part), :])
                total = term if total is None else total + term
            both.append(total)
        both = jnp.concatenate(both, axis=1)
        one, two = both[:, :half_size], both[:, half_size:]
        at = span(half, half_size)
        gate[:, at] = one
        lifted[:, at] = two
        product[:, at] = (one * jax.nn.sigmoid(one) * two).astype(low)


def mlp_forward_kernel(count, part, form, index, *refs):
    pieces, refs = refs[:count], refs[count:]
    weights, refs = refs[:2], refs[2:]
    given, refs = (weights, refs) if form == "strided" else (refs[:1], refs[1:])
    kept, (*parts, whole) = refs[:4], refs[4:]
    lift_kernel(count, part, False, *pieces, *weights, *kept)
    rows_kernel(count, form, False, index, kept[3], *given, *parts, whole)


def mlp_backward_kernel(count, part, form, index, *refs):
    pieces, refs = refs[:count], refs[count:]
    own_weight, far_weight, gate, lifted, *refs = refs
    if form == "strided":
        given = [own_weight, far_weight]
    else:
        given, refs = refs[:1], refs[1:]
    parts, (branch, grad_both, down) = refs[:count], refs[count:]
    gather_rows(form, count, index, given, down)
    size = gate.shape[1] // 2
    depth = own_weight.shape[0]
    join(pieces, branch)
    for half in range(2):
        at = span(half, size)
        grad = dot_cols(branch[...], down[at, :])
        one, two = gate[:, at], lifted[:, at]
        sigmoid = jax.nn.sigmoid(one)
        grad_gate = grad * two * sigmoid * (1.0 + one * (1.0 - sigmoid))
        grad_both[:, span(2 * half, size)] = grad_gate.astype(low)
        grad_both[:, span(2 * half + 1, size)] = (grad * one * sigmoid).astype(low)
    for z in range(depth):
        total = None
        for half, weight in enumerate((own_weight, far_weight)):
            for j in range(2 * size // LANES):
                at = 2 * half * size + j * LANES
                term = dot_cols(grad_both[:, at : at + LANES], weight[z, span(j, part), :])
                total = term if total is None else total + term
        deal_out(parts, span(z, part), total)


def attention_backward_kernel(count, part, dealt, *refs):
    pieces, refs = refs[:count], refs[count:]
    if dealt:
        chosen, *refs = refs
    own_weight, far_weight, out, *refs = refs
    cosine, sine, query_gain, key_gain, start, place, place_row, *refs = refs
    raw, queries, keys, spread, *refs = refs
    parts, refs = refs[:count], refs[count:]
    branch, grad_raw, grad_query_gain, grad_key_gain, *refs = refs
    if dealt:
        dealt_branch, *refs = refs
    grad_mixed, values, grad_queries, grad_keys, grad_values = refs
    tokens, width = branch.shape
    rows = pieces[0].shape[0]
    depth = own_weight.shape[0]
    halves = keys.shape[1] // HEAD_DIM
    group = queries.shape[1] // keys.shape[1]
    step = (group + 2) * HEAD_DIM
    join(pieces, branch)
    if dealt:
        dealt_branch[...] = dot(chosen[:rows, :], branch[...]).astype(low)

    @pl.loop(0, grad_mixed.shape[1] // LANES)
    def _(j):
        block = chunk(j, LANES)
        grad_mixed[:, block] = dot_cols(branch[...], out[block, :]).astype(low)

    for half in range(halves):
        at = half * step + (group + 1) * HEAD_DIM
        values[:, span(half, HEAD_DIM)] = raw[:, at : at + HEAD_DIM].astype(low)
    grad_keys[...] = jnp.zeros_like(grad_keys)
    grad_values[...] = jnp.zeros_like(grad_values)

    @pl.loop(0, tokens // rows)
    def _(i):
        block = chunk(i, rows)
        visible = (place_row[...] >= start[block, :]) & (place_row[...] <= place[block, :])
        visible = jnp.concatenate([visible] * group, axis=0)
        for half in range(halves):
            own = span(half, HEAD_DIM)
            heads = range(half * group, (half + 1) * group)
            query = jnp.concatenate([queries[block, span(h, HEAD_DIM)] for h in heads], axis=0)
            grad = jnp.concatenate([grad_mixed[block, span(h, HEAD_DIM)] for h in heads], axis=0)
            log_total = jnp.concatenate([spread[block, h : h + 1] for h in heads], axis=0)
            scores = dot_cols(query, keys[:, own]) * SCALE
            scores = jnp.where(visible, scores, -1e30)
            probs = jnp.exp(scores - log_total)
            grad_probs = dot_cols(grad, values[:, own])
            weighted = jnp.sum(probs * grad_probs, axis=-1, keepdims=True)
            grad_scores = (probs * (grad_probs - weighted)).astype(low)
            grad_query = dot(grad_scores, keys[:, own]) * SCALE
            for g, head in enumerate(heads):
                grad_queries[block, span(head, HEAD_DIM)] = grad_query[span(g, rows)]
            grad_keys[:, own] += dot_rows(grad_scores, query) * SCALE
            grad_values[:, own] += dot_rows(probs.astype(low), grad)

    total_query = jnp.zeros((1, HEAD_DIM), f32)
    total_key = jnp.zeros((1, HEAD_DIM), f32)
    for half in range(halves):
        base = half * step
        own = span(half, HEAD_DIM)
        for g in range(group + 1):
            at = slice(base + g * HEAD_DIM, base + (g + 1) * HEAD_DIM)
            if g < group:
                grad, gain = grad_queries[:, span(half * group + g, HEAD_DIM)], query_gain[...]
            else:
                grad, gain = grad_keys[:, own], key_gain[...]
            grad = turn_back(grad, cosine[...], sine[...])
            grad, grad_gain = rms_back(raw[:, at], gain, grad)
            grad_raw[:, at] = grad.astype(low)
            if g < group:
                total_query += grad_gain
            else:
                total_key += grad_gain
        at = base + (group + 1) * HEAD_DIM
        grad_raw[:, at : at + HEAD_DIM] = grad_values[:, own].astype(low)
    grad_query_gain[...] = total_query
    grad_key_gain[...] = total_key
    for z in range(depth):
        total = None
        for half, weight in enumerate((own_weight, far_weight)):
            for j, at in enumerate((0, part + GAIN_ROWS)):
                grad = grad_raw[:, span(2 * half + j, LANES)]
                term = dot_cols(grad, weight[z, at : at + part, :])
                total = term if total is None else total + term
        if dealt:
            total = dot(chosen[...], total.astype(low))
        deal_out(parts, span(z, part), total)


def weight_grads_kernel(part, strided, index, left, grads, inner, branch, own, far, *refs):
    *rows_out, turned = refs
    depth = own.shape[0]
    chunks = grads.shape[1] // (2 * LANES)
    size = inner.shape[1] // 2
    for z in range(depth):
        turned[span(z, part), :] = left[:, span(z, part)].T
    for half, target in enumerate((own, far)):
        for j in range(chunks):
            total = dot(turned[...], grads[:, span(half * chunks + j, LANES)])
            for z in range(depth):
                target[z, span(j, part), :] = total[span(z, part)].astype(target.dtype)
    for half in range(2):
        rows = inner[:, span(half, size)].T
        for j in range(branch.shape[1] // LANES):
            total = dot(rows, branch[:, span(j, LANES)])
            if strided:
                share = size // (depth // 2)
                carried = share // 2
                at = slice(chunks * part + j * carried, chunks * part + (j + 1) * carried)
                for i in range(depth // 2):
                    z = (index[1] ^ half) * (depth // 2) + i
                    block = total[span(i, share)]
                    one, two = block[:carried], block[carried:]
                    own[z, at, :] = jnp.where(index[1] == 0, one, two)
                    far[z, at, :] = jnp.where(index[1] == 0, two, one).astype(far.dtype)
            else:
                target = rows_out[half]
                count = target.shape[0]
                share = size // count
                for k in range(count):
                    target[k, span(j, share), :] = total[span(k, share)].astype(target.dtype)


def sum_kernel(own, recv, total):
    total[...] = (own[...] + recv[...].astype(f32)).astype(low)


def meet_kernel(index, own, recv, own_rows, recv_rows, total, *rows):
    total[...] = (own[...] + recv[...].astype(f32)).astype(low)
    for k, row in enumerate(rows):
        at = index[0] ^ k
        row[...] = (own_rows[at] + recv_rows[at].astype(f32)).astype(low)


def layout_kernel(index, total, gains, far_gains, *refs):
    *rows, out = refs
    at = total.shape[1]
    end = at + rows[0].shape[0]
    out[:, :at, :] = total[...]
    for k, row in enumerate(rows):
        out[index[0] ^ k, at:end, :] = row[...]
    out[:, end:, :] = (gains[...] + far_gains[...]).astype(low)


def shards(
    stream_in,
    lengths,
    dealing,
    attention_gain,
    query_weight,
    key_weight,
    value_weight,
    query_gain,
    key_gain,
    out_weight,
    mlp_gain,
    gate_weight,
    up_weight,
    down_weight,
):
    core = lax.axis_index("section")
    piece = lax.axis_index("ctx")
    count = lax.axis_size("ctx")
    depth = lax.axis_size("fsdp")
    rows, width = stream_in.shape[3], stream_in.shape[4]
    tokens = rows * count
    first = core == 0
    query_half = query_weight.shape[2] // (2 * count)
    key_half = key_weight.shape[2] // (2 * count)
    hidden_half = gate_weight.shape[2] // (2 * count)
    part = query_weight.shape[1]
    aligned = depth == count == 4
    out_share, down_share = query_half // count, hidden_half // count
    index = jnp.stack([piece, core]).astype(jnp.int32)
    chunks = width // LANES
    qkv_rows = 2 * part + GAIN_ROWS
    lift_rows = 2 * hidden_half // LANES * part

    own = lax.dynamic_index_in_dim(stream_in[0, 0], core, 0, keepdims=False)
    other = swap(lax.dynamic_index_in_dim(stream_in[0, 0], 1 - core, 0, keepdims=False))
    entering = jnp.where(first, own, other)
    cotangent = jnp.where(first, other, own)

    entering_pieces = hops(entering)

    where = jnp.stack([piece, core]).astype(jnp.int32)

    def cut(kernel, weights, constants, size, after=None):
        def half(i, where):
            return jnp.where(i == 0, 1 - where[1], where[1])

        def columns(i, where):
            return 0, 0, where[0] * 2 + half(i, where)

        def shares(i, where):
            return 0, half(i, where) * count + where[0], 0

        def even(i, where):
            return 0, 0, half(i, where) * 2

        def odd(i, where):
            return 0, 0, half(i, where) * 2 + 1

        def carried(i, where):
            return 0, where[0] * 2 + half(i, where), 0

        maps = {"columns": columns, "shares": shares, "even": even, "odd": odd, "carried": carried}
        in_specs = [
            pl.BlockSpec((1, height, breadth), maps[which]) for _, height, breadth, which in weights
        ]
        in_specs += [pl.BlockSpec(v.shape, lambda i, where: (0, 0)) for v in constants]
        return pl.pallas_call(
            kernel,
            grid_spec=pltpu.PrefetchScalarGridSpec(
                num_scalar_prefetch=1,
                grid=(2,),
                in_specs=in_specs,
                out_specs=pl.BlockSpec((1, size, LANES), lambda i, where: (i, 0, 0)),
            ),
            out_shape=jax.ShapeDtypeStruct((2, size, LANES), low),
            compiler_params=pltpu.CompilerParams(vmem_limit_bytes=VMEM_LIMIT),
            cost_estimate=pl.CostEstimate(
                flops=int(3 * FLOPS_PER_US), bytes_accessed=12 * size * LANES, transcendentals=0
            ),
        )(tie(where, after), *[weight for weight, *_ in weights], *constants)

    def place_shares(weight, out, at):
        share = weight.shape[1]
        for j in range(chunks):
            out[0, at + j * share : at + (j + 1) * share, :] = weight[0, :, span(j, LANES)].astype(low)

    def qkv_cut_kernel(where, query, key, value, *refs):
        *rest, gains, out = refs
        out[0, :part, :] = query[0].astype(low)
        out[0, part : part + GAIN_ROWS, :] = gains[...]
        at = slice(part + GAIN_ROWS, qkv_rows)
        out[0, at, :key_half] = key[0].astype(low)
        out[0, at, key_half:] = value[0].astype(low)
        if aligned:
            place_shares(rest[0], out, qkv_rows)

    def mlp_cut_kernel(where, gate, up, out):
        both = jnp.concatenate([gate[0].astype(low), up[0].astype(low)], axis=1)
        for j in range(2 * hidden_half // LANES):
            out[0, span(j, part), :] = both[:, span(j, LANES)]

    def strided_cut_kernel(where, gate, gate_next, up, up_next, down, out):
        share = hidden_half // 2

        for c in range(count):

            @pl.when(where[0] == c)
            def _(c=c):
                sides = [window(v[0], c * share, share) for v in (gate, gate_next, up, up_next)]
                both = [side_by_side(*sides[:2], share), side_by_side(*sides[2:], share)]
                both = jnp.concatenate(both, axis=1).astype(low)
                for j in range(2 * hidden_half // LANES):
                    out[0, span(j, part), :] = both[:, span(j, LANES)]

        place_shares(down, out, lift_rows)

    gains = (attention_gain[0], mlp_gain[0], query_gain[0], key_gain[0])
    sizes = [gain.shape[0] for gain in gains]
    gain_block = jnp.concatenate(gains).astype(low)
    gain_block = jnp.pad(gain_block, (0, GAIN_ROWS * LANES - gain_block.shape[0]))
    gain_block = gain_block.reshape(GAIN_ROWS, LANES)

    def by_layer(cuts):
        mine, other = cuts[1], swap(cuts[0])
        return jnp.where(first, mine, other), jnp.where(first, other, mine)

    weights = [(query_weight, part, query_half, "columns"), (key_weight, part, key_half, "columns")]
    weights += [(value_weight, part, key_half, "columns")]
    weights += [(out_weight, out_share, width, "shares")] if aligned else []
    size = qkv_rows + (chunks * out_share if aligned else 0)
    cuts = cut(qkv_cut_kernel, weights, [gain_block], size)
    attention_blocks = by_layer(cuts)
    line = jnp.arange(size, dtype=jnp.int32)[:, None]
    gain_rows = (line >= part) & (line < part + GAIN_ROWS)
    attention_blocks = jnp.where(gain_rows, cuts[1], attention_blocks[0]), attention_blocks[1]
    if aligned:
        block = 2 * hidden_half
        weights = [(gate_weight, part, block, "even"), (gate_weight, part, block, "odd")]
        weights += [(up_weight, part, block, "even"), (up_weight, part, block, "odd")]
        weights += [(down_weight, down_share, width, "carried")]
        size = lift_rows + chunks * down_share
        mlp_blocks = by_layer(cut(strided_cut_kernel, weights, [], size, entering_pieces[1]))
    else:
        weights = [(gate_weight, part, hidden_half, "columns"), (up_weight, part, hidden_half, "columns")]
        mlp_blocks = by_layer(cut(mlp_cut_kernel, weights, [], lift_rows))

    def gathered(block):
        return lax.all_gather(block, "fsdp", axis=0, tiled=False)

    def whole_rows(weight, size):
        full = lax.all_gather(weight[0].astype(low), "fsdp", axis=0, tiled=True)
        full = lax.dynamic_slice_in_dim(full, piece * 2 * size, 2 * size, 0)
        other = swap(full)
        layers = jnp.where(first, full, other), jnp.where(first, other, full)
        own = [lax.dynamic_slice_in_dim(v, core * size, size, 0) for v in layers]
        far = [lax.dynamic_slice_in_dim(v, (1 - core) * size, size, 0) for v in layers]
        return [jnp.concatenate(pair, axis=0) for pair in zip(own, far)]

    def picked_rows(own, first_row):
        size = own.shape[1] - first_row
        kernel = functools.partial(pick_kernel, first_row)
        return call(kernel, [own], [((size, LANES), low)] * count, 1, scalars=[index])

    def split_gains(own):
        found, at = [], 0
        flat = own[:, part : part + GAIN_ROWS].reshape(depth, -1)
        for size in sizes:
            found.append(flat[:, at : at + size].reshape(1, -1).astype(f32))
            at += size
        return found

    lens = lax.dynamic_index_in_dim(lengths[0], core, 0, keepdims=False)
    slots = lax.dynamic_index_in_dim(dealing[0], core, 0, keepdims=False)
    order = jnp.arange(tokens, dtype=jnp.int32)
    natural = ((order // rows) ^ piece) * rows + order % rows
    bounds = jnp.cumsum(lens)
    passed = (bounds[None, :] <= natural[:, None]).astype(jnp.int32)
    start = jnp.sum(passed * lens[None, :], axis=1)
    position = natural - start
    rates = jnp.power(rope_base, jnp.arange(HEAD_DIM // 2, dtype=f32) * (-2.0 / HEAD_DIM))
    phase = position.astype(f32)[:, None] * rates
    cosine, sine = jnp.cos(phase), jnp.sin(phase)
    cosine = jnp.concatenate([cosine, cosine], axis=-1)
    sine = jnp.concatenate([-sine, sine], axis=-1)
    places = [start[:, None], natural[:, None], natural[None, :]]

    wanted = slots.reshape(count, rows)
    wanted = jnp.concatenate(xored([wanted[j] for j in range(count)], piece))
    wanted = ((wanted // rows) ^ piece) * rows + wanted % rows
    chosen = (wanted[:, None] == order[None, :]).astype(low)

    wide, half_wide = (rows, width), (tokens, width)
    heads_wide, hidden_wide = 2 * query_half, 2 * hidden_half

    def add(parts, residual, gain, rounded, sends_rows=False, after=()):
        kernel = functools.partial(add_kernel, count, rounded, sends_rows)
        outputs = [(wide, f32), (wide, low)]
        return call(kernel, [*parts, residual, gain], outputs, 2, after=after)

    def add_back(parts, upstream, middle, gain, rounded, gains=(), after=()):
        packs = aligned and len(gains) > 0
        kernel = functools.partial(add_back_kernel, count, rounded, packs)
        outputs = [(wide, f32), (wide, low), ((1, width), f32)]
        outputs += [((depth, GAIN_ROWS, LANES), f32)] if packs else []
        operands = [*parts, upstream, middle, gain] + (list(gains) if packs else [])
        return call(kernel, operands, outputs, 2, after=after)

    def attention_forward(pieces, weights, found, raw_rows, after=()):
        kernel = functools.partial(attention_forward_kernel, count, part, raw_rows)
        outputs = [(half_wide, low), ((tokens, 2 * (query_half + 2 * key_half)), f32)]
        outputs += [((tokens, heads_wide), low), ((tokens, 2 * key_half), low)]
        outputs += [((tokens, heads_wide), low), ((tokens, heads_wide // HEAD_DIM), f32)]
        operands = [*pieces] + ([found[0], chosen] if raw_rows else [])
        outputs += [(wide, low)] if raw_rows else []
        operands += [*weights, cosine, sine, found[2], found[3], *places]
        return call(kernel, operands, outputs, 12, [((tokens, 2 * key_half), low)], after=after)

    def rows_product(form, left, given, dealt=False, after=()):
        kernel = functools.partial(rows_kernel, count, form, dealt)
        outputs = [(wide, low)] * count + [((left.shape[1], width), low)]
        operands = [left] + ([chosen] if dealt else []) + [*given]
        *parts, whole = call(kernel, operands, outputs, 4, scalars=[index], after=after)
        return parts, whole

    def lift_forward(pieces, weights, gain=None, after=()):
        kernel = functools.partial(lift_kernel, count, part, gain is not None)
        outputs = [(half_wide, low)] + [((tokens, hidden_wide), f32)] * 2
        outputs += [((tokens, hidden_wide), low)]
        operands = [*pieces]
        if gain is not None:
            operands += [gain, chosen]
            outputs += [(wide, low)]
        return call(kernel, [*operands, *weights], outputs, 6, after=after)

    def mlp_forward(pieces, weights, form, down):
        kernel = functools.partial(mlp_forward_kernel, count, part, form)
        outputs = [(half_wide, low)] + [((tokens, hidden_wide), f32)] * 2
        outputs += [((tokens, hidden_wide), low)] + [(wide, low)] * count
        outputs += [((hidden_wide, width), low)]
        operands = [*pieces, *weights] + ([] if form == "strided" else [down])
        *results, whole = call(kernel, operands, outputs, 8, scalars=[index])
        return results[:4], results[4:], whole

    def mlp_backward(pieces, weights, form, down, kept, after=()):
        kernel = functools.partial(mlp_backward_kernel, count, part, form)
        outputs = [(wide, low)] * count + [(half_wide, low), ((tokens, 2 * hidden_wide), low)]
        outputs += [((hidden_wide, width), low)]
        operands = [*pieces, *weights, kept[1], kept[2]] + ([] if form == "strided" else [down])
        results = call(kernel, operands, outputs, 6, scalars=[index], after=after)
        parts, (branch, both, whole) = results[:count], results[count:]
        return parts, branch, both, whole

    def attention_backward(pieces, weights, out, found, kept, dealt=False, after=()):
        kernel = functools.partial(attention_backward_kernel, count, part, dealt)
        normed, raw, queries, keys, mixed, spread = kept
        outputs = [(wide, low)] * count + [(half_wide, low), (raw.shape, low)]
        outputs += [((1, HEAD_DIM), f32)] * 2
        outputs += [(wide, low)] if dealt else []
        scratch = [(queries.shape, low), (keys.shape, low), (queries.shape, f32)]
        scratch += [(keys.shape, f32)] * 2
        operands = [*pieces] + ([chosen] if dealt else [])
        operands += [*weights, out, cosine, sine, found[2], found[3], *places]
        operands += [raw, queries, keys, spread]
        results = call(
            kernel, operands, outputs, 18, scratch, after=after
        )
        parts, (branch, grad_raw, query, key, *rest) = results[:count], results[count:]
        return (parts, branch, grad_raw, (query, key), *rest)

    def weight_grads(left, grads, inner, branch, strided=False, after=()):
        kernel = functools.partial(weight_grads_kernel, part, strided)
        size = grads.shape[1] // (2 * LANES) * part
        row_shape = (count, inner.shape[1] // (2 * count) * chunks, LANES)
        if strided:
            size += row_shape[1]
        outputs = [((depth, size, LANES), f32), ((depth, size, LANES), low)]
        outputs += [] if strided else [(row_shape, f32), (row_shape, low)]
        operands = [left, grads, inner, branch]
        scratch = [((width, tokens), low)]
        return call(kernel, operands, outputs, 6, scratch, scalars=[index], after=after)

    if not aligned:
        outs, downs = whole_rows(out_weight, query_half), whole_rows(down_weight, hidden_half)

    def arrived(value, after):
        own = tie(value, after)
        return [own, swap(own)]

    def moving_rows(weights, first_row, whole):
        return met(picked_rows(weights[0], first_row)) if aligned else [whole]

    def with_far(shares):
        return [*shares, *map(swap, shares)] if aligned else shares

    out_form, down_form = ("shares", "strided") if aligned else ("whole", "whole")
    pieces = entering_pieces
    cotangents = hops(tie(cotangent, pieces[1]))
    early = pieces, cotangents, mlp_blocks, attention_blocks[1], chosen, cosine, sine, places
    qkv_first = arrived(gathered(attention_blocks[0]), early)
    found_own, found_far = split_gains(qkv_first[0]), split_gains(qkv_first[1])
    found_first = [jnp.where(first, own, far) for own, far in zip(found_own, found_far)]
    found_last = [jnp.where(first, far, own) for own, far in zip(found_own, found_far)]
    shares = moving_rows(qkv_first, qkv_rows, None if aligned else outs[0])
    kept_attention_first = attention_forward(pieces, qkv_first, found_first, True)
    kept_attention_first, shares = beside(kept_attention_first, shares)
    *kept_attention_first, dealt_entering = kept_attention_first
    parts, out_first = rows_product(out_form, kept_attention_first[4], with_far(shares))
    middle_first, normed = add(met(parts), entering, found_first[1], False)
    pieces = hops(normed)
    lift_first = arrived(gathered(mlp_blocks[0]), pieces)
    kept_mlp_first, parts, down_first = mlp_forward(
        pieces, lift_first, down_form, None if aligned else downs[0]
    )

    hidden_last, normed = add(met(parts), middle_first, found_last[0], True)
    pieces = hops(normed)
    qkv_last = arrived(gathered(attention_blocks[1]), pieces)
    shares = moving_rows(qkv_last, qkv_rows, None if aligned else outs[1])
    kept_attention_last = attention_forward(pieces, qkv_last, found_last, False)
    kept_attention_last, shares = beside(kept_attention_last, shares)
    parts, out_last = rows_product(out_form, kept_attention_last[4], with_far(shares))
    middle_last, sent = add(met(parts), hidden_last, found_last[1], False, True)
    pieces = hops(sent)
    lift_last = arrived(gathered(mlp_blocks[1]), pieces)
    *kept_mlp_last, dealt_middle = lift_forward(pieces, lift_last, found_last[1])

    def meet(grads, swapped):
        own, far, own_rows, far_rows = grads
        if not aligned:
            total = (own + swapped[0].astype(f32)).astype(low)
            return total, [own_rows + swapped[1].astype(f32)]
        outputs = [(own.shape, low)] + [(own_rows.shape[1:], low)] * count
        operands = [own, swapped[0], own_rows, swapped[1]]
        total, *rows_by = call(meet_kernel, operands, outputs, 4, scalars=[index])
        return total, rows_by

    def laid_out(total, rows_by, packed):
        if not aligned:
            return total
        size = total.shape[1] + rows_by[0].shape[0] + GAIN_ROWS
        outputs = [((depth, size, LANES), low)]
        operands = [total, packed[0], swap(packed[0]), *rows_by]
        return call(layout_kernel, operands, outputs, 3, scalars=[index])[0]

    def gains_reduced(from_first, from_last):
        def by_pack(gains):
            return jnp.concatenate([gain.reshape(depth, -1) for gain in gains], axis=1)

        one, two = by_pack(from_first), by_pack(from_last)
        total = jnp.where(first, one, two) + swap(jnp.where(first, two, one))
        pack = lax.axis_index("fsdp")
        summed = lax.dynamic_index_in_dim(total, pack, 0)
        for k in range(1, depth):
            sent = lax.dynamic_index_in_dim(total, pack ^ k, 0)
            summed = summed + lax.ppermute(sent, "fsdp", [(i, i ^ k) for i in range(depth)])
        return sum(hops(summed))

    def scattered(operand):
        return lax.psum_scatter(operand, "fsdp", scatter_dimension=0, tiled=False)

    def met_rows(rows_by):
        return met(rows_by) if aligned else rows_by

    def rows_fallback(rest):
        (rest,) = rest
        share = rest.shape[1] // chunks
        rest = rest.reshape(count, chunks, share, LANES).swapaxes(1, 2).reshape(-1, width)
        full = jnp.zeros((2 * count * rest.shape[0], width), low)
        at = (piece * 2 + core) * rest.shape[0]
        full = lax.dynamic_update_slice_in_dim(full, rest.astype(low), at, 0)
        return lax.psum(lax.psum_scatter(full, "fsdp", scatter_dimension=0, tiled=True), "ctx")

    def returned(pieces, layer):
        own = jnp.stack(pieces)
        return own, lax.ppermute(own, "section", [(1 - layer, layer)])

    def mlp_meet(grads, swapped):
        if aligned:
            return call(sum_kernel, [grads[0], swapped[0]], [(grads[0].shape, low)], 2)
        return meet(grads, swapped)

    down_whole = None if aligned else downs[1]
    parts, branch, both, whole = mlp_backward(cotangents, lift_last, down_form, down_whole, kept_mlp_last)
    mlp_grads = weight_grads(kept_mlp_last[0], both, kept_mlp_last[3], branch, aligned)
    last_parts, unused = rows_product("whole", kept_mlp_last[3], [whole], True, after=[both])
    (mlp_grads, last_parts), parts = beside((mlp_grads, last_parts), met(parts))
    swapped = [swap(v) for v in mlp_grads[1::2]]
    grad, sent, mlp_gain = add_back(parts, cotangent, middle_last, found_last[1], False)
    (total, *down_rows), pieces = beside(mlp_meet(mlp_grads, swapped), hops(sent))
    mlp_last = scattered(total)

    results = attention_backward(
        pieces, qkv_last, out_last, found_last, kept_attention_last, after=[mark(total)]
    )
    results, last_parts = beside(results, met(tie(last_parts, pieces[1])))
    parts, branch, grad_raw, head_gains = results
    last = dealt_middle.astype(f32)
    for value in last_parts:
        last = last + value.astype(f32)
    last = last.astype(low)
    attention_grads = weight_grads(kept_attention_last[0], grad_raw, kept_attention_last[4], branch)
    attention_grads, parts = beside(attention_grads, met(parts))
    swapped = swap(attention_grads[1]), swap(attention_grads[3])
    grad, sent, gain, *packed = add_back(
        parts, grad, hidden_last, found_last[0], True, (mlp_gain, *head_gains)
    )
    gains_last = (gain, mlp_gain, *head_gains)
    down_grad_last = None if aligned else rows_fallback(*down_rows)
    total, out_rows = meet(attention_grads, swapped)
    moved, pieces = beside(met_rows(out_rows), hops(sent))
    operand, mlp_last = beside(laid_out(total, moved, packed), mlp_last)
    attention_last = scattered(operand)

    near = [hop(mlp_last, k) for k in range(1, count - 1)]
    results = mlp_backward(
        pieces, lift_first, "whole", down_first, kept_mlp_first, after=[mark(operand, mlp_last)]
    )
    parts, branch, both, unused = results
    mlp_grads = weight_grads(kept_mlp_first[0], both, kept_mlp_first[3], branch, aligned)
    mlp_grads, parts = beside(mlp_grads, met(parts))
    out_grad_last = None if aligned else rows_fallback(out_rows)
    swapped = [swap(v) for v in mlp_grads[1::2]]
    grad, sent, mlp_gain = add_back(parts, grad, middle_first, found_first[1], False)
    (total, *down_rows), pieces = beside(mlp_meet(mlp_grads, swapped), hops(sent))
    total, attention_last = beside(total, attention_last)
    mlp_first = scattered(total)

    attention_last = hops(tie(attention_last, pieces[1]))
    results = attention_backward(
        pieces,
        qkv_first,
        out_first,
        found_first,
        kept_attention_first,
        True,
        after=[mark(total, attention_last[0])],
    )
    results, near, attention_last = lax.optimization_barrier((results, near, attention_last))
    parts, branch, grad_raw, head_gains, dealt_branch = results
    attention_grads = weight_grads(kept_attention_first[0], grad_raw, kept_attention_first[4], branch)
    attention_grads, parts = beside(attention_grads, met(parts))
    swapped = swap(attention_grads[1]), swap(attention_grads[3])
    unused, grad, gain, *packed = add_back(
        parts, dealt_branch, dealt_entering, found_first[0], True, (mlp_gain, *head_gains)
    )
    down_grad_first = None if aligned else rows_fallback(*down_rows)
    (total, out_rows), mlp_first = beside(meet(attention_grads, swapped), mlp_first)
    mlp_first = hops(mlp_first)
    moved = met_rows(out_rows)
    operand = laid_out(total, moved, packed)
    out_grad_first = None if aligned else rows_fallback(out_rows)
    gains_first = (gain, mlp_gain, *head_gains)
    attention_first = scattered(operand)
    point = mark(operand)
    sums = None if aligned else gains_reduced(gains_first, gains_last)
    mlp_last = [mlp_last, *near, hop(tie(mlp_last, point), count - 1)]
    mlp_last, attention_last = returned(mlp_last, 1), returned(attention_last, 1)
    attention_first = hops(tie(attention_first, mlp_first))
    mlp_first = returned(mlp_first, 0)
    own = jnp.where(first, grad, last)
    other = swap(jnp.where(first, last, grad))
    boundary = jnp.where(first, jnp.stack([own, other]), jnp.stack([other, own]))

    def settle(kernel, from_first, from_last, outputs, at_once=1, after=()):
        size = from_first[0].shape[1]

        def block_of(layer):
            def at(i, where):
                return jnp.where(where[1] == layer, i ^ (where[0] // at_once), 0), 0, 0

            return pl.BlockSpec((at_once, size, LANES), at)

        def body(where, *refs):
            kernel(where, *refs[:4], *refs[4 + len(after) :])

        return pl.pallas_call(
            body,
            grid_spec=pltpu.PrefetchScalarGridSpec(
                num_scalar_prefetch=1,
                grid=(count // at_once,),
                in_specs=[block_of(0), block_of(0), block_of(1), block_of(1)]
                + [pl.BlockSpec(memory_space=pl.ANY)] * len(after),
                out_specs=[
                    pl.BlockSpec(block, functools.partial(lambda at, i, where: at(i), at))
                    for _, block, at in outputs
                ],
            ),
            out_shape=[jax.ShapeDtypeStruct(shape, f32) for shape, _, _ in outputs],
            compiler_params=pltpu.CompilerParams(vmem_limit_bytes=VMEM_LIMIT),
            cost_estimate=pl.CostEstimate(
                flops=0, bytes_accessed=12 * count * size * LANES, transcendentals=0
            ),
        )(where, *from_first, *from_last, *after)

    def halves_of(where, blocks, body):
        @pl.when(where[1] == 0)
        def _():
            body(0, blocks[0])
            body(1, blocks[1])

        @pl.when(where[1] == 1)
        def _():
            body(1, blocks[2])
            body(0, blocks[3])

    def place_rows(block, at, half, out):
        share = out.shape[1]
        for j in range(chunks):
            out[half, :, span(j, LANES)] = block[0, at + j * share : at + (j + 1) * share, :].astype(f32)

    def mlp_settle_kernel(where, *refs):
        blocks, (gate, up) = refs[:4], refs[4:]

        def body(half, block):
            both = [block[0, span(j, part), :].astype(f32) for j in range(2 * hidden_half // LANES)]
            both = jnp.concatenate(both, axis=1)
            gate[:, span(half, hidden_half)] = both[:, :hidden_half]
            up[:, span(half, hidden_half)] = both[:, hidden_half:]

        halves_of(where, blocks, body)

    def strided_settle_kernel(where, *refs):
        blocks, (gate, up, down) = refs[:4], refs[4:]
        share = hidden_half // 2
        step = pl.program_id(0)

        def body(half, block):
            pair = []
            for side in range(2):
                at = (where[0] % 2) ^ side
                both = [block[at, span(j, part), :].astype(f32) for j in range(2 * hidden_half // LANES)]
                pair.append(jnp.concatenate(both, axis=1))
                for j in range(chunks):
                    rows_at = slice(lift_rows + j * down_share, lift_rows + (j + 1) * down_share)
                    down[2 * side + half, :, span(j, LANES)] = block[at, rows_at, :].astype(f32)
            for target, start in ((gate, 0), (up, hidden_half)):
                for i in range(2):
                    sides = [window(v[:, start : start + hidden_half], i * share, share) for v in pair]
                    to = (2 * half + i) * 2 * hidden_half + step * hidden_half
                    to = pl.ds(pl.multiple_of(to, 128), hidden_half)
                    target[:, to] = side_by_side(*sides, share)

        halves_of(where, blocks, body)

    def attention_settle_kernel(where, *refs):
        blocks, (query, key, value, *out) = refs[:4], refs[4:]
        if aligned:

            @pl.when(pl.program_id(0) == 0)
            def _():
                out[1][...] = jnp.zeros_like(out[1])

        def body(half, block):
            query[:, span(half, query_half)] = block[0, :part, :].astype(f32)
            both = block[0, part : 2 * part, :].astype(f32)
            key[:, span(half, key_half)] = both[:, :key_half]
            value[:, span(half, key_half)] = both[:, key_half:]
            if aligned:
                place_rows(block, 2 * part, half, out[0])
                if half == 0:
                    out[1][...] += block[0, 2 * part + chunks * out_share :, :].astype(f32)

        halves_of(where, blocks, body)

    def column_output(size):
        return ((part, 2 * count * size), (part, 2 * size), lambda i: (0, i))

    def row_output(size):
        return ((2, size, width), (2, size // count, width), lambda i: (0, i, 0))

    if aligned:
        whole_columns = (part, 2 * count * hidden_half)
        outputs = [(whole_columns, whole_columns, lambda i: (0, 0))] * 2
        outputs += [((2 * count, down_share, width), (count, down_share, width), lambda i: (i, 0, 0))]
        settled = settle(strided_settle_kernel, mlp_first, mlp_last, outputs, 2, [other])
    else:
        settled = settle(mlp_settle_kernel, mlp_first, mlp_last, [column_output(hidden_half)] * 2)
    (grad_gate, grad_up, *grad_down), attention_first = beside(settled, attention_first)
    outputs = [column_output(query_half)] + [column_output(key_half)] * 2
    if aligned:
        outputs += [row_output(query_half)]
        outputs += [((GAIN_ROWS, LANES), (GAIN_ROWS, LANES), lambda i: (0, 0))]
    grad_query, grad_key, grad_value, *grad_out = settle(
        attention_settle_kernel, returned(attention_first, 0), attention_last, outputs
    )
    if aligned:
        sums = grad_out[1]
        at = lax.axis_index("fsdp") * sizes[2]
        head_sums = [lax.dynamic_slice_in_dim(sums[2:3], at + k * HEAD_DIM, sizes[2], 1) for k in range(2)]
        split = [sums[0:1], sums[1:2], *head_sums]
    else:
        split, at = [], 0
        for size in sizes:
            split.append(sums[:, at : at + size])
            at += size

    if aligned:
        grad_out, grad_down = grad_out[0].reshape(-1, width), grad_down[0].reshape(-1, width)
    else:
        pair = []
        for one, two in ((out_grad_first, out_grad_last), (down_grad_first, down_grad_last)):
            own = jnp.where(first, one, two).astype(f32)
            pair.append(own + swap(jnp.where(first, two, one)).astype(f32))
        grad_out, grad_down = pair
    return (
        boundary[None, None],
        split[0],
        grad_query[None],
        grad_key[None],
        grad_value[None],
        split[2],
        split[3],
        grad_out[None],
        split[1],
        grad_gate[None],
        grad_up[None],
        grad_down[None],
    )


def solution(mesh):
    weight, gain, row = P("section", "fsdp", None), P("section", "fsdp"), P("fsdp", None, None)
    stream = P("section", "fsdp", None, "ctx", None)
    masters = (gain, weight, weight, weight, gain, gain, weight, gain, weight, weight, weight)
    return jax.shard_map(
        shards,
        mesh=mesh,
        in_specs=(stream, row, row) + masters,
        out_specs=(stream,) + masters,
        check_vma=False,
    )
```

```python
import functools

import jax
import jax.numpy as jnp
from jax import lax
from jax.experimental import pallas as pl
from jax.experimental.pallas import tpu as pltpu
from jax.sharding import PartitionSpec as P

HEAD_DIM = 128
GAIN_ROWS = 16
LANES = 256
VMEM_LIMIT = 56 * 1024 * 1024
VMEM_SLACK = 6 * 1024 * 1024
FLOPS_PER_US = 1.15e9
SCALE = HEAD_DIM ** (-0.5)
epsilon = 1e-06
rope_base = 1000000.0
low = jnp.bfloat16
f32 = jnp.float32


def swap(value):
    return lax.ppermute(value, "section", [(0, 1), (1, 0)])


def hop(value, step):
    count = lax.axis_size("ctx")
    return lax.ppermute(value, "ctx", [(i, i ^ step) for i in range(count)])


def hops(own):
    return [own] + [hop(own, k) for k in range(1, lax.axis_size("ctx"))]


def hops_split(own):
    if lax.axis_size("ctx") != 4:
        return hops(own)
    one, two = own[: own.shape[0] // 2], own[own.shape[0] // 2 :]
    one_near, two_near = hop(one, 1), hop(two, 2)
    near = jnp.concatenate([one_near, hop(two, 1)]), jnp.concatenate([hop(one, 2), two_near])
    return [own, *near, jnp.concatenate([hop(one_near, 2), hop(two_near, 1)])]


def met(parts):
    return [parts[0]] + [hop(parts[k], k) for k in range(1, len(parts))]


def beside(results, others):
    return lax.optimization_barrier((results, others))


def tie(value, other):
    return lax.optimization_barrier((value, other))[0]


def xored(pieces, index):
    for bit in range(len(pieces).bit_length() - 1):
        turned = ((index >> bit) & 1) == 1
        pieces = [jnp.where(turned, pieces[j ^ (1 << bit)], v) for j, v in enumerate(pieces)]
    return pieces


def dot(left, right):
    return jnp.dot(left, right, preferred_element_type=f32)


def dot_rows(left, right):
    return lax.dot_general(left, right, (((0,), (0,)), ((), ())), preferred_element_type=f32)


def dot_cols(left, right):
    return lax.dot_general(left, right, (((1,), (1,)), ((), ())), preferred_element_type=f32)


def rms_scale(values, gain):
    scale = lax.rsqrt(jnp.mean(values * values, axis=-1, keepdims=True) + epsilon)
    return values * scale * gain


def rms_back(values, gain, grad):
    scale = lax.rsqrt(jnp.mean(values * values, axis=-1, keepdims=True) + epsilon)
    unit = values * scale
    lifted = grad * gain
    grad_values = (lifted - unit * jnp.mean(lifted * unit, axis=-1, keepdims=True)) * scale
    return grad_values, jnp.sum(grad * unit, axis=0, keepdims=True)


def turn(values, cosine, sine):
    return values * cosine + pltpu.roll(values, HEAD_DIM // 2, 1) * sine


def turn_back(grad, cosine, sine):
    return grad * cosine + pltpu.roll(grad * sine, HEAD_DIM // 2, 1)


def chunk(j, size):
    return pl.ds(pl.multiple_of(j * size, size), size)


def span(j, size):
    return slice(j * size, (j + 1) * size)


def join(pieces, target):
    rows = pieces[0].shape[0]
    for i, piece in enumerate(pieces):
        target[span(i, rows), :] = piece[...]


def deal_out(parts, block, value):
    rows = parts[0].shape[0]
    for i, part in enumerate(parts):
        part[:, block] = value[span(i, rows)].astype(part.dtype)


def call(kernel, operands, outputs, took, scratch=(), scalars=(), after=(), limit=0):
    vmem = pl.BlockSpec(memory_space=pltpu.VMEM)
    smem = pl.BlockSpec(memory_space=pltpu.SMEM)
    anywhere = pl.BlockSpec(memory_space=pl.ANY)
    shapes = [jax.ShapeDtypeStruct(shape, dtype) for shape, dtype in outputs]
    moved = sum(v.size * v.dtype.itemsize for v in [*operands, *shapes])
    skipped, used = len(after), len(scalars)
    held = moved + sum(jnp.dtype(dtype).itemsize * shape[0] * shape[1] for shape, dtype in scratch)

    def body(*refs):
        kernel(*refs[skipped:])

    return pl.pallas_call(
        body,
        out_shape=shapes,
        in_specs=[anywhere] * skipped + [smem] * used + [vmem] * len(operands),
        out_specs=[vmem] * len(shapes),
        scratch_shapes=[pltpu.VMEM(shape, dtype) for shape, dtype in scratch],
        compiler_params=pltpu.CompilerParams(vmem_limit_bytes=limit or held + VMEM_SLACK),
        cost_estimate=pl.CostEstimate(
            flops=int(took * FLOPS_PER_US), bytes_accessed=moved, transcendentals=0
        ),
    )(*after, *scalars, *operands)


def mark_kernel(out):
    out[...] = jnp.zeros_like(out)


def mark(*values, took=20):
    return call(mark_kernel, [], [((8, 128), f32)], took, after=values)[0]


def window(values, at, size):
    base = at // 128 * 128
    block = values[:, base : base + LANES]
    return pltpu.roll(block, LANES - (at - base), 1) if at != base else block


def side_by_side(left, right, size):
    if size == LANES:
        return jnp.concatenate([left, right], axis=1)
    lane = lax.broadcasted_iota(jnp.int32, (left.shape[0], 128), 1)
    turned = pltpu.roll(right, size - 128, 1)
    middle = jnp.where(lane < size - 128, left[:, 128:], turned[:, :128])
    return jnp.concatenate([left[:, :128], middle, turned[:, 128:]], axis=1)


def add_kernel(count, rounded, sends_rows, *refs):
    parts, (residual, gain, total, normed) = refs[:count], refs[count:]
    value = residual[...].astype(f32)
    for part in parts:
        value = value + part[...].astype(f32)
    if rounded:
        value = value.astype(low).astype(f32)
    total[...] = value
    normed[...] = (value if sends_rows else rms_scale(value, gain[...])).astype(low)


def add_back_kernel(count, rounded, packs, *refs):
    parts, (upstream, middle, gain, *refs) = refs[:count], refs[count:]
    if packs:
        mlp_gains, query_gains, key_gains, *refs = refs
    total, sent, grad_gain, *packed = refs
    grad = parts[0][...].astype(f32)
    for part in parts[1:]:
        grad = grad + part[...].astype(f32)
    grad, gains = rms_back(middle[...].astype(f32), gain[...], grad)
    grad = upstream[...].astype(f32) + grad
    sent[...] = grad.astype(low)
    total[...] = grad.astype(low).astype(f32) if rounded else grad
    grad_gain[...] = gains
    if packs:
        (packed,) = packed
        packed[...] = jnp.zeros_like(packed)
        for z in range(packed.shape[0]):
            packed[z, 0:1, :] = gains[:, span(z, LANES)]
            packed[z, 1:2, :] = mlp_gains[:, span(z, LANES)]
            packed[z, 2:3, :HEAD_DIM] = query_gains[...]
            packed[z, 2:3, HEAD_DIM:] = key_gains[...]


def attention_forward_kernel(count, part, raw_rows, *refs):
    pieces, refs = refs[:count], refs[count:]
    if raw_rows:
        gain, chosen, *refs = refs
    own_weight, far_weight, cosine, sine, query_gain, key_gain, start, place, place_row, *refs = refs
    normed, raw, queries, keys, mixed, spread, *refs = refs
    values = refs[-1]
    tokens = normed.shape[0]
    rows = pieces[0].shape[0]
    depth = own_weight.shape[0]
    halves = keys.shape[1] // HEAD_DIM
    group = queries.shape[1] // keys.shape[1]
    step = (group + 2) * HEAD_DIM
    join(pieces, normed)
    if raw_rows:
        refs[0][...] = dot(chosen[:rows, :], normed[...]).astype(low)
        normed[...] = rms_scale(normed[...].astype(f32), gain[...]).astype(low)
    for half, weight in enumerate((own_weight, far_weight)):
        for j, at in enumerate((0, part + GAIN_ROWS)):
            total = None
            for z in range(depth):
                term = dot(normed[:, span(z, part)], weight[z, at : at + part, :])
                total = term if total is None else total + term
            raw[:, span(2 * half + j, LANES)] = total

    for half in range(halves):
        base = half * step
        at = base + group * HEAD_DIM
        own = span(half, HEAD_DIM)
        unit = rms_scale(raw[:, at : at + HEAD_DIM], key_gain[...])
        keys[:, own] = turn(unit, cosine[...], sine[...]).astype(low)
        values[:, own] = raw[:, at + HEAD_DIM : at + 2 * HEAD_DIM].astype(low)
        for g in range(group):
            unit = rms_scale(raw[:, base + g * HEAD_DIM : base + (g + 1) * HEAD_DIM], query_gain[...])
            unit = turn(unit, cosine[...], sine[...])
            queries[:, span(half * group + g, HEAD_DIM)] = unit.astype(low)

    @pl.loop(0, tokens // rows)
    def _(i):
        block = chunk(i, rows)
        visible = (place_row[...] >= start[block, :]) & (place_row[...] <= place[block, :])
        visible = jnp.concatenate([visible] * group, axis=0)
        for half in range(halves):
            own = span(half, HEAD_DIM)
            heads = range(half * group, (half + 1) * group)
            query = jnp.concatenate([queries[block, span(h, HEAD_DIM)] for h in heads], axis=0)
            scores = dot_cols(query, keys[:, own]) * SCALE
            scores = jnp.where(visible, scores, -1e30)
            top = jnp.max(scores, axis=-1, keepdims=True)
            raised = jnp.exp(scores - top)
            total = jnp.sum(raised, axis=-1, keepdims=True)
            probs = (raised * (1.0 / total)).astype(low)
            value = dot(probs, values[:, own]).astype(low)
            log_total = top + jnp.log(total)
            for g, head in enumerate(heads):
                mixed[block, span(head, HEAD_DIM)] = value[span(g, rows)]
                spread[block, head : head + 1] = log_total[span(g, rows)]


def pick_kernel(first_row, index, own, *out):
    for k, share in enumerate(out):
        share[...] = own[index[0] ^ k, first_row:, :]


def gather_shares(count, index, shares, whole):
    size = whole.shape[0] // 2
    share = size // count
    for k, value in enumerate(shares):
        to = k // count * size + (index[0] ^ (k % count)) * share
        to = pl.ds(pl.multiple_of(to, share), share)
        for j in range(whole.shape[1] // LANES):
            whole[to, span(j, LANES)] = value[span(j, share), :]


def gather_strided(index, own, far, whole):
    depth, core = own.shape[0], index[1]
    chunks = whole.shape[1] // LANES
    share = whole.shape[0] // depth
    half = share // 2
    at = own.shape[1] - chunks * half
    for z in range(depth):
        place = (z // (depth // 2) ^ core) * (depth // 2) + z % (depth // 2)
        for value, carried in ((own, core), (far, 1 - core)):
            to = pl.ds(pl.multiple_of(place * share + carried * half, 32), half)
            for j in range(chunks):
                whole[to, span(j, LANES)] = value[z, at + j * half : at + (j + 1) * half, :]


def gather_rows(form, count, index, given, whole):
    if form == "whole":
        whole[...] = given[0][...]
    elif form == "shares":
        gather_shares(count, index, given, whole)
    else:
        gather_strided(index, *given, whole)


def rows_kernel(count, form, dealt, index, left, *refs):
    if dealt:
        chosen, *refs = refs
    given, refs = refs[: -count - 1], refs[-count - 1 :]
    parts, whole = refs[:count], refs[count]
    gather_rows(form, count, index, given, whole)

    @pl.loop(0, whole.shape[1] // LANES)
    def _(j):
        block = chunk(j, LANES)
        value = dot(left[...], whole[:, block])
        deal_out(parts, block, dot(chosen[...], value.astype(low)) if dealt else value)


def lift_kernel(count, part, raw_rows, *refs):
    pieces, refs = refs[:count], refs[count:]
    if raw_rows:
        gain, chosen, *refs = refs
    own_weight, far_weight, normed, gate, lifted, product, *refs = refs
    half_size = product.shape[1] // 2
    depth = own_weight.shape[0]
    join(pieces, normed)
    if raw_rows:
        refs[0][...] = dot(chosen[: pieces[0].shape[0], :], normed[...]).astype(low)
        normed[...] = rms_scale(normed[...].astype(f32), gain[...]).astype(low)
    for half, weight in enumerate((own_weight, far_weight)):
        both = []
        for j in range(2 * half_size // LANES):
            total = None
            for z in range(depth):
                term = dot(normed[:, span(z, part)], weight[z, span(j, part), :])
                total = term if total is None else total + term
            both.append(total)
        both = jnp.concatenate(both, axis=1)
        one, two = both[:, :half_size], both[:, half_size:]
        at = span(half, half_size)
        gate[:, at] = one
        lifted[:, at] = two
        product[:, at] = (one * jax.nn.sigmoid(one) * two).astype(low)


def mlp_forward_kernel(count, part, form, index, *refs):
    pieces, refs = refs[:count], refs[count:]
    weights, refs = refs[:2], refs[2:]
    given, refs = (weights, refs) if form == "strided" else (refs[:1], refs[1:])
    kept, (*parts, whole) = refs[:4], refs[4:]
    lift_kernel(count, part, False, *pieces, *weights, *kept)
    rows_kernel(count, form, False, index, kept[3], *given, *parts, whole)


def mlp_backward_kernel(count, part, form, index, *refs):
    pieces, refs = refs[:count], refs[count:]
    own_weight, far_weight, gate, lifted, *refs = refs
    if form == "strided":
        given = [own_weight, far_weight]
    else:
        given, refs = refs[:1], refs[1:]
    parts, (branch, grad_both, down) = refs[:count], refs[count:]
    gather_rows(form, count, index, given, down)
    size = gate.shape[1] // 2
    depth = own_weight.shape[0]
    join(pieces, branch)
    for half in range(2):
        at = span(half, size)
        grad = dot_cols(branch[...], down[at, :])
        one, two = gate[:, at], lifted[:, at]
        sigmoid = jax.nn.sigmoid(one)
        grad_gate = grad * two * sigmoid * (1.0 + one * (1.0 - sigmoid))
        grad_both[:, span(2 * half, size)] = grad_gate.astype(low)
        grad_both[:, span(2 * half + 1, size)] = (grad * one * sigmoid).astype(low)
    for z in range(depth):
        total = None
        for half, weight in enumerate((own_weight, far_weight)):
            for j in range(2 * size // LANES):
                at = 2 * half * size + j * LANES
                term = dot_cols(grad_both[:, at : at + LANES], weight[z, span(j, part), :])
                total = term if total is None else total + term
        deal_out(parts, span(z, part), total)


def attention_backward_kernel(count, part, dealt, *refs):
    pieces, refs = refs[:count], refs[count:]
    if dealt:
        chosen, *refs = refs
    own_weight, far_weight, out, *refs = refs
    cosine, sine, query_gain, key_gain, start, place, place_row, *refs = refs
    raw, queries, keys, spread, *refs = refs
    parts, refs = refs[:count], refs[count:]
    branch, grad_raw, grad_query_gain, grad_key_gain, *refs = refs
    if dealt:
        dealt_branch, *refs = refs
    grad_mixed, values, grad_queries, grad_keys, grad_values = refs
    tokens, width = branch.shape
    rows = pieces[0].shape[0]
    depth = own_weight.shape[0]
    halves = keys.shape[1] // HEAD_DIM
    group = queries.shape[1] // keys.shape[1]
    step = (group + 2) * HEAD_DIM
    join(pieces, branch)
    if dealt:
        dealt_branch[...] = dot(chosen[:rows, :], branch[...]).astype(low)

    @pl.loop(0, grad_mixed.shape[1] // LANES)
    def _(j):
        block = chunk(j, LANES)
        grad_mixed[:, block] = dot_cols(branch[...], out[block, :]).astype(low)

    for half in range(halves):
        at = half * step + (group + 1) * HEAD_DIM
        values[:, span(half, HEAD_DIM)] = raw[:, at : at + HEAD_DIM].astype(low)
    grad_keys[...] = jnp.zeros_like(grad_keys)
    grad_values[...] = jnp.zeros_like(grad_values)

    @pl.loop(0, tokens // rows)
    def _(i):
        block = chunk(i, rows)
        visible = (place_row[...] >= start[block, :]) & (place_row[...] <= place[block, :])
        visible = jnp.concatenate([visible] * group, axis=0)
        for half in range(halves):
            own = span(half, HEAD_DIM)
            heads = range(half * group, (half + 1) * group)
            query = jnp.concatenate([queries[block, span(h, HEAD_DIM)] for h in heads], axis=0)
            grad = jnp.concatenate([grad_mixed[block, span(h, HEAD_DIM)] for h in heads], axis=0)
            log_total = jnp.concatenate([spread[block, h : h + 1] for h in heads], axis=0)
            scores = dot_cols(query, keys[:, own]) * SCALE
            scores = jnp.where(visible, scores, -1e30)
            probs = jnp.exp(scores - log_total)
            grad_probs = dot_cols(grad, values[:, own])
            weighted = jnp.sum(probs * grad_probs, axis=-1, keepdims=True)
            grad_scores = (probs * (grad_probs - weighted)).astype(low)
            grad_query = dot(grad_scores, keys[:, own]) * SCALE
            for g, head in enumerate(heads):
                grad_queries[block, span(head, HEAD_DIM)] = grad_query[span(g, rows)]
            grad_keys[:, own] += dot_rows(grad_scores, query) * SCALE
            grad_values[:, own] += dot_rows(probs.astype(low), grad)

    total_query = jnp.zeros((1, HEAD_DIM), f32)
    total_key = jnp.zeros((1, HEAD_DIM), f32)
    for half in range(halves):
        base = half * step
        own = span(half, HEAD_DIM)
        for g in range(group + 1):
            at = slice(base + g * HEAD_DIM, base + (g + 1) * HEAD_DIM)
            if g < group:
                grad, gain = grad_queries[:, span(half * group + g, HEAD_DIM)], query_gain[...]
            else:
                grad, gain = grad_keys[:, own], key_gain[...]
            grad = turn_back(grad, cosine[...], sine[...])
            grad, grad_gain = rms_back(raw[:, at], gain, grad)
            grad_raw[:, at] = grad.astype(low)
            if g < group:
                total_query += grad_gain
            else:
                total_key += grad_gain
        at = base + (group + 1) * HEAD_DIM
        grad_raw[:, at : at + HEAD_DIM] = grad_values[:, own].astype(low)
    grad_query_gain[...] = total_query
    grad_key_gain[...] = total_key
    for z in range(depth):
        total = None
        for half, weight in enumerate((own_weight, far_weight)):
            for j, at in enumerate((0, part + GAIN_ROWS)):
                grad = grad_raw[:, span(2 * half + j, LANES)]
                term = dot_cols(grad, weight[z, at : at + part, :])
                total = term if total is None else total + term
        if dealt:
            total = dot(chosen[...], total.astype(low))
        deal_out(parts, span(z, part), total)


def weight_grads_kernel(part, strided, index, left, grads, inner, branch, own, far, *refs):
    *rows_out, turned = refs
    depth = own.shape[0]
    chunks = grads.shape[1] // (2 * LANES)
    size = inner.shape[1] // 2
    for z in range(depth):
        turned[span(z, part), :] = left[:, span(z, part)].T
    for half, target in enumerate((own, far)):
        for j in range(chunks):
            total = dot(turned[...], grads[:, span(half * chunks + j, LANES)])
            for z in range(depth):
                target[z, span(j, part), :] = total[span(z, part)].astype(target.dtype)
    for half in range(2):
        rows = inner[:, span(half, size)].T
        for j in range(branch.shape[1] // LANES):
            total = dot(rows, branch[:, span(j, LANES)])
            if strided:
                share = size // (depth // 2)
                carried = share // 2
                at = slice(chunks * part + j * carried, chunks * part + (j + 1) * carried)
                for i in range(depth // 2):
                    z = (index[1] ^ half) * (depth // 2) + i
                    block = total[span(i, share)]
                    one, two = block[:carried], block[carried:]
                    own[z, at, :] = jnp.where(index[1] == 0, one, two)
                    far[z, at, :] = jnp.where(index[1] == 0, two, one).astype(far.dtype)
            else:
                target = rows_out[half]
                count = target.shape[0]
                share = size // count
                for k in range(count):
                    target[k, span(j, share), :] = total[span(k, share)].astype(target.dtype)


def sum_kernel(own, recv, total):
    total[...] = (own[...] + recv[...].astype(f32)).astype(low)


def meet_kernel(index, own, recv, own_rows, recv_rows, total, *rows):
    total[...] = (own[...] + recv[...].astype(f32)).astype(low)
    for k, row in enumerate(rows):
        at = index[0] ^ k
        row[...] = (own_rows[at] + recv_rows[at].astype(f32)).astype(low)


def layout_kernel(index, total, gains, far_gains, *refs):
    *rows, out = refs
    at = total.shape[1]
    end = at + rows[0].shape[0]
    out[:, :at, :] = total[...]
    for k, row in enumerate(rows):
        out[index[0] ^ k, at:end, :] = row[...]
    out[:, end:, :] = (gains[...] + far_gains[...]).astype(low)


def shards(
    stream_in,
    lengths,
    dealing,
    attention_gain,
    query_weight,
    key_weight,
    value_weight,
    query_gain,
    key_gain,
    out_weight,
    mlp_gain,
    gate_weight,
    up_weight,
    down_weight,
):
    core = lax.axis_index("section")
    piece = lax.axis_index("ctx")
    count = lax.axis_size("ctx")
    depth = lax.axis_size("fsdp")
    rows, width = stream_in.shape[3], stream_in.shape[4]
    tokens = rows * count
    first = core == 0
    query_half = query_weight.shape[2] // (2 * count)
    key_half = key_weight.shape[2] // (2 * count)
    hidden_half = gate_weight.shape[2] // (2 * count)
    part = query_weight.shape[1]
    aligned = depth == count == 4
    out_share, down_share = query_half // count, hidden_half // count
    index = jnp.stack([piece, core]).astype(jnp.int32)
    chunks = width // LANES
    qkv_rows = 2 * part + GAIN_ROWS
    lift_rows = 2 * hidden_half // LANES * part

    own = lax.dynamic_index_in_dim(stream_in[0, 0], core, 0, keepdims=False)
    other = swap(lax.dynamic_index_in_dim(stream_in[0, 0], 1 - core, 0, keepdims=False))
    entering = jnp.where(first, own, other)
    cotangent = jnp.where(first, other, own)

    where = jnp.stack([piece, core]).astype(jnp.int32)

    def cut(kernel, weights, constants, size, after=()):
        def half(i, where):
            return jnp.where(i == 0, 1 - where[1], where[1])

        def columns(i, where):
            return 0, 0, where[0] * 2 + half(i, where)

        def shares(i, where):
            return 0, half(i, where) * count + where[0], 0

        def even(i, where):
            return 0, 0, half(i, where) * 2

        def odd(i, where):
            return 0, 0, half(i, where) * 2 + 1

        def carried(i, where):
            return 0, where[0] * 2 + half(i, where), 0

        maps = {"columns": columns, "shares": shares, "even": even, "odd": odd, "carried": carried}
        in_specs = [
            pl.BlockSpec((1, height, breadth), maps[which]) for _, height, breadth, which in weights
        ]
        in_specs += [pl.BlockSpec(v.shape, lambda i, where: (0, 0)) for v in constants]
        in_specs += [pl.BlockSpec(memory_space=pl.ANY)] * len(after)

        def body(where, *refs):
            kernel(where, *refs[: len(refs) - 1 - len(after)], refs[-1])

        return pl.pallas_call(
            body,
            grid_spec=pltpu.PrefetchScalarGridSpec(
                num_scalar_prefetch=1,
                grid=(2,),
                in_specs=in_specs,
                out_specs=pl.BlockSpec((1, size, LANES), lambda i, where: (i, 0, 0)),
            ),
            out_shape=jax.ShapeDtypeStruct((2, size, LANES), low),
            compiler_params=pltpu.CompilerParams(vmem_limit_bytes=VMEM_LIMIT),
            cost_estimate=pl.CostEstimate(
                flops=int(3 * FLOPS_PER_US), bytes_accessed=12 * size * LANES, transcendentals=0
            ),
        )(where, *[weight for weight, *_ in weights], *constants, *after)

    def place_shares(weight, out, at):
        share = weight.shape[1]
        for j in range(chunks):
            out[0, at + j * share : at + (j + 1) * share, :] = weight[0, :, span(j, LANES)].astype(low)

    def qkv_cut_kernel(where, query, key, value, *refs):
        *rest, gains, out = refs
        out[0, :part, :] = query[0].astype(low)
        out[0, part : part + GAIN_ROWS, :] = gains[...]
        at = slice(part + GAIN_ROWS, qkv_rows)
        out[0, at, :key_half] = key[0].astype(low)
        out[0, at, key_half:] = value[0].astype(low)
        if aligned:
            place_shares(rest[0], out, qkv_rows)

    def mlp_cut_kernel(where, gate, up, out):
        both = jnp.concatenate([gate[0].astype(low), up[0].astype(low)], axis=1)
        for j in range(2 * hidden_half // LANES):
            out[0, span(j, part), :] = both[:, span(j, LANES)]

    def strided_cut_kernel(where, gate, gate_next, up, up_next, down, out):
        share = hidden_half // 2

        for c in range(count):

            @pl.when(where[0] == c)
            def _(c=c):
                sides = [window(v[0], c * share, share) for v in (gate, gate_next, up, up_next)]
                both = [side_by_side(*sides[:2], share), side_by_side(*sides[2:], share)]
                both = jnp.concatenate(both, axis=1).astype(low)
                for j in range(2 * hidden_half // LANES):
                    out[0, span(j, part), :] = both[:, span(j, LANES)]

        place_shares(down, out, lift_rows)

    gains = (attention_gain[0], mlp_gain[0], query_gain[0], key_gain[0])
    sizes = [gain.shape[0] for gain in gains]
    gain_block = jnp.concatenate(gains).astype(low)
    gain_block = jnp.pad(gain_block, (0, GAIN_ROWS * LANES - gain_block.shape[0]))
    gain_block = gain_block.reshape(GAIN_ROWS, LANES)

    def by_layer(cuts):
        mine, other = cuts[1], swap(cuts[0])
        return jnp.where(first, mine, other), jnp.where(first, other, mine)

    weights = [(query_weight, part, query_half, "columns"), (key_weight, part, key_half, "columns")]
    weights += [(value_weight, part, key_half, "columns")]
    weights += [(out_weight, out_share, width, "shares")] if aligned else []
    size = qkv_rows + (chunks * out_share if aligned else 0)
    cuts = cut(qkv_cut_kernel, weights, [gain_block], size)
    attention_blocks = by_layer(cuts)
    line = jnp.arange(size, dtype=jnp.int32)[:, None]
    gain_rows = (line >= part) & (line < part + GAIN_ROWS)
    attention_blocks = jnp.where(gain_rows, cuts[1], attention_blocks[0]), attention_blocks[1]
    point = mark(attention_blocks[0])
    if aligned:
        block = 2 * hidden_half
        weights = [(gate_weight, part, block, "even"), (gate_weight, part, block, "odd")]
        weights += [(up_weight, part, block, "even"), (up_weight, part, block, "odd")]
        weights += [(down_weight, down_share, width, "carried")]
        size = lift_rows + chunks * down_share
        mlp_blocks = by_layer(cut(strided_cut_kernel, weights, [], size, [point]))
    else:
        weights = [(gate_weight, part, hidden_half, "columns"), (up_weight, part, hidden_half, "columns")]
        mlp_blocks = by_layer(cut(mlp_cut_kernel, weights, [], lift_rows))

    def gathered(block):
        return lax.all_gather(block, "fsdp", axis=0, tiled=False)

    def whole_rows(weight, size):
        full = lax.all_gather(weight[0].astype(low), "fsdp", axis=0, tiled=True)
        full = lax.dynamic_slice_in_dim(full, piece * 2 * size, 2 * size, 0)
        other = swap(full)
        layers = jnp.where(first, full, other), jnp.where(first, other, full)
        own = [lax.dynamic_slice_in_dim(v, core * size, size, 0) for v in layers]
        far = [lax.dynamic_slice_in_dim(v, (1 - core) * size, size, 0) for v in layers]
        return [jnp.concatenate(pair, axis=0) for pair in zip(own, far)]

    def picked_rows(own, first_row):
        size = own.shape[1] - first_row
        kernel = functools.partial(pick_kernel, first_row)
        return call(kernel, [own], [((size, LANES), low)] * count, 1, scalars=[index])

    def split_gains(own):
        found, at = [], 0
        flat = own[:, part : part + GAIN_ROWS].reshape(depth, -1)
        for size in sizes:
            found.append(flat[:, at : at + size].reshape(1, -1).astype(f32))
            at += size
        return found

    lens = lax.dynamic_index_in_dim(lengths[0], core, 0, keepdims=False)
    slots = lax.dynamic_index_in_dim(dealing[0], core, 0, keepdims=False)
    order = jnp.arange(tokens, dtype=jnp.int32)
    natural = ((order // rows) ^ piece) * rows + order % rows
    bounds = jnp.cumsum(lens)
    passed = (bounds[None, :] <= natural[:, None]).astype(jnp.int32)
    start = jnp.sum(passed * lens[None, :], axis=1)
    position = natural - start
    rates = jnp.power(rope_base, jnp.arange(HEAD_DIM // 2, dtype=f32) * (-2.0 / HEAD_DIM))
    phase = position.astype(f32)[:, None] * rates
    cosine, sine = jnp.cos(phase), jnp.sin(phase)
    cosine = jnp.concatenate([cosine, cosine], axis=-1)
    sine = jnp.concatenate([-sine, sine], axis=-1)
    places = [start[:, None], natural[:, None], natural[None, :]]

    wanted = slots.reshape(count, rows)
    wanted = jnp.concatenate(xored([wanted[j] for j in range(count)], piece))
    wanted = ((wanted // rows) ^ piece) * rows + wanted % rows
    chosen = (wanted[:, None] == order[None, :]).astype(low)

    wide, half_wide = (rows, width), (tokens, width)
    heads_wide, hidden_wide = 2 * query_half, 2 * hidden_half

    def add(parts, residual, gain, rounded, sends_rows=False, after=()):
        kernel = functools.partial(add_kernel, count, rounded, sends_rows)
        outputs = [(wide, f32), (wide, low)]
        return call(kernel, [*parts, residual, gain], outputs, 2, after=after)

    def add_back(parts, upstream, middle, gain, rounded, gains=(), after=()):
        packs = aligned and len(gains) > 0
        kernel = functools.partial(add_back_kernel, count, rounded, packs)
        outputs = [(wide, f32), (wide, low), ((1, width), f32)]
        outputs += [((depth, GAIN_ROWS, LANES), f32)] if packs else []
        operands = [*parts, upstream, middle, gain] + (list(gains) if packs else [])
        return call(kernel, operands, outputs, 2, after=after)

    def attention_forward(pieces, weights, found, raw_rows, after=()):
        kernel = functools.partial(attention_forward_kernel, count, part, raw_rows)
        outputs = [(half_wide, low), ((tokens, 2 * (query_half + 2 * key_half)), f32)]
        outputs += [((tokens, heads_wide), low), ((tokens, 2 * key_half), low)]
        outputs += [((tokens, heads_wide), low), ((tokens, heads_wide // HEAD_DIM), f32)]
        operands = [*pieces] + ([found[0], chosen] if raw_rows else [])
        outputs += [(wide, low)] if raw_rows else []
        operands += [*weights, cosine, sine, found[2], found[3], *places]
        return call(kernel, operands, outputs, 12, [((tokens, 2 * key_half), low)], after=after)

    def rows_product(form, left, given, dealt=False, after=()):
        kernel = functools.partial(rows_kernel, count, form, dealt)
        outputs = [(wide, low)] * count + [((left.shape[1], width), low)]
        operands = [left] + ([chosen] if dealt else []) + [*given]
        *parts, whole = call(kernel, operands, outputs, 8, scalars=[index], after=after)
        return parts, whole

    def lift_forward(pieces, weights, gain=None, after=()):
        kernel = functools.partial(lift_kernel, count, part, gain is not None)
        outputs = [(half_wide, low)] + [((tokens, hidden_wide), f32)] * 2
        outputs += [((tokens, hidden_wide), low)]
        operands = [*pieces]
        if gain is not None:
            operands += [gain, chosen]
            outputs += [(wide, low)]
        return call(kernel, [*operands, *weights], outputs, 0.6, after=after)

    def mlp_forward(pieces, weights, form, down):
        kernel = functools.partial(mlp_forward_kernel, count, part, form)
        outputs = [(half_wide, low)] + [((tokens, hidden_wide), f32)] * 2
        outputs += [((tokens, hidden_wide), low)] + [(wide, low)] * count
        outputs += [((hidden_wide, width), low)]
        operands = [*pieces, *weights] + ([] if form == "strided" else [down])
        *results, whole = call(kernel, operands, outputs, 2.4, scalars=[index])
        return results[:4], results[4:], whole

    def mlp_backward(pieces, weights, form, down, kept, after=()):
        kernel = functools.partial(mlp_backward_kernel, count, part, form)
        outputs = [(wide, low)] * count + [(half_wide, low), ((tokens, 2 * hidden_wide), low)]
        outputs += [((hidden_wide, width), low)]
        operands = [*pieces, *weights, kept[1], kept[2]] + ([] if form == "strided" else [down])
        results = call(kernel, operands, outputs, 3.0, scalars=[index], after=after)
        parts, (branch, both, whole) = results[:count], results[count:]
        return parts, branch, both, whole

    def attention_backward(pieces, weights, out, found, kept, dealt=False, after=()):
        kernel = functools.partial(attention_backward_kernel, count, part, dealt)
        normed, raw, queries, keys, mixed, spread = kept
        outputs = [(wide, low)] * count + [(half_wide, low), (raw.shape, low)]
        outputs += [((1, HEAD_DIM), f32)] * 2
        outputs += [(wide, low)] if dealt else []
        scratch = [(queries.shape, low), (keys.shape, low), (queries.shape, f32)]
        scratch += [(keys.shape, f32)] * 2
        operands = [*pieces] + ([chosen] if dealt else [])
        operands += [*weights, out, cosine, sine, found[2], found[3], *places]
        operands += [raw, queries, keys, spread]
        results = call(
            kernel, operands, outputs, 18, scratch, after=after
        )
        parts, (branch, grad_raw, query, key, *rest) = results[:count], results[count:]
        return (parts, branch, grad_raw, (query, key), *rest)

    def weight_grads(left, grads, inner, branch, strided=False, after=()):
        kernel = functools.partial(weight_grads_kernel, part, strided)
        size = grads.shape[1] // (2 * LANES) * part
        row_shape = (count, inner.shape[1] // (2 * count) * chunks, LANES)
        if strided:
            size += row_shape[1]
        outputs = [((depth, size, LANES), f32), ((depth, size, LANES), low)]
        outputs += [] if strided else [(row_shape, f32), (row_shape, low)]
        operands = [left, grads, inner, branch]
        scratch = [((width, tokens), low)]
        return call(kernel, operands, outputs, 3.0, scratch, scalars=[index], after=after)

    if not aligned:
        outs, downs = whole_rows(out_weight, query_half), whole_rows(down_weight, hidden_half)

    def arrived(value, after):
        own = tie(value, after)
        return [own, swap(own)]

    def moving_rows(weights, first_row, whole):
        return met(picked_rows(weights[0], first_row)) if aligned else [whole]

    def with_far(shares):
        return [*shares, *map(swap, shares)] if aligned else shares

    out_form, down_form = ("shares", "strided") if aligned else ("whole", "whole")
    pieces = hops(tie(entering, point))
    cotangents = hops(tie(cotangent, point))
    early = pieces, cotangents, mlp_blocks, attention_blocks[1], chosen, cosine, sine, places
    if aligned:
        pack = lax.axis_index("fsdp")
        out_rows = tie(attention_blocks[0][qkv_rows:], point)
        out_rows = [out_rows] + [
            lax.ppermute(out_rows, "fsdp", [(i, i ^ k) for i in range(depth)]) for k in range(1, depth)
        ]
        out_rows = xored(out_rows, piece ^ pack)
        early = *early, out_rows
        shares = met(out_rows)
    else:
        shares = [outs[0]]
    qkv_first = arrived(gathered(attention_blocks[0][:qkv_rows]), early)
    found_own, found_far = split_gains(qkv_first[0]), split_gains(qkv_first[1])
    found_first = [jnp.where(first, own, far) for own, far in zip(found_own, found_far)]
    found_last = [jnp.where(first, far, own) for own, far in zip(found_own, found_far)]
    kept_attention_first = attention_forward(pieces, qkv_first, found_first, True)
    kept_attention_first, shares = beside(kept_attention_first, shares)
    *kept_attention_first, dealt_entering = kept_attention_first
    parts, out_first = rows_product(out_form, kept_attention_first[4], with_far(shares))
    middle_first, normed = add(met(parts), entering, found_first[1], False)
    pieces = hops(normed)
    lift_first = arrived(gathered(mlp_blocks[0]), pieces)
    kept_mlp_first, parts, down_first = mlp_forward(
        pieces, lift_first, down_form, None if aligned else downs[0]
    )

    hidden_last, normed = add(met(parts), middle_first, found_last[0], True)
    pieces = hops(normed)
    qkv_last = arrived(gathered(attention_blocks[1]), pieces)
    shares = moving_rows(qkv_last, qkv_rows, None if aligned else outs[1])
    kept_attention_last = attention_forward(pieces, qkv_last, found_last, False)
    kept_attention_last, shares = beside(kept_attention_last, shares)
    parts, out_last = rows_product(out_form, kept_attention_last[4], with_far(shares))
    middle_last, sent = add(met(parts), hidden_last, found_last[1], False, True)
    pieces = hops(sent)
    lift_last = arrived(gathered(mlp_blocks[1]), pieces)
    *kept_mlp_last, dealt_middle = lift_forward(pieces, lift_last, found_last[1])

    def meet(grads, swapped):
        own, far, own_rows, far_rows = grads
        if not aligned:
            total = (own + swapped[0].astype(f32)).astype(low)
            return total, [own_rows + swapped[1].astype(f32)]
        outputs = [(own.shape, low)] + [(own_rows.shape[1:], low)] * count
        operands = [own, swapped[0], own_rows, swapped[1]]
        total, *rows_by = call(meet_kernel, operands, outputs, 4, scalars=[index])
        return total, rows_by

    def laid_out(total, rows_by, packed):
        if not aligned:
            return total
        size = total.shape[1] + rows_by[0].shape[0] + GAIN_ROWS
        outputs = [((depth, size, LANES), low)]
        operands = [total, packed[0], swap(packed[0]), *rows_by]
        return call(layout_kernel, operands, outputs, 3, scalars=[index])[0]

    def gains_reduced(from_first, from_last):
        def by_pack(gains):
            return jnp.concatenate([gain.reshape(depth, -1) for gain in gains], axis=1)

        one, two = by_pack(from_first), by_pack(from_last)
        total = jnp.where(first, one, two) + swap(jnp.where(first, two, one))
        pack = lax.axis_index("fsdp")
        summed = lax.dynamic_index_in_dim(total, pack, 0)
        for k in range(1, depth):
            sent = lax.dynamic_index_in_dim(total, pack ^ k, 0)
            summed = summed + lax.ppermute(sent, "fsdp", [(i, i ^ k) for i in range(depth)])
        return sum(hops(summed))

    def scattered(operand):
        return lax.psum_scatter(operand, "fsdp", scatter_dimension=0, tiled=False)

    def met_rows(rows_by):
        return met(rows_by) if aligned else rows_by

    def rows_fallback(rest):
        (rest,) = rest
        share = rest.shape[1] // chunks
        rest = rest.reshape(count, chunks, share, LANES).swapaxes(1, 2).reshape(-1, width)
        full = jnp.zeros((2 * count * rest.shape[0], width), low)
        at = (piece * 2 + core) * rest.shape[0]
        full = lax.dynamic_update_slice_in_dim(full, rest.astype(low), at, 0)
        return lax.psum(lax.psum_scatter(full, "fsdp", scatter_dimension=0, tiled=True), "ctx")

    def returned(pieces, layer):
        own = jnp.stack(pieces)
        return own, lax.ppermute(own, "section", [(1 - layer, layer)])

    def mlp_meet(grads, swapped):
        if aligned:
            return call(sum_kernel, [grads[0], swapped[0]], [(grads[0].shape, low)], 2)
        return meet(grads, swapped)

    down_whole = None if aligned else downs[1]
    parts, branch, both, whole = mlp_backward(cotangents, lift_last, down_form, down_whole, kept_mlp_last)
    mlp_grads = weight_grads(kept_mlp_last[0], both, kept_mlp_last[3], branch, aligned)
    last_parts, unused = rows_product("whole", kept_mlp_last[3], [whole], True, after=[both])
    (mlp_grads, last_parts), parts = beside((mlp_grads, last_parts), met(parts))
    swapped = [swap(v) for v in mlp_grads[1::2]]
    grad, sent, mlp_gain = add_back(parts, cotangent, middle_last, found_last[1], False)
    (total, *down_rows), pieces = beside(mlp_meet(mlp_grads, swapped), hops(sent))
    mlp_last = scattered(total)

    results = attention_backward(
        pieces, qkv_last, out_last, found_last, kept_attention_last, after=[mark(total)]
    )
    results, last_parts = beside(results, met(tie(last_parts, pieces[1])))
    parts, branch, grad_raw, head_gains = results
    last = dealt_middle.astype(f32)
    for value in last_parts:
        last = last + value.astype(f32)
    last = last.astype(low)
    attention_grads = weight_grads(kept_attention_last[0], grad_raw, kept_attention_last[4], branch)
    attention_grads, parts = beside(attention_grads, met(parts))
    swapped = swap(attention_grads[1]), swap(attention_grads[3])
    grad, sent, gain, *packed = add_back(
        parts, grad, hidden_last, found_last[0], True, (mlp_gain, *head_gains)
    )
    gains_last = (gain, mlp_gain, *head_gains)
    down_grad_last = None if aligned else rows_fallback(*down_rows)
    total, out_rows = meet(attention_grads, swapped)
    moved, pieces = beside(met_rows(out_rows), hops(sent))
    operand, mlp_last = beside(laid_out(total, moved, packed), mlp_last)
    attention_last = scattered(operand)

    near = [hop(mlp_last, k) for k in range(1, count - 1)]
    results = mlp_backward(
        pieces, lift_first, "whole", down_first, kept_mlp_first, after=[mark(operand, mlp_last)]
    )
    parts, branch, both, unused = results
    mlp_grads = weight_grads(kept_mlp_first[0], both, kept_mlp_first[3], branch, aligned)
    mlp_grads, parts = beside(mlp_grads, met(parts))
    out_grad_last = None if aligned else rows_fallback(out_rows)
    swapped = [swap(v) for v in mlp_grads[1::2]]
    grad, sent, mlp_gain = add_back(parts, grad, middle_first, found_first[1], False)
    (total, *down_rows), pieces = beside(mlp_meet(mlp_grads, swapped), hops(sent))
    total, attention_last = beside(total, attention_last)
    mlp_first = scattered(total)

    attention_last = tie(attention_last, pieces[1])
    near_last = [hop(attention_last, k) for k in range(1, count - 1)]
    results = attention_backward(
        pieces,
        qkv_first,
        out_first,
        found_first,
        kept_attention_first,
        True,
        after=[mark(total, attention_last)],
    )
    results, near, near_last = lax.optimization_barrier((results, near, near_last))
    parts, branch, grad_raw, head_gains, dealt_branch = results
    grads = weight_grads(kept_attention_first[0], grad_raw, kept_attention_first[4], branch)
    swapped = swap(grads[1]), swap(grads[3])
    held, parts = beside((grads[0], grads[2]), met(parts))
    unused, grad, gain, *packed = add_back(
        parts, dealt_branch, dealt_entering, found_first[0], True, (mlp_gain, *head_gains)
    )
    down_grad_first = None if aligned else rows_fallback(*down_rows)
    total, out_rows = meet((held[0], grads[1], held[1], grads[3]), swapped)
    moved, mlp_first = beside(met_rows(out_rows), mlp_first)
    operand = laid_out(total, moved, packed)
    out_grad_first = None if aligned else rows_fallback(out_rows)
    gains_first = (gain, mlp_gain, *head_gains)
    attention_first = scattered(operand)
    point = mark(operand)
    sums = None if aligned else gains_reduced(gains_first, gains_last)
    mlp_last = [mlp_last, *near, hop(tie(mlp_last, parts), count - 1)]
    attention_last = [attention_last, *near_last, hop(tie(attention_last, parts), count - 1)]
    mlp_first = hops(tie(mlp_first, point))
    mlp_last, attention_last = returned(mlp_last, 1), returned(attention_last, 1)
    attention_first = hops(tie(attention_first, mlp_first))
    mlp_first = returned(mlp_first, 0)
    own = jnp.where(first, grad, last)
    other = swap(jnp.where(first, last, grad))
    boundary = jnp.where(first, jnp.stack([own, other]), jnp.stack([other, own]))

    def settle(kernel, from_first, from_last, outputs, at_once=1, after=()):
        size = from_first[0].shape[1]

        def block_of(layer):
            def at(i, where):
                return jnp.where(where[1] == layer, i ^ (where[0] // at_once), 0), 0, 0

            return pl.BlockSpec((at_once, size, LANES), at)

        def body(where, *refs):
            kernel(where, *refs[:4], *refs[4 + len(after) :])

        return pl.pallas_call(
            body,
            grid_spec=pltpu.PrefetchScalarGridSpec(
                num_scalar_prefetch=1,
                grid=(count // at_once,),
                in_specs=[block_of(0), block_of(0), block_of(1), block_of(1)]
                + [pl.BlockSpec(memory_space=pl.ANY)] * len(after),
                out_specs=[
                    pl.BlockSpec(block, functools.partial(lambda at, i, where: at(i), at))
                    for _, block, at in outputs
                ],
            ),
            out_shape=[jax.ShapeDtypeStruct(shape, f32) for shape, _, _ in outputs],
            compiler_params=pltpu.CompilerParams(vmem_limit_bytes=VMEM_LIMIT),
            cost_estimate=pl.CostEstimate(
                flops=0, bytes_accessed=12 * count * size * LANES, transcendentals=0
            ),
        )(where, *from_first, *from_last, *after)

    def halves_of(where, blocks, body):
        @pl.when(where[1] == 0)
        def _():
            body(0, blocks[0])
            body(1, blocks[1])

        @pl.when(where[1] == 1)
        def _():
            body(1, blocks[2])
            body(0, blocks[3])

    def place_rows(block, at, half, out):
        share = out.shape[1]
        for j in range(chunks):
            out[half, :, span(j, LANES)] = block[0, at + j * share : at + (j + 1) * share, :].astype(f32)

    def mlp_settle_kernel(where, *refs):
        blocks, (gate, up) = refs[:4], refs[4:]

        def body(half, block):
            both = [block[0, span(j, part), :].astype(f32) for j in range(2 * hidden_half // LANES)]
            both = jnp.concatenate(both, axis=1)
            gate[:, span(half, hidden_half)] = both[:, :hidden_half]
            up[:, span(half, hidden_half)] = both[:, hidden_half:]

        halves_of(where, blocks, body)

    def strided_settle_kernel(where, *refs):
        blocks, (gate, up, down) = refs[:4], refs[4:]
        share = hidden_half // 2
        step = pl.program_id(0)

        def body(half, block):
            pair = []
            for side in range(2):
                at = (where[0] % 2) ^ side
                both = [block[at, span(j, part), :].astype(f32) for j in range(2 * hidden_half // LANES)]
                pair.append(jnp.concatenate(both, axis=1))
                for j in range(chunks):
                    rows_at = slice(lift_rows + j * down_share, lift_rows + (j + 1) * down_share)
                    down[2 * side + half, :, span(j, LANES)] = block[at, rows_at, :].astype(f32)
            for target, start in ((gate, 0), (up, hidden_half)):
                for i in range(2):
                    sides = [window(v[:, start : start + hidden_half], i * share, share) for v in pair]
                    to = (2 * half + i) * 2 * hidden_half + step * hidden_half
                    to = pl.ds(pl.multiple_of(to, 128), hidden_half)
                    target[:, to] = side_by_side(*sides, share)

        halves_of(where, blocks, body)

    def attention_settle_kernel(where, *refs):
        blocks, (query, key, value, *out) = refs[:4], refs[4:]
        if aligned:

            @pl.when(pl.program_id(0) == 0)
            def _():
                out[1][...] = jnp.zeros_like(out[1])

        def body(half, block):
            query[:, span(half, query_half)] = block[0, :part, :].astype(f32)
            both = block[0, part : 2 * part, :].astype(f32)
            key[:, span(half, key_half)] = both[:, :key_half]
            value[:, span(half, key_half)] = both[:, key_half:]
            if aligned:
                place_rows(block, 2 * part, half, out[0])
                if half == 0:
                    out[1][...] += block[0, 2 * part + chunks * out_share :, :].astype(f32)

        halves_of(where, blocks, body)

    def column_output(size):
        return ((part, 2 * count * size), (part, 2 * size), lambda i: (0, i))

    def row_output(size):
        return ((2, size, width), (2, size // count, width), lambda i: (0, i, 0))

    if aligned:
        whole_columns = (part, 2 * count * hidden_half)
        outputs = [(whole_columns, whole_columns, lambda i: (0, 0))] * 2
        outputs += [((2 * count, down_share, width), (count, down_share, width), lambda i: (i, 0, 0))]
        settled = settle(strided_settle_kernel, mlp_first, mlp_last, outputs, 2, [other])
    else:
        settled = settle(mlp_settle_kernel, mlp_first, mlp_last, [column_output(hidden_half)] * 2)
    (grad_gate, grad_up, *grad_down), attention_first = beside(settled, attention_first)
    outputs = [column_output(query_half)] + [column_output(key_half)] * 2
    if aligned:
        outputs += [row_output(query_half)]
        outputs += [((GAIN_ROWS, LANES), (GAIN_ROWS, LANES), lambda i: (0, 0))]
    grad_query, grad_key, grad_value, *grad_out = settle(
        attention_settle_kernel, returned(attention_first, 0), attention_last, outputs
    )
    if aligned:
        sums = grad_out[1]
        at = lax.axis_index("fsdp") * sizes[2]
        head_sums = [lax.dynamic_slice_in_dim(sums[2:3], at + k * HEAD_DIM, sizes[2], 1) for k in range(2)]
        split = [sums[0:1], sums[1:2], *head_sums]
    else:
        split, at = [], 0
        for size in sizes:
            split.append(sums[:, at : at + size])
            at += size

    if aligned:
        grad_out, grad_down = grad_out[0].reshape(-1, width), grad_down[0].reshape(-1, width)
    else:
        pair = []
        for one, two in ((out_grad_first, out_grad_last), (down_grad_first, down_grad_last)):
            own = jnp.where(first, one, two).astype(f32)
            pair.append(own + swap(jnp.where(first, two, one)).astype(f32))
        grad_out, grad_down = pair
    return (
        boundary[None, None],
        split[0],
        grad_query[None],
        grad_key[None],
        grad_value[None],
        split[2],
        split[3],
        grad_out[None],
        split[1],
        grad_gate[None],
        grad_up[None],
        grad_down[None],
    )


def solution(mesh):
    weight, gain, row = P("section", "fsdp", None), P("section", "fsdp"), P("fsdp", None, None)
    stream = P("section", "fsdp", None, "ctx", None)
    masters = (gain, weight, weight, weight, gain, gain, weight, gain, weight, weight, weight)
    return jax.shard_map(
        shards,
        mesh=mesh,
        in_specs=(stream, row, row) + masters,
        out_specs=(stream,) + masters,
        check_vma=False,
    )
```

```python
import functools

import jax
import jax.numpy as jnp
from jax import lax
from jax.experimental import pallas as pl
from jax.experimental.pallas import tpu as pltpu
from jax.sharding import PartitionSpec as P

HEAD_DIM = 128
GAIN_ROWS = 16
LANES = 256
VMEM_LIMIT = 56 * 1024 * 1024
VMEM_SLACK = 6 * 1024 * 1024
FLOPS_PER_US = 1.15e9
SCALE = HEAD_DIM ** (-0.5)
epsilon = 1e-06
rope_base = 1000000.0
low = jnp.bfloat16
f32 = jnp.float32


def swap(value):
    return lax.ppermute(value, "section", [(0, 1), (1, 0)])


def hop(value, step):
    count = lax.axis_size("ctx")
    return lax.ppermute(value, "ctx", [(i, i ^ step) for i in range(count)])


def hops(own):
    return [own] + [hop(own, k) for k in range(1, lax.axis_size("ctx"))]


def hops_split(own):
    if lax.axis_size("ctx") != 4:
        return hops(own)
    one, two = own[: own.shape[0] // 2], own[own.shape[0] // 2 :]
    one_near, two_near = hop(one, 1), hop(two, 2)
    near = jnp.concatenate([one_near, hop(two, 1)]), jnp.concatenate([hop(one, 2), two_near])
    return [own, *near, jnp.concatenate([hop(one_near, 2), hop(two_near, 1)])]


def met(parts):
    return [parts[0]] + [hop(parts[k], k) for k in range(1, len(parts))]


def beside(results, others):
    return lax.optimization_barrier((results, others))


def tie(value, other):
    return lax.optimization_barrier((value, other))[0]


def xored(pieces, index):
    for bit in range(len(pieces).bit_length() - 1):
        turned = ((index >> bit) & 1) == 1
        pieces = [jnp.where(turned, pieces[j ^ (1 << bit)], v) for j, v in enumerate(pieces)]
    return pieces


def dot(left, right):
    return jnp.dot(left, right, preferred_element_type=f32)


def dot_rows(left, right):
    return lax.dot_general(left, right, (((0,), (0,)), ((), ())), preferred_element_type=f32)


def dot_cols(left, right):
    return lax.dot_general(left, right, (((1,), (1,)), ((), ())), preferred_element_type=f32)


def rms_scale(values, gain):
    scale = lax.rsqrt(jnp.mean(values * values, axis=-1, keepdims=True) + epsilon)
    return values * scale * gain


def rms_back(values, gain, grad):
    scale = lax.rsqrt(jnp.mean(values * values, axis=-1, keepdims=True) + epsilon)
    unit = values * scale
    lifted = grad * gain
    grad_values = (lifted - unit * jnp.mean(lifted * unit, axis=-1, keepdims=True)) * scale
    return grad_values, jnp.sum(grad * unit, axis=0, keepdims=True)


def turn(values, cosine, sine):
    return values * cosine + pltpu.roll(values, HEAD_DIM // 2, 1) * sine


def turn_back(grad, cosine, sine):
    return grad * cosine + pltpu.roll(grad * sine, HEAD_DIM // 2, 1)


def chunk(j, size):
    return pl.ds(pl.multiple_of(j * size, size), size)


def span(j, size):
    return slice(j * size, (j + 1) * size)


def join(pieces, target):
    rows = pieces[0].shape[0]
    for i, piece in enumerate(pieces):
        target[span(i, rows), :] = piece[...]


def deal_out(parts, block, value):
    rows = parts[0].shape[0]
    for i, part in enumerate(parts):
        part[:, block] = value[span(i, rows)].astype(part.dtype)


def call(kernel, operands, outputs, took, scratch=(), scalars=(), after=(), limit=0):
    vmem = pl.BlockSpec(memory_space=pltpu.VMEM)
    smem = pl.BlockSpec(memory_space=pltpu.SMEM)
    anywhere = pl.BlockSpec(memory_space=pl.ANY)
    shapes = [jax.ShapeDtypeStruct(shape, dtype) for shape, dtype in outputs]
    moved = sum(v.size * v.dtype.itemsize for v in [*operands, *shapes])
    skipped, used = len(after), len(scalars)
    held = moved + sum(jnp.dtype(dtype).itemsize * shape[0] * shape[1] for shape, dtype in scratch)

    def body(*refs):
        kernel(*refs[skipped:])

    return pl.pallas_call(
        body,
        out_shape=shapes,
        in_specs=[anywhere] * skipped + [smem] * used + [vmem] * len(operands),
        out_specs=[vmem] * len(shapes),
        scratch_shapes=[pltpu.VMEM(shape, dtype) for shape, dtype in scratch],
        compiler_params=pltpu.CompilerParams(vmem_limit_bytes=limit or held + VMEM_SLACK),
        cost_estimate=pl.CostEstimate(
            flops=int(took * FLOPS_PER_US), bytes_accessed=moved, transcendentals=0
        ),
    )(*after, *scalars, *operands)


def mark_kernel(out):
    out[...] = jnp.zeros_like(out)


def mark(*values, took=20):
    return call(mark_kernel, [], [((8, 128), f32)], took, after=values)[0]


def window(values, at, size):
    base = at // 128 * 128
    block = values[:, base : base + LANES]
    return pltpu.roll(block, LANES - (at - base), 1) if at != base else block


def side_by_side(left, right, size):
    if size == LANES:
        return jnp.concatenate([left, right], axis=1)
    lane = lax.broadcasted_iota(jnp.int32, (left.shape[0], 128), 1)
    turned = pltpu.roll(right, size - 128, 1)
    middle = jnp.where(lane < size - 128, left[:, 128:], turned[:, :128])
    return jnp.concatenate([left[:, :128], middle, turned[:, 128:]], axis=1)


def add_kernel(count, rounded, sends_rows, *refs):
    parts, (residual, gain, total, normed) = refs[:count], refs[count:]
    value = residual[...].astype(f32)
    for part in parts:
        value = value + part[...].astype(f32)
    if rounded:
        value = value.astype(low).astype(f32)
    total[...] = value
    normed[...] = (value if sends_rows else rms_scale(value, gain[...])).astype(low)


def add_back_kernel(count, rounded, packs, *refs):
    parts, (upstream, middle, gain, *refs) = refs[:count], refs[count:]
    if packs:
        mlp_gains, query_gains, key_gains, *refs = refs
    total, sent, grad_gain, *packed = refs
    grad = parts[0][...].astype(f32)
    for part in parts[1:]:
        grad = grad + part[...].astype(f32)
    grad, gains = rms_back(middle[...].astype(f32), gain[...], grad)
    grad = upstream[...].astype(f32) + grad
    sent[...] = grad.astype(low)
    total[...] = grad.astype(low).astype(f32) if rounded else grad
    grad_gain[...] = gains
    if packs:
        (packed,) = packed
        packed[...] = jnp.zeros_like(packed)
        for z in range(packed.shape[0]):
            packed[z, 0:1, :] = gains[:, span(z, LANES)]
            packed[z, 1:2, :] = mlp_gains[:, span(z, LANES)]
            packed[z, 2:3, :HEAD_DIM] = query_gains[...]
            packed[z, 2:3, HEAD_DIM:] = key_gains[...]


def attention_forward_kernel(count, part, raw_rows, *refs):
    pieces, refs = refs[:count], refs[count:]
    if raw_rows:
        gain, chosen, *refs = refs
    own_weight, far_weight, cosine, sine, query_gain, key_gain, start, place, place_row, *refs = refs
    normed, raw, queries, keys, mixed, spread, *refs = refs
    values = refs[-1]
    tokens = normed.shape[0]
    rows = pieces[0].shape[0]
    depth = own_weight.shape[0]
    halves = keys.shape[1] // HEAD_DIM
    group = queries.shape[1] // keys.shape[1]
    step = (group + 2) * HEAD_DIM
    join(pieces, normed)
    if raw_rows:
        refs[0][...] = dot(chosen[:rows, :], normed[...]).astype(low)
        normed[...] = rms_scale(normed[...].astype(f32), gain[...]).astype(low)
    for half, weight in enumerate((own_weight, far_weight)):
        for j, at in enumerate((0, part + GAIN_ROWS)):
            total = None
            for z in range(depth):
                term = dot(normed[:, span(z, part)], weight[z, at : at + part, :])
                total = term if total is None else total + term
            raw[:, span(2 * half + j, LANES)] = total

    for half in range(halves):
        base = half * step
        at = base + group * HEAD_DIM
        own = span(half, HEAD_DIM)
        unit = rms_scale(raw[:, at : at + HEAD_DIM], key_gain[...])
        keys[:, own] = turn(unit, cosine[...], sine[...]).astype(low)
        values[:, own] = raw[:, at + HEAD_DIM : at + 2 * HEAD_DIM].astype(low)
        for g in range(group):
            unit = rms_scale(raw[:, base + g * HEAD_DIM : base + (g + 1) * HEAD_DIM], query_gain[...])
            unit = turn(unit, cosine[...], sine[...])
            queries[:, span(half * group + g, HEAD_DIM)] = unit.astype(low)

    @pl.loop(0, tokens // rows)
    def _(i):
        block = chunk(i, rows)
        visible = (place_row[...] >= start[block, :]) & (place_row[...] <= place[block, :])
        visible = jnp.concatenate([visible] * group, axis=0)
        for half in range(halves):
            own = span(half, HEAD_DIM)
            heads = range(half * group, (half + 1) * group)
            query = jnp.concatenate([queries[block, span(h, HEAD_DIM)] for h in heads], axis=0)
            scores = dot_cols(query, keys[:, own]) * SCALE
            scores = jnp.where(visible, scores, -1e30)
            top = jnp.max(scores, axis=-1, keepdims=True)
            raised = jnp.exp(scores - top)
            total = jnp.sum(raised, axis=-1, keepdims=True)
            probs = (raised * (1.0 / total)).astype(low)
            value = dot(probs, values[:, own]).astype(low)
            log_total = top + jnp.log(total)
            for g, head in enumerate(heads):
                mixed[block, span(head, HEAD_DIM)] = value[span(g, rows)]
                spread[block, head : head + 1] = log_total[span(g, rows)]


def pick_kernel(first_row, index, own, *out):
    for k, share in enumerate(out):
        share[...] = own[index[0] ^ k, first_row:, :]


def gather_shares(count, index, shares, whole):
    size = whole.shape[0] // 2
    share = size // count
    for k, value in enumerate(shares):
        to = k // count * size + (index[0] ^ (k % count)) * share
        to = pl.ds(pl.multiple_of(to, share), share)
        for j in range(whole.shape[1] // LANES):
            whole[to, span(j, LANES)] = value[span(j, share), :]


def gather_strided(index, own, far, whole):
    depth, core = own.shape[0], index[1]
    chunks = whole.shape[1] // LANES
    share = whole.shape[0] // depth
    half = share // 2
    at = own.shape[1] - chunks * half
    for z in range(depth):
        place = (z // (depth // 2) ^ core) * (depth // 2) + z % (depth // 2)
        for value, carried in ((own, core), (far, 1 - core)):
            to = pl.ds(pl.multiple_of(place * share + carried * half, 32), half)
            for j in range(chunks):
                whole[to, span(j, LANES)] = value[z, at + j * half : at + (j + 1) * half, :]


def gather_rows(form, count, index, given, whole):
    if form == "whole":
        whole[...] = given[0][...]
    elif form == "shares":
        gather_shares(count, index, given, whole)
    else:
        gather_strided(index, *given, whole)


def rows_kernel(count, form, dealt, index, left, *refs):
    if dealt:
        chosen, *refs = refs
    given, refs = refs[: -count - 1], refs[-count - 1 :]
    parts, whole = refs[:count], refs[count]
    gather_rows(form, count, index, given, whole)

    @pl.loop(0, whole.shape[1] // LANES)
    def _(j):
        block = chunk(j, LANES)
        value = dot(left[...], whole[:, block])
        deal_out(parts, block, dot(chosen[...], value.astype(low)) if dealt else value)


def lift_kernel(count, part, raw_rows, *refs):
    pieces, refs = refs[:count], refs[count:]
    if raw_rows:
        gain, chosen, *refs = refs
    own_weight, far_weight, normed, gate, lifted, product, *refs = refs
    half_size = product.shape[1] // 2
    depth = own_weight.shape[0]
    join(pieces, normed)
    if raw_rows:
        refs[0][...] = dot(chosen[: pieces[0].shape[0], :], normed[...]).astype(low)
        normed[...] = rms_scale(normed[...].astype(f32), gain[...]).astype(low)
    for half, weight in enumerate((own_weight, far_weight)):
        both = []
        for j in range(2 * half_size // LANES):
            total = None
            for z in range(depth):
                term = dot(normed[:, span(z, part)], weight[z, span(j, part), :])
                total = term if total is None else total + term
            both.append(total)
        both = jnp.concatenate(both, axis=1)
        one, two = both[:, :half_size], both[:, half_size:]
        at = span(half, half_size)
        gate[:, at] = one
        lifted[:, at] = two
        product[:, at] = (one * jax.nn.sigmoid(one) * two).astype(low)


def mlp_forward_kernel(count, part, form, index, *refs):
    pieces, refs = refs[:count], refs[count:]
    weights, refs = refs[:2], refs[2:]
    given, refs = (weights, refs) if form == "strided" else (refs[:1], refs[1:])
    kept, (*parts, whole) = refs[:4], refs[4:]
    lift_kernel(count, part, False, *pieces, *weights, *kept)
    rows_kernel(count, form, False, index, kept[3], *given, *parts, whole)


def mlp_backward_kernel(count, part, form, index, *refs):
    pieces, refs = refs[:count], refs[count:]
    own_weight, far_weight, gate, lifted, *refs = refs
    if form == "strided":
        given = [own_weight, far_weight]
    else:
        given, refs = refs[:1], refs[1:]
    parts, (branch, grad_both, down) = refs[:count], refs[count:]
    gather_rows(form, count, index, given, down)
    size = gate.shape[1] // 2
    depth = own_weight.shape[0]
    join(pieces, branch)
    for half in range(2):
        at = span(half, size)
        grad = dot_cols(branch[...], down[at, :])
        one, two = gate[:, at], lifted[:, at]
        sigmoid = jax.nn.sigmoid(one)
        grad_gate = grad * two * sigmoid * (1.0 + one * (1.0 - sigmoid))
        grad_both[:, span(2 * half, size)] = grad_gate.astype(low)
        grad_both[:, span(2 * half + 1, size)] = (grad * one * sigmoid).astype(low)
    for z in range(depth):
        total = None
        for half, weight in enumerate((own_weight, far_weight)):
            for j in range(2 * size // LANES):
                at = 2 * half * size + j * LANES
                term = dot_cols(grad_both[:, at : at + LANES], weight[z, span(j, part), :])
                total = term if total is None else total + term
        deal_out(parts, span(z, part), total)


def attention_backward_kernel(count, part, dealt, *refs):
    pieces, refs = refs[:count], refs[count:]
    if dealt:
        chosen, *refs = refs
    own_weight, far_weight, out, *refs = refs
    cosine, sine, query_gain, key_gain, start, place, place_row, *refs = refs
    raw, queries, keys, spread, *refs = refs
    parts, refs = refs[:count], refs[count:]
    branch, grad_raw, grad_query_gain, grad_key_gain, *refs = refs
    if dealt:
        dealt_branch, *refs = refs
    grad_mixed, values, grad_queries, grad_keys, grad_values = refs
    tokens, width = branch.shape
    rows = pieces[0].shape[0]
    depth = own_weight.shape[0]
    halves = keys.shape[1] // HEAD_DIM
    group = queries.shape[1] // keys.shape[1]
    step = (group + 2) * HEAD_DIM
    join(pieces, branch)
    if dealt:
        dealt_branch[...] = dot(chosen[:rows, :], branch[...]).astype(low)

    @pl.loop(0, grad_mixed.shape[1] // LANES)
    def _(j):
        block = chunk(j, LANES)
        grad_mixed[:, block] = dot_cols(branch[...], out[block, :]).astype(low)

    for half in range(halves):
        at = half * step + (group + 1) * HEAD_DIM
        values[:, span(half, HEAD_DIM)] = raw[:, at : at + HEAD_DIM].astype(low)
    grad_keys[...] = jnp.zeros_like(grad_keys)
    grad_values[...] = jnp.zeros_like(grad_values)

    @pl.loop(0, tokens // rows)
    def _(i):
        block = chunk(i, rows)
        visible = (place_row[...] >= start[block, :]) & (place_row[...] <= place[block, :])
        visible = jnp.concatenate([visible] * group, axis=0)
        for half in range(halves):
            own = span(half, HEAD_DIM)
            heads = range(half * group, (half + 1) * group)
            query = jnp.concatenate([queries[block, span(h, HEAD_DIM)] for h in heads], axis=0)
            grad = jnp.concatenate([grad_mixed[block, span(h, HEAD_DIM)] for h in heads], axis=0)
            log_total = jnp.concatenate([spread[block, h : h + 1] for h in heads], axis=0)
            scores = dot_cols(query, keys[:, own]) * SCALE
            scores = jnp.where(visible, scores, -1e30)
            probs = jnp.exp(scores - log_total)
            grad_probs = dot_cols(grad, values[:, own])
            weighted = jnp.sum(probs * grad_probs, axis=-1, keepdims=True)
            grad_scores = (probs * (grad_probs - weighted)).astype(low)
            grad_query = dot(grad_scores, keys[:, own]) * SCALE
            for g, head in enumerate(heads):
                grad_queries[block, span(head, HEAD_DIM)] = grad_query[span(g, rows)]
            grad_keys[:, own] += dot_rows(grad_scores, query) * SCALE
            grad_values[:, own] += dot_rows(probs.astype(low), grad)

    total_query = jnp.zeros((1, HEAD_DIM), f32)
    total_key = jnp.zeros((1, HEAD_DIM), f32)
    for half in range(halves):
        base = half * step
        own = span(half, HEAD_DIM)
        for g in range(group + 1):
            at = slice(base + g * HEAD_DIM, base + (g + 1) * HEAD_DIM)
            if g < group:
                grad, gain = grad_queries[:, span(half * group + g, HEAD_DIM)], query_gain[...]
            else:
                grad, gain = grad_keys[:, own], key_gain[...]
            grad = turn_back(grad, cosine[...], sine[...])
            grad, grad_gain = rms_back(raw[:, at], gain, grad)
            grad_raw[:, at] = grad.astype(low)
            if g < group:
                total_query += grad_gain
            else:
                total_key += grad_gain
        at = base + (group + 1) * HEAD_DIM
        grad_raw[:, at : at + HEAD_DIM] = grad_values[:, own].astype(low)
    grad_query_gain[...] = total_query
    grad_key_gain[...] = total_key
    for z in range(depth):
        total = None
        for half, weight in enumerate((own_weight, far_weight)):
            for j, at in enumerate((0, part + GAIN_ROWS)):
                grad = grad_raw[:, span(2 * half + j, LANES)]
                term = dot_cols(grad, weight[z, at : at + part, :])
                total = term if total is None else total + term
        if dealt:
            total = dot(chosen[...], total.astype(low))
        deal_out(parts, span(z, part), total)


def weight_grads_kernel(part, strided, index, left, grads, inner, branch, own, far, *refs):
    *rows_out, turned = refs
    depth = own.shape[0]
    chunks = grads.shape[1] // (2 * LANES)
    size = inner.shape[1] // 2
    for z in range(depth):
        turned[span(z, part), :] = left[:, span(z, part)].T
    for half, target in enumerate((own, far)):
        for j in range(chunks):
            total = dot(turned[...], grads[:, span(half * chunks + j, LANES)])
            for z in range(depth):
                target[z, span(j, part), :] = total[span(z, part)].astype(target.dtype)
    for half in range(2):
        rows = inner[:, span(half, size)].T
        for j in range(branch.shape[1] // LANES):
            total = dot(rows, branch[:, span(j, LANES)])
            if strided:
                share = size // (depth // 2)
                carried = share // 2
                at = slice(chunks * part + j * carried, chunks * part + (j + 1) * carried)
                for i in range(depth // 2):
                    z = (index[1] ^ half) * (depth // 2) + i
                    block = total[span(i, share)]
                    one, two = block[:carried], block[carried:]
                    own[z, at, :] = jnp.where(index[1] == 0, one, two)
                    far[z, at, :] = jnp.where(index[1] == 0, two, one).astype(far.dtype)
            else:
                target = rows_out[half]
                count = target.shape[0]
                share = size // count
                for k in range(count):
                    target[k, span(j, share), :] = total[span(k, share)].astype(target.dtype)


def sum_kernel(own, recv, total):
    total[...] = (own[...] + recv[...].astype(f32)).astype(low)


def meet_kernel(index, own, recv, own_rows, recv_rows, total, *rows):
    total[...] = (own[...] + recv[...].astype(f32)).astype(low)
    for k, row in enumerate(rows):
        at = index[0] ^ k
        row[...] = (own_rows[at] + recv_rows[at].astype(f32)).astype(low)


def layout_kernel(index, total, gains, far_gains, *refs):
    *rows, out = refs
    at = total.shape[1]
    end = at + rows[0].shape[0]
    out[:, :at, :] = total[...]
    for k, row in enumerate(rows):
        out[index[0] ^ k, at:end, :] = row[...]
    out[:, end:, :] = (gains[...] + far_gains[...]).astype(low)


def shards(
    stream_in,
    lengths,
    dealing,
    attention_gain,
    query_weight,
    key_weight,
    value_weight,
    query_gain,
    key_gain,
    out_weight,
    mlp_gain,
    gate_weight,
    up_weight,
    down_weight,
):
    core = lax.axis_index("section")
    piece = lax.axis_index("ctx")
    count = lax.axis_size("ctx")
    depth = lax.axis_size("fsdp")
    rows, width = stream_in.shape[3], stream_in.shape[4]
    tokens = rows * count
    first = core == 0
    query_half = query_weight.shape[2] // (2 * count)
    key_half = key_weight.shape[2] // (2 * count)
    hidden_half = gate_weight.shape[2] // (2 * count)
    part = query_weight.shape[1]
    aligned = depth == count == 4
    out_share, down_share = query_half // count, hidden_half // count
    index = jnp.stack([piece, core]).astype(jnp.int32)
    chunks = width // LANES
    qkv_rows = 2 * part + GAIN_ROWS
    lift_rows = 2 * hidden_half // LANES * part

    own = lax.dynamic_index_in_dim(stream_in[0, 0], core, 0, keepdims=False)
    other = swap(lax.dynamic_index_in_dim(stream_in[0, 0], 1 - core, 0, keepdims=False))
    entering = jnp.where(first, own, other)
    cotangent = jnp.where(first, other, own)

    where = jnp.stack([piece, core]).astype(jnp.int32)

    def cut(kernel, weights, constants, size, after=()):
        def half(i, where):
            return jnp.where(i == 0, 1 - where[1], where[1])

        def columns(i, where):
            return 0, 0, where[0] * 2 + half(i, where)

        def shares(i, where):
            return 0, half(i, where) * count + where[0], 0

        def even(i, where):
            return 0, 0, half(i, where) * 2

        def odd(i, where):
            return 0, 0, half(i, where) * 2 + 1

        def carried(i, where):
            return 0, where[0] * 2 + half(i, where), 0

        maps = {"columns": columns, "shares": shares, "even": even, "odd": odd, "carried": carried}
        in_specs = [
            pl.BlockSpec((1, height, breadth), maps[which]) for _, height, breadth, which in weights
        ]
        in_specs += [pl.BlockSpec(v.shape, lambda i, where: (0, 0)) for v in constants]
        in_specs += [pl.BlockSpec(memory_space=pl.ANY)] * len(after)

        def body(where, *refs):
            kernel(where, *refs[: len(refs) - 1 - len(after)], refs[-1])

        return pl.pallas_call(
            body,
            grid_spec=pltpu.PrefetchScalarGridSpec(
                num_scalar_prefetch=1,
                grid=(2,),
                in_specs=in_specs,
                out_specs=pl.BlockSpec((1, size, LANES), lambda i, where: (i, 0, 0)),
            ),
            out_shape=jax.ShapeDtypeStruct((2, size, LANES), low),
            compiler_params=pltpu.CompilerParams(vmem_limit_bytes=VMEM_LIMIT),
            cost_estimate=pl.CostEstimate(
                flops=int(3 * FLOPS_PER_US), bytes_accessed=12 * size * LANES, transcendentals=0
            ),
        )(where, *[weight for weight, *_ in weights], *constants, *after)

    def place_shares(weight, out, at):
        share = weight.shape[1]
        for j in range(chunks):
            out[0, at + j * share : at + (j + 1) * share, :] = weight[0, :, span(j, LANES)].astype(low)

    def qkv_cut_kernel(where, query, key, value, *refs):
        *rest, gains, out = refs
        out[0, :part, :] = query[0].astype(low)
        out[0, part : part + GAIN_ROWS, :] = gains[...]
        at = slice(part + GAIN_ROWS, qkv_rows)
        out[0, at, :key_half] = key[0].astype(low)
        out[0, at, key_half:] = value[0].astype(low)
        if aligned:
            place_shares(rest[0], out, qkv_rows)

    def mlp_cut_kernel(where, gate, up, out):
        both = jnp.concatenate([gate[0].astype(low), up[0].astype(low)], axis=1)
        for j in range(2 * hidden_half // LANES):
            out[0, span(j, part), :] = both[:, span(j, LANES)]

    def strided_cut_kernel(where, gate, gate_next, up, up_next, down, out):
        share = hidden_half // 2

        for c in range(count):

            @pl.when(where[0] == c)
            def _(c=c):
                sides = [window(v[0], c * share, share) for v in (gate, gate_next, up, up_next)]
                both = [side_by_side(*sides[:2], share), side_by_side(*sides[2:], share)]
                both = jnp.concatenate(both, axis=1).astype(low)
                for j in range(2 * hidden_half // LANES):
                    out[0, span(j, part), :] = both[:, span(j, LANES)]

        place_shares(down, out, lift_rows)

    gains = (attention_gain[0], mlp_gain[0], query_gain[0], key_gain[0])
    sizes = [gain.shape[0] for gain in gains]
    gain_block = jnp.concatenate(gains).astype(low)
    gain_block = jnp.pad(gain_block, (0, GAIN_ROWS * LANES - gain_block.shape[0]))
    gain_block = gain_block.reshape(GAIN_ROWS, LANES)

    def by_layer(cuts):
        mine, other = cuts[1], swap(cuts[0])
        return jnp.where(first, mine, other), jnp.where(first, other, mine)

    weights = [(query_weight, part, query_half, "columns"), (key_weight, part, key_half, "columns")]
    weights += [(value_weight, part, key_half, "columns")]
    weights += [(out_weight, out_share, width, "shares")] if aligned else []
    size = qkv_rows + (chunks * out_share if aligned else 0)
    cuts = cut(qkv_cut_kernel, weights, [gain_block], size)
    attention_blocks = by_layer(cuts)
    line = jnp.arange(size, dtype=jnp.int32)[:, None]
    gain_rows = (line >= part) & (line < part + GAIN_ROWS)
    attention_blocks = jnp.where(gain_rows, cuts[1], attention_blocks[0]), attention_blocks[1]
    point = mark(attention_blocks[0])
    if aligned:
        block = 2 * hidden_half
        weights = [(gate_weight, part, block, "even"), (gate_weight, part, block, "odd")]
        weights += [(up_weight, part, block, "even"), (up_weight, part, block, "odd")]
        weights += [(down_weight, down_share, width, "carried")]
        size = lift_rows + chunks * down_share
        mlp_blocks = by_layer(cut(strided_cut_kernel, weights, [], size, [point]))
    else:
        weights = [(gate_weight, part, hidden_half, "columns"), (up_weight, part, hidden_half, "columns")]
        mlp_blocks = by_layer(cut(mlp_cut_kernel, weights, [], lift_rows))

    def gathered(block):
        return lax.all_gather(block, "fsdp", axis=0, tiled=False)

    def whole_rows(weight, size):
        full = lax.all_gather(weight[0].astype(low), "fsdp", axis=0, tiled=True)
        full = lax.dynamic_slice_in_dim(full, piece * 2 * size, 2 * size, 0)
        other = swap(full)
        layers = jnp.where(first, full, other), jnp.where(first, other, full)
        own = [lax.dynamic_slice_in_dim(v, core * size, size, 0) for v in layers]
        far = [lax.dynamic_slice_in_dim(v, (1 - core) * size, size, 0) for v in layers]
        return [jnp.concatenate(pair, axis=0) for pair in zip(own, far)]

    def picked_rows(own, first_row):
        size = own.shape[1] - first_row
        kernel = functools.partial(pick_kernel, first_row)
        return call(kernel, [own], [((size, LANES), low)] * count, 1, scalars=[index])

    def split_gains(own):
        found, at = [], 0
        flat = own[:, part : part + GAIN_ROWS].reshape(depth, -1)
        for size in sizes:
            found.append(flat[:, at : at + size].reshape(1, -1).astype(f32))
            at += size
        return found

    lens = lax.dynamic_index_in_dim(lengths[0], core, 0, keepdims=False)
    slots = lax.dynamic_index_in_dim(dealing[0], core, 0, keepdims=False)
    order = jnp.arange(tokens, dtype=jnp.int32)
    natural = ((order // rows) ^ piece) * rows + order % rows
    bounds = jnp.cumsum(lens)
    passed = (bounds[None, :] <= natural[:, None]).astype(jnp.int32)
    start = jnp.sum(passed * lens[None, :], axis=1)
    position = natural - start
    rates = jnp.power(rope_base, jnp.arange(HEAD_DIM // 2, dtype=f32) * (-2.0 / HEAD_DIM))
    phase = position.astype(f32)[:, None] * rates
    cosine, sine = jnp.cos(phase), jnp.sin(phase)
    cosine = jnp.concatenate([cosine, cosine], axis=-1)
    sine = jnp.concatenate([-sine, sine], axis=-1)
    places = [start[:, None], natural[:, None], natural[None, :]]

    wanted = slots.reshape(count, rows)
    wanted = jnp.concatenate(xored([wanted[j] for j in range(count)], piece))
    wanted = ((wanted // rows) ^ piece) * rows + wanted % rows
    chosen = (wanted[:, None] == order[None, :]).astype(low)

    wide, half_wide = (rows, width), (tokens, width)
    heads_wide, hidden_wide = 2 * query_half, 2 * hidden_half

    def add(parts, residual, gain, rounded, sends_rows=False, after=()):
        kernel = functools.partial(add_kernel, count, rounded, sends_rows)
        outputs = [(wide, f32), (wide, low)]
        return call(kernel, [*parts, residual, gain], outputs, 2, after=after)

    def add_back(parts, upstream, middle, gain, rounded, gains=(), after=()):
        packs = aligned and len(gains) > 0
        kernel = functools.partial(add_back_kernel, count, rounded, packs)
        outputs = [(wide, f32), (wide, low), ((1, width), f32)]
        outputs += [((depth, GAIN_ROWS, LANES), f32)] if packs else []
        operands = [*parts, upstream, middle, gain] + (list(gains) if packs else [])
        return call(kernel, operands, outputs, 2, after=after)

    def attention_forward(pieces, weights, found, raw_rows, after=()):
        kernel = functools.partial(attention_forward_kernel, count, part, raw_rows)
        outputs = [(half_wide, low), ((tokens, 2 * (query_half + 2 * key_half)), f32)]
        outputs += [((tokens, heads_wide), low), ((tokens, 2 * key_half), low)]
        outputs += [((tokens, heads_wide), low), ((tokens, heads_wide // HEAD_DIM), f32)]
        operands = [*pieces] + ([found[0], chosen] if raw_rows else [])
        outputs += [(wide, low)] if raw_rows else []
        operands += [*weights, cosine, sine, found[2], found[3], *places]
        return call(kernel, operands, outputs, 6.0, [((tokens, 2 * key_half), low)], after=after)

    def rows_product(form, left, given, dealt=False, after=()):
        kernel = functools.partial(rows_kernel, count, form, dealt)
        outputs = [(wide, low)] * count + [((left.shape[1], width), low)]
        operands = [left] + ([chosen] if dealt else []) + [*given]
        *parts, whole = call(kernel, operands, outputs, 8, scalars=[index], after=after)
        return parts, whole

    def lift_forward(pieces, weights, gain=None, after=()):
        kernel = functools.partial(lift_kernel, count, part, gain is not None)
        outputs = [(half_wide, low)] + [((tokens, hidden_wide), f32)] * 2
        outputs += [((tokens, hidden_wide), low)]
        operands = [*pieces]
        if gain is not None:
            operands += [gain, chosen]
            outputs += [(wide, low)]
        return call(kernel, [*operands, *weights], outputs, 6, after=after)

    def mlp_forward(pieces, weights, form, down):
        kernel = functools.partial(mlp_forward_kernel, count, part, form)
        outputs = [(half_wide, low)] + [((tokens, hidden_wide), f32)] * 2
        outputs += [((tokens, hidden_wide), low)] + [(wide, low)] * count
        outputs += [((hidden_wide, width), low)]
        operands = [*pieces, *weights] + ([] if form == "strided" else [down])
        *results, whole = call(kernel, operands, outputs, 8, scalars=[index])
        return results[:4], results[4:], whole

    def mlp_backward(pieces, weights, form, down, kept, after=()):
        kernel = functools.partial(mlp_backward_kernel, count, part, form)
        outputs = [(wide, low)] * count + [(half_wide, low), ((tokens, 2 * hidden_wide), low)]
        outputs += [((hidden_wide, width), low)]
        operands = [*pieces, *weights, kept[1], kept[2]] + ([] if form == "strided" else [down])
        results = call(kernel, operands, outputs, 3.0, scalars=[index], after=after)
        parts, (branch, both, whole) = results[:count], results[count:]
        return parts, branch, both, whole

    def attention_backward(pieces, weights, out, found, kept, dealt=False, after=()):
        kernel = functools.partial(attention_backward_kernel, count, part, dealt)
        normed, raw, queries, keys, mixed, spread = kept
        outputs = [(wide, low)] * count + [(half_wide, low), (raw.shape, low)]
        outputs += [((1, HEAD_DIM), f32)] * 2
        outputs += [(wide, low)] if dealt else []
        scratch = [(queries.shape, low), (keys.shape, low), (queries.shape, f32)]
        scratch += [(keys.shape, f32)] * 2
        operands = [*pieces] + ([chosen] if dealt else [])
        operands += [*weights, out, cosine, sine, found[2], found[3], *places]
        operands += [raw, queries, keys, spread]
        results = call(
            kernel, operands, outputs, 18, scratch, after=after
        )
        parts, (branch, grad_raw, query, key, *rest) = results[:count], results[count:]
        return (parts, branch, grad_raw, (query, key), *rest)

    def weight_grads(left, grads, inner, branch, strided=False, after=()):
        kernel = functools.partial(weight_grads_kernel, part, strided)
        size = grads.shape[1] // (2 * LANES) * part
        row_shape = (count, inner.shape[1] // (2 * count) * chunks, LANES)
        if strided:
            size += row_shape[1]
        outputs = [((depth, size, LANES), f32), ((depth, size, LANES), low)]
        outputs += [] if strided else [(row_shape, f32), (row_shape, low)]
        operands = [left, grads, inner, branch]
        scratch = [((width, tokens), low)]
        return call(kernel, operands, outputs, 3.0, scratch, scalars=[index], after=after)

    if not aligned:
        outs, downs = whole_rows(out_weight, query_half), whole_rows(down_weight, hidden_half)

    def arrived(value, after):
        own = tie(value, after)
        return [own, swap(own)]

    def moving_rows(weights, first_row, whole):
        return met(picked_rows(weights[0], first_row)) if aligned else [whole]

    def with_far(shares):
        return [*shares, *map(swap, shares)] if aligned else shares

    out_form, down_form = ("shares", "strided") if aligned else ("whole", "whole")
    pieces = hops(tie(entering, point))
    cotangents = hops(tie(cotangent, point))
    early = pieces, cotangents, mlp_blocks, attention_blocks[1], chosen, cosine, sine, places
    if aligned:
        pack = lax.axis_index("fsdp")
        out_rows = tie(attention_blocks[0][qkv_rows:], point)
        out_rows = [out_rows] + [
            lax.ppermute(out_rows, "fsdp", [(i, i ^ k) for i in range(depth)]) for k in range(1, depth)
        ]
        out_rows = xored(out_rows, piece ^ pack)
        early = *early, out_rows
        shares = met(out_rows)
    else:
        shares = [outs[0]]
    qkv_first = arrived(gathered(attention_blocks[0][:qkv_rows]), early)
    found_own, found_far = split_gains(qkv_first[0]), split_gains(qkv_first[1])
    found_first = [jnp.where(first, own, far) for own, far in zip(found_own, found_far)]
    found_last = [jnp.where(first, far, own) for own, far in zip(found_own, found_far)]
    kept_attention_first = attention_forward(pieces, qkv_first, found_first, True)
    kept_attention_first, shares = beside(kept_attention_first, shares)
    *kept_attention_first, dealt_entering = kept_attention_first
    parts, out_first = rows_product(out_form, kept_attention_first[4], with_far(shares))
    middle_first, normed = add(met(parts), entering, found_first[1], False)
    pieces = hops(normed)
    lift_first = arrived(gathered(mlp_blocks[0]), pieces)
    kept_mlp_first, parts, down_first = mlp_forward(
        pieces, lift_first, down_form, None if aligned else downs[0]
    )

    hidden_last, normed = add(met(parts), middle_first, found_last[0], True)
    pieces = hops(normed)
    qkv_last = arrived(gathered(attention_blocks[1]), pieces)
    shares = moving_rows(qkv_last, qkv_rows, None if aligned else outs[1])
    kept_attention_last = attention_forward(pieces, qkv_last, found_last, False)
    kept_attention_last, shares = beside(kept_attention_last, shares)
    parts, out_last = rows_product(out_form, kept_attention_last[4], with_far(shares))
    middle_last, sent = add(met(parts), hidden_last, found_last[1], False, True)
    pieces = hops(sent)
    lift_last = arrived(gathered(mlp_blocks[1]), pieces)
    *kept_mlp_last, dealt_middle = lift_forward(pieces, lift_last, found_last[1])

    def meet(grads, swapped):
        own, far, own_rows, far_rows = grads
        if not aligned:
            total = (own + swapped[0].astype(f32)).astype(low)
            return total, [own_rows + swapped[1].astype(f32)]
        outputs = [(own.shape, low)] + [(own_rows.shape[1:], low)] * count
        operands = [own, swapped[0], own_rows, swapped[1]]
        total, *rows_by = call(meet_kernel, operands, outputs, 4, scalars=[index])
        return total, rows_by

    def laid_out(total, rows_by, packed):
        if not aligned:
            return total
        size = total.shape[1] + rows_by[0].shape[0] + GAIN_ROWS
        outputs = [((depth, size, LANES), low)]
        operands = [total, packed[0], swap(packed[0]), *rows_by]
        return call(layout_kernel, operands, outputs, 0.9, scalars=[index])[0]

    def gains_reduced(from_first, from_last):
        def by_pack(gains):
            return jnp.concatenate([gain.reshape(depth, -1) for gain in gains], axis=1)

        one, two = by_pack(from_first), by_pack(from_last)
        total = jnp.where(first, one, two) + swap(jnp.where(first, two, one))
        pack = lax.axis_index("fsdp")
        summed = lax.dynamic_index_in_dim(total, pack, 0)
        for k in range(1, depth):
            sent = lax.dynamic_index_in_dim(total, pack ^ k, 0)
            summed = summed + lax.ppermute(sent, "fsdp", [(i, i ^ k) for i in range(depth)])
        return sum(hops(summed))

    def scattered(operand):
        return lax.psum_scatter(operand, "fsdp", scatter_dimension=0, tiled=False)

    def met_rows(rows_by):
        return met(rows_by) if aligned else rows_by

    def rows_fallback(rest):
        (rest,) = rest
        share = rest.shape[1] // chunks
        rest = rest.reshape(count, chunks, share, LANES).swapaxes(1, 2).reshape(-1, width)
        full = jnp.zeros((2 * count * rest.shape[0], width), low)
        at = (piece * 2 + core) * rest.shape[0]
        full = lax.dynamic_update_slice_in_dim(full, rest.astype(low), at, 0)
        return lax.psum(lax.psum_scatter(full, "fsdp", scatter_dimension=0, tiled=True), "ctx")

    def returned(pieces, layer):
        own = jnp.stack(pieces)
        return own, lax.ppermute(own, "section", [(1 - layer, layer)])

    def mlp_meet(grads, swapped):
        if aligned:
            return call(sum_kernel, [grads[0], swapped[0]], [(grads[0].shape, low)], 2)
        return meet(grads, swapped)

    down_whole = None if aligned else downs[1]
    parts, branch, both, whole = mlp_backward(cotangents, lift_last, down_form, down_whole, kept_mlp_last)
    mlp_grads = weight_grads(kept_mlp_last[0], both, kept_mlp_last[3], branch, aligned)
    last_parts, unused = rows_product("whole", kept_mlp_last[3], [whole], True, after=[both])
    (mlp_grads, last_parts), parts = beside((mlp_grads, last_parts), met(parts))
    swapped = [swap(v) for v in mlp_grads[1::2]]
    grad, sent, mlp_gain = add_back(parts, cotangent, middle_last, found_last[1], False)
    (total, *down_rows), pieces = beside(mlp_meet(mlp_grads, swapped), hops(sent))
    mlp_last = scattered(total)

    results = attention_backward(
        pieces, qkv_last, out_last, found_last, kept_attention_last, after=[mark(total)]
    )
    results, last_parts = beside(results, met(tie(last_parts, pieces[1])))
    parts, branch, grad_raw, head_gains = results
    last = dealt_middle.astype(f32)
    for value in last_parts:
        last = last + value.astype(f32)
    last = last.astype(low)
    attention_grads = weight_grads(kept_attention_last[0], grad_raw, kept_attention_last[4], branch)
    attention_grads, parts = beside(attention_grads, met(parts))
    swapped = swap(attention_grads[1]), swap(attention_grads[3])
    grad, sent, gain, *packed = add_back(
        parts, grad, hidden_last, found_last[0], True, (mlp_gain, *head_gains)
    )
    gains_last = (gain, mlp_gain, *head_gains)
    down_grad_last = None if aligned else rows_fallback(*down_rows)
    total, out_rows = meet(attention_grads, swapped)
    moved, pieces = beside(met_rows(out_rows), hops(sent))
    operand, mlp_last = beside(laid_out(total, moved, packed), mlp_last)
    attention_last = scattered(operand)

    near = [hop(mlp_last, k) for k in range(1, count - 1)]
    results = mlp_backward(
        pieces, lift_first, "whole", down_first, kept_mlp_first, after=[mark(operand, mlp_last)]
    )
    parts, branch, both, unused = results
    mlp_grads = weight_grads(kept_mlp_first[0], both, kept_mlp_first[3], branch, aligned)
    mlp_grads, parts = beside(mlp_grads, met(parts))
    out_grad_last = None if aligned else rows_fallback(out_rows)
    swapped = [swap(v) for v in mlp_grads[1::2]]
    grad, sent, mlp_gain = add_back(parts, grad, middle_first, found_first[1], False)
    (total, *down_rows), pieces = beside(mlp_meet(mlp_grads, swapped), hops(sent))
    total, attention_last = beside(total, attention_last)
    mlp_first = scattered(total)

    attention_last = tie(attention_last, pieces[1])
    near_last = [hop(attention_last, k) for k in range(1, count - 1)]
    results = attention_backward(
        pieces,
        qkv_first,
        out_first,
        found_first,
        kept_attention_first,
        True,
        after=[mark(total, attention_last)],
    )
    results, near, near_last = lax.optimization_barrier((results, near, near_last))
    parts, branch, grad_raw, head_gains, dealt_branch = results
    grads = weight_grads(kept_attention_first[0], grad_raw, kept_attention_first[4], branch)
    swapped = swap(grads[1]), swap(grads[3])
    grads, parts = beside(grads, met(parts))
    held = grads[0], grads[2]
    unused, grad, gain, *packed = add_back(
        parts, dealt_branch, dealt_entering, found_first[0], True, (mlp_gain, *head_gains)
    )
    down_grad_first = None if aligned else rows_fallback(*down_rows)
    total, out_rows = meet((held[0], grads[1], held[1], grads[3]), swapped)
    moved, mlp_first = beside(met_rows(out_rows), mlp_first)
    operand = laid_out(total, moved, packed)
    out_grad_first = None if aligned else rows_fallback(out_rows)
    gains_first = (gain, mlp_gain, *head_gains)
    attention_first = scattered(operand)
    point = mark(operand)
    sums = None if aligned else gains_reduced(gains_first, gains_last)
    mlp_last = [mlp_last, *near, hop(tie(mlp_last, parts), count - 1)]
    attention_last = [attention_last, *near_last, hop(tie(attention_last, point), count - 1)]
    mlp_first = hops(tie(mlp_first, point))
    mlp_last, attention_last = returned(mlp_last, 1), returned(attention_last, 1)
    attention_first = hops(tie(attention_first, mlp_first))
    mlp_first = returned(mlp_first, 0)
    own = jnp.where(first, grad, last)
    other = swap(jnp.where(first, last, grad))
    boundary = jnp.where(first, jnp.stack([own, other]), jnp.stack([other, own]))

    def settle(kernel, from_first, from_last, outputs, at_once=1, after=()):
        size = from_first[0].shape[1]

        def block_of(layer):
            def at(i, where):
                return jnp.where(where[1] == layer, i ^ (where[0] // at_once), 0), 0, 0

            return pl.BlockSpec((at_once, size, LANES), at)

        def body(where, *refs):
            kernel(where, *refs[:4], *refs[4 + len(after) :])

        return pl.pallas_call(
            body,
            grid_spec=pltpu.PrefetchScalarGridSpec(
                num_scalar_prefetch=1,
                grid=(count // at_once,),
                in_specs=[block_of(0), block_of(0), block_of(1), block_of(1)]
                + [pl.BlockSpec(memory_space=pl.ANY)] * len(after),
                out_specs=[
                    pl.BlockSpec(block, functools.partial(lambda at, i, where: at(i), at))
                    for _, block, at in outputs
                ],
            ),
            out_shape=[jax.ShapeDtypeStruct(shape, f32) for shape, _, _ in outputs],
            compiler_params=pltpu.CompilerParams(vmem_limit_bytes=VMEM_LIMIT),
            cost_estimate=pl.CostEstimate(
                flops=0, bytes_accessed=12 * count * size * LANES, transcendentals=0
            ),
        )(where, *from_first, *from_last, *after)

    def halves_of(where, blocks, body):
        @pl.when(where[1] == 0)
        def _():
            body(0, blocks[0])
            body(1, blocks[1])

        @pl.when(where[1] == 1)
        def _():
            body(1, blocks[2])
            body(0, blocks[3])

    def place_rows(block, at, half, out):
        share = out.shape[1]
        for j in range(chunks):
            out[half, :, span(j, LANES)] = block[0, at + j * share : at + (j + 1) * share, :].astype(f32)

    def mlp_settle_kernel(where, *refs):
        blocks, (gate, up) = refs[:4], refs[4:]

        def body(half, block):
            both = [block[0, span(j, part), :].astype(f32) for j in range(2 * hidden_half // LANES)]
            both = jnp.concatenate(both, axis=1)
            gate[:, span(half, hidden_half)] = both[:, :hidden_half]
            up[:, span(half, hidden_half)] = both[:, hidden_half:]

        halves_of(where, blocks, body)

    def strided_settle_kernel(where, *refs):
        blocks, (gate, up, down) = refs[:4], refs[4:]
        share = hidden_half // 2
        step = pl.program_id(0)

        def body(half, block):
            pair = []
            for side in range(2):
                at = (where[0] % 2) ^ side
                both = [block[at, span(j, part), :].astype(f32) for j in range(2 * hidden_half // LANES)]
                pair.append(jnp.concatenate(both, axis=1))
                for j in range(chunks):
                    rows_at = slice(lift_rows + j * down_share, lift_rows + (j + 1) * down_share)
                    down[2 * side + half, :, span(j, LANES)] = block[at, rows_at, :].astype(f32)
            for target, start in ((gate, 0), (up, hidden_half)):
                for i in range(2):
                    sides = [window(v[:, start : start + hidden_half], i * share, share) for v in pair]
                    to = (2 * half + i) * 2 * hidden_half + step * hidden_half
                    to = pl.ds(pl.multiple_of(to, 128), hidden_half)
                    target[:, to] = side_by_side(*sides, share)

        halves_of(where, blocks, body)

    def attention_settle_kernel(where, *refs):
        blocks, (query, key, value, *out) = refs[:4], refs[4:]
        if aligned:

            @pl.when(pl.program_id(0) == 0)
            def _():
                out[1][...] = jnp.zeros_like(out[1])

        def body(half, block):
            query[:, span(half, query_half)] = block[0, :part, :].astype(f32)
            both = block[0, part : 2 * part, :].astype(f32)
            key[:, span(half, key_half)] = both[:, :key_half]
            value[:, span(half, key_half)] = both[:, key_half:]
            if aligned:
                place_rows(block, 2 * part, half, out[0])
                if half == 0:
                    out[1][...] += block[0, 2 * part + chunks * out_share :, :].astype(f32)

        halves_of(where, blocks, body)

    def column_output(size):
        return ((part, 2 * count * size), (part, 2 * size), lambda i: (0, i))

    def row_output(size):
        return ((2, size, width), (2, size // count, width), lambda i: (0, i, 0))

    if aligned:
        whole_columns = (part, 2 * count * hidden_half)
        outputs = [(whole_columns, whole_columns, lambda i: (0, 0))] * 2
        outputs += [((2 * count, down_share, width), (count, down_share, width), lambda i: (i, 0, 0))]
        settled = settle(strided_settle_kernel, mlp_first, mlp_last, outputs, 2, [other])
    else:
        settled = settle(mlp_settle_kernel, mlp_first, mlp_last, [column_output(hidden_half)] * 2)
    (grad_gate, grad_up, *grad_down), attention_first = beside(settled, attention_first)
    outputs = [column_output(query_half)] + [column_output(key_half)] * 2
    if aligned:
        outputs += [row_output(query_half)]
        outputs += [((GAIN_ROWS, LANES), (GAIN_ROWS, LANES), lambda i: (0, 0))]
    grad_query, grad_key, grad_value, *grad_out = settle(
        attention_settle_kernel, returned(attention_first, 0), attention_last, outputs
    )
    if aligned:
        sums = grad_out[1]
        at = lax.axis_index("fsdp") * sizes[2]
        head_sums = [lax.dynamic_slice_in_dim(sums[2:3], at + k * HEAD_DIM, sizes[2], 1) for k in range(2)]
        split = [sums[0:1], sums[1:2], *head_sums]
    else:
        split, at = [], 0
        for size in sizes:
            split.append(sums[:, at : at + size])
            at += size

    if aligned:
        grad_out, grad_down = grad_out[0].reshape(-1, width), grad_down[0].reshape(-1, width)
    else:
        pair = []
        for one, two in ((out_grad_first, out_grad_last), (down_grad_first, down_grad_last)):
            own = jnp.where(first, one, two).astype(f32)
            pair.append(own + swap(jnp.where(first, two, one)).astype(f32))
        grad_out, grad_down = pair
    return (
        boundary[None, None],
        split[0],
        grad_query[None],
        grad_key[None],
        grad_value[None],
        split[2],
        split[3],
        grad_out[None],
        split[1],
        grad_gate[None],
        grad_up[None],
        grad_down[None],
    )


def solution(mesh):
    weight, gain, row = P("section", "fsdp", None), P("section", "fsdp"), P("fsdp", None, None)
    stream = P("section", "fsdp", None, "ctx", None)
    masters = (gain, weight, weight, weight, gain, gain, weight, gain, weight, weight, weight)
    return jax.shard_map(
        shards,
        mesh=mesh,
        in_specs=(stream, row, row) + masters,
        out_specs=(stream,) + masters,
        check_vma=False,
    )
```

```python
import functools

import jax
import jax.numpy as jnp
from jax import lax
from jax.experimental import pallas as pl
from jax.experimental.pallas import tpu as pltpu
from jax.sharding import PartitionSpec as P

HEAD_DIM = 128
GAIN_ROWS = 16
LANES = 256
VMEM_LIMIT = 56 * 1024 * 1024
VMEM_SLACK = 6 * 1024 * 1024
FLOPS_PER_US = 1.15e9
SCALE = HEAD_DIM ** (-0.5)
epsilon = 1e-06
rope_base = 1000000.0
low = jnp.bfloat16
f32 = jnp.float32


def swap(value):
    return lax.ppermute(value, "section", [(0, 1), (1, 0)])


def hop(value, step):
    count = lax.axis_size("ctx")
    return lax.ppermute(value, "ctx", [(i, i ^ step) for i in range(count)])


def hops(own):
    return [own] + [hop(own, k) for k in range(1, lax.axis_size("ctx"))]


def hops_split(own):
    if lax.axis_size("ctx") != 4:
        return hops(own)
    one, two = own[: own.shape[0] // 2], own[own.shape[0] // 2 :]
    one_near, two_near = hop(one, 1), hop(two, 2)
    near = jnp.concatenate([one_near, hop(two, 1)]), jnp.concatenate([hop(one, 2), two_near])
    return [own, *near, jnp.concatenate([hop(one_near, 2), hop(two_near, 1)])]


def met(parts):
    return [parts[0]] + [hop(parts[k], k) for k in range(1, len(parts))]


def beside(results, others):
    return lax.optimization_barrier((results, others))


def tie(value, other):
    return lax.optimization_barrier((value, other))[0]


def xored(pieces, index):
    for bit in range(len(pieces).bit_length() - 1):
        turned = ((index >> bit) & 1) == 1
        pieces = [jnp.where(turned, pieces[j ^ (1 << bit)], v) for j, v in enumerate(pieces)]
    return pieces


def dot(left, right):
    return jnp.dot(left, right, preferred_element_type=f32)


def dot_rows(left, right):
    return lax.dot_general(left, right, (((0,), (0,)), ((), ())), preferred_element_type=f32)


def dot_cols(left, right):
    return lax.dot_general(left, right, (((1,), (1,)), ((), ())), preferred_element_type=f32)


def rms_scale(values, gain):
    scale = lax.rsqrt(jnp.mean(values * values, axis=-1, keepdims=True) + epsilon)
    return values * scale * gain


def rms_back(values, gain, grad):
    scale = lax.rsqrt(jnp.mean(values * values, axis=-1, keepdims=True) + epsilon)
    unit = values * scale
    lifted = grad * gain
    grad_values = (lifted - unit * jnp.mean(lifted * unit, axis=-1, keepdims=True)) * scale
    return grad_values, jnp.sum(grad * unit, axis=0, keepdims=True)


def turn(values, cosine, sine):
    return values * cosine + pltpu.roll(values, HEAD_DIM // 2, 1) * sine


def turn_back(grad, cosine, sine):
    return grad * cosine + pltpu.roll(grad * sine, HEAD_DIM // 2, 1)


def chunk(j, size):
    return pl.ds(pl.multiple_of(j * size, size), size)


def span(j, size):
    return slice(j * size, (j + 1) * size)


def join(pieces, target):
    rows = pieces[0].shape[0]
    for i, piece in enumerate(pieces):
        target[span(i, rows), :] = piece[...]


def deal_out(parts, block, value):
    rows = parts[0].shape[0]
    for i, part in enumerate(parts):
        part[:, block] = value[span(i, rows)].astype(part.dtype)


def call(kernel, operands, outputs, took, scratch=(), scalars=(), after=(), limit=0):
    vmem = pl.BlockSpec(memory_space=pltpu.VMEM)
    smem = pl.BlockSpec(memory_space=pltpu.SMEM)
    anywhere = pl.BlockSpec(memory_space=pl.ANY)
    shapes = [jax.ShapeDtypeStruct(shape, dtype) for shape, dtype in outputs]
    moved = sum(v.size * v.dtype.itemsize for v in [*operands, *shapes])
    skipped, used = len(after), len(scalars)
    held = moved + sum(jnp.dtype(dtype).itemsize * shape[0] * shape[1] for shape, dtype in scratch)

    def body(*refs):
        kernel(*refs[skipped:])

    return pl.pallas_call(
        body,
        out_shape=shapes,
        in_specs=[anywhere] * skipped + [smem] * used + [vmem] * len(operands),
        out_specs=[vmem] * len(shapes),
        scratch_shapes=[pltpu.VMEM(shape, dtype) for shape, dtype in scratch],
        compiler_params=pltpu.CompilerParams(vmem_limit_bytes=limit or held + VMEM_SLACK),
        cost_estimate=pl.CostEstimate(
            flops=int(took * FLOPS_PER_US), bytes_accessed=moved, transcendentals=0
        ),
    )(*after, *scalars, *operands)


def mark_kernel(out):
    out[...] = jnp.zeros_like(out)


def mark(*values, took=20):
    return call(mark_kernel, [], [((8, 128), f32)], took, after=values)[0]


def window(values, at, size):
    base = at // 128 * 128
    block = values[:, base : base + LANES]
    return pltpu.roll(block, LANES - (at - base), 1) if at != base else block


def side_by_side(left, right, size):
    if size == LANES:
        return jnp.concatenate([left, right], axis=1)
    lane = lax.broadcasted_iota(jnp.int32, (left.shape[0], 128), 1)
    turned = pltpu.roll(right, size - 128, 1)
    middle = jnp.where(lane < size - 128, left[:, 128:], turned[:, :128])
    return jnp.concatenate([left[:, :128], middle, turned[:, 128:]], axis=1)


def add_kernel(count, rounded, sends_rows, *refs):
    parts, (residual, gain, total, normed) = refs[:count], refs[count:]
    value = residual[...].astype(f32)
    for part in parts:
        value = value + part[...].astype(f32)
    if rounded:
        value = value.astype(low).astype(f32)
    total[...] = value
    normed[...] = (value if sends_rows else rms_scale(value, gain[...])).astype(low)


def add_back_kernel(count, rounded, packs, *refs):
    parts, (upstream, middle, gain, *refs) = refs[:count], refs[count:]
    if packs:
        mlp_gains, query_gains, key_gains, *refs = refs
    total, sent, grad_gain, *packed = refs
    grad = parts[0][...].astype(f32)
    for part in parts[1:]:
        grad = grad + part[...].astype(f32)
    grad, gains = rms_back(middle[...].astype(f32), gain[...], grad)
    grad = upstream[...].astype(f32) + grad
    sent[...] = grad.astype(low)
    total[...] = grad.astype(low).astype(f32) if rounded else grad
    grad_gain[...] = gains
    if packs:
        (packed,) = packed
        packed[...] = jnp.zeros_like(packed)
        for z in range(packed.shape[0]):
            packed[z, 0:1, :] = gains[:, span(z, LANES)]
            packed[z, 1:2, :] = mlp_gains[:, span(z, LANES)]
            packed[z, 2:3, :HEAD_DIM] = query_gains[...]
            packed[z, 2:3, HEAD_DIM:] = key_gains[...]


def attention_forward_kernel(count, part, raw_rows, *refs):
    pieces, refs = refs[:count], refs[count:]
    if raw_rows:
        gain, chosen, *refs = refs
    own_weight, far_weight, cosine, sine, query_gain, key_gain, start, place, place_row, *refs = refs
    normed, raw, queries, keys, mixed, spread, *refs = refs
    values = refs[-1]
    tokens = normed.shape[0]
    rows = pieces[0].shape[0]
    depth = own_weight.shape[0]
    halves = keys.shape[1] // HEAD_DIM
    group = queries.shape[1] // keys.shape[1]
    step = (group + 2) * HEAD_DIM
    join(pieces, normed)
    if raw_rows:
        refs[0][...] = dot(chosen[:rows, :], normed[...]).astype(low)
        normed[...] = rms_scale(normed[...].astype(f32), gain[...]).astype(low)
    for half, weight in enumerate((own_weight, far_weight)):
        for j, at in enumerate((0, part + GAIN_ROWS)):
            total = None
            for z in range(depth):
                term = dot(normed[:, span(z, part)], weight[z, at : at + part, :])
                total = term if total is None else total + term
            raw[:, span(2 * half + j, LANES)] = total

    for half in range(halves):
        base = half * step
        at = base + group * HEAD_DIM
        own = span(half, HEAD_DIM)
        unit = rms_scale(raw[:, at : at + HEAD_DIM], key_gain[...])
        keys[:, own] = turn(unit, cosine[...], sine[...]).astype(low)
        values[:, own] = raw[:, at + HEAD_DIM : at + 2 * HEAD_DIM].astype(low)
        for g in range(group):
            unit = rms_scale(raw[:, base + g * HEAD_DIM : base + (g + 1) * HEAD_DIM], query_gain[...])
            unit = turn(unit, cosine[...], sine[...])
            queries[:, span(half * group + g, HEAD_DIM)] = unit.astype(low)

    @pl.loop(0, tokens // rows)
    def _(i):
        block = chunk(i, rows)
        visible = (place_row[...] >= start[block, :]) & (place_row[...] <= place[block, :])
        visible = jnp.concatenate([visible] * group, axis=0)
        for half in range(halves):
            own = span(half, HEAD_DIM)
            heads = range(half * group, (half + 1) * group)
            query = jnp.concatenate([queries[block, span(h, HEAD_DIM)] for h in heads], axis=0)
            scores = dot_cols(query, keys[:, own]) * SCALE
            scores = jnp.where(visible, scores, -1e30)
            top = jnp.max(scores, axis=-1, keepdims=True)
            raised = jnp.exp(scores - top)
            total = jnp.sum(raised, axis=-1, keepdims=True)
            probs = (raised * (1.0 / total)).astype(low)
            value = dot(probs, values[:, own]).astype(low)
            log_total = top + jnp.log(total)
            for g, head in enumerate(heads):
                mixed[block, span(head, HEAD_DIM)] = value[span(g, rows)]
                spread[block, head : head + 1] = log_total[span(g, rows)]


def pick_kernel(first_row, index, own, *out):
    for k, share in enumerate(out):
        share[...] = own[index[0] ^ k, first_row:, :]


def gather_shares(count, index, shares, whole):
    size = whole.shape[0] // 2
    share = size // count
    for k, value in enumerate(shares):
        to = k // count * size + (index[0] ^ (k % count)) * share
        to = pl.ds(pl.multiple_of(to, share), share)
        for j in range(whole.shape[1] // LANES):
            whole[to, span(j, LANES)] = value[span(j, share), :]


def gather_strided(index, own, far, whole):
    depth, core = own.shape[0], index[1]
    chunks = whole.shape[1] // LANES
    share = whole.shape[0] // depth
    half = share // 2
    at = own.shape[1] - chunks * half
    for z in range(depth):
        place = (z // (depth // 2) ^ core) * (depth // 2) + z % (depth // 2)
        for value, carried in ((own, core), (far, 1 - core)):
            to = pl.ds(pl.multiple_of(place * share + carried * half, 32), half)
            for j in range(chunks):
                whole[to, span(j, LANES)] = value[z, at + j * half : at + (j + 1) * half, :]


def gather_rows(form, count, index, given, whole):
    if form == "whole":
        whole[...] = given[0][...]
    elif form == "shares":
        gather_shares(count, index, given, whole)
    else:
        gather_strided(index, *given, whole)


def rows_kernel(count, form, dealt, index, left, *refs):
    if dealt:
        chosen, *refs = refs
    given, refs = refs[: -count - 1], refs[-count - 1 :]
    parts, whole = refs[:count], refs[count]
    gather_rows(form, count, index, given, whole)

    @pl.loop(0, whole.shape[1] // LANES)
    def _(j):
        block = chunk(j, LANES)
        value = dot(left[...], whole[:, block])
        deal_out(parts, block, dot(chosen[...], value.astype(low)) if dealt else value)


def lift_kernel(count, part, raw_rows, *refs):
    pieces, refs = refs[:count], refs[count:]
    if raw_rows:
        gain, chosen, *refs = refs
    own_weight, far_weight, normed, gate, lifted, product, *refs = refs
    half_size = product.shape[1] // 2
    depth = own_weight.shape[0]
    join(pieces, normed)
    if raw_rows:
        refs[0][...] = dot(chosen[: pieces[0].shape[0], :], normed[...]).astype(low)
        normed[...] = rms_scale(normed[...].astype(f32), gain[...]).astype(low)
    for half, weight in enumerate((own_weight, far_weight)):
        both = []
        for j in range(2 * half_size // LANES):
            total = None
            for z in range(depth):
                term = dot(normed[:, span(z, part)], weight[z, span(j, part), :])
                total = term if total is None else total + term
            both.append(total)
        both = jnp.concatenate(both, axis=1)
        one, two = both[:, :half_size], both[:, half_size:]
        at = span(half, half_size)
        gate[:, at] = one
        lifted[:, at] = two
        product[:, at] = (one * jax.nn.sigmoid(one) * two).astype(low)


def mlp_forward_kernel(count, part, form, index, *refs):
    pieces, refs = refs[:count], refs[count:]
    weights, refs = refs[:2], refs[2:]
    given, refs = (weights, refs) if form == "strided" else (refs[:1], refs[1:])
    kept, (*parts, whole) = refs[:4], refs[4:]
    lift_kernel(count, part, False, *pieces, *weights, *kept)
    rows_kernel(count, form, False, index, kept[3], *given, *parts, whole)


def mlp_backward_kernel(count, part, form, index, *refs):
    pieces, refs = refs[:count], refs[count:]
    own_weight, far_weight, gate, lifted, *refs = refs
    if form == "strided":
        given = [own_weight, far_weight]
    else:
        given, refs = refs[:1], refs[1:]
    parts, (branch, grad_both, down) = refs[:count], refs[count:]
    gather_rows(form, count, index, given, down)
    size = gate.shape[1] // 2
    depth = own_weight.shape[0]
    join(pieces, branch)
    for half in range(2):
        at = span(half, size)
        grad = dot_cols(branch[...], down[at, :])
        one, two = gate[:, at], lifted[:, at]
        sigmoid = jax.nn.sigmoid(one)
        grad_gate = grad * two * sigmoid * (1.0 + one * (1.0 - sigmoid))
        grad_both[:, span(2 * half, size)] = grad_gate.astype(low)
        grad_both[:, span(2 * half + 1, size)] = (grad * one * sigmoid).astype(low)
    for z in range(depth):
        total = None
        for half, weight in enumerate((own_weight, far_weight)):
            for j in range(2 * size // LANES):
                at = 2 * half * size + j * LANES
                term = dot_cols(grad_both[:, at : at + LANES], weight[z, span(j, part), :])
                total = term if total is None else total + term
        deal_out(parts, span(z, part), total)


def attention_backward_kernel(count, part, dealt, *refs):
    pieces, refs = refs[:count], refs[count:]
    if dealt:
        chosen, *refs = refs
    own_weight, far_weight, out, *refs = refs
    cosine, sine, query_gain, key_gain, start, place, place_row, *refs = refs
    raw, queries, keys, spread, *refs = refs
    parts, refs = refs[:count], refs[count:]
    branch, grad_raw, grad_query_gain, grad_key_gain, *refs = refs
    if dealt:
        dealt_branch, *refs = refs
    grad_mixed, values, grad_queries, grad_keys, grad_values = refs
    tokens, width = branch.shape
    rows = pieces[0].shape[0]
    depth = own_weight.shape[0]
    halves = keys.shape[1] // HEAD_DIM
    group = queries.shape[1] // keys.shape[1]
    step = (group + 2) * HEAD_DIM
    join(pieces, branch)
    if dealt:
        dealt_branch[...] = dot(chosen[:rows, :], branch[...]).astype(low)

    @pl.loop(0, grad_mixed.shape[1] // LANES)
    def _(j):
        block = chunk(j, LANES)
        grad_mixed[:, block] = dot_cols(branch[...], out[block, :]).astype(low)

    for half in range(halves):
        at = half * step + (group + 1) * HEAD_DIM
        values[:, span(half, HEAD_DIM)] = raw[:, at : at + HEAD_DIM].astype(low)
    grad_keys[...] = jnp.zeros_like(grad_keys)
    grad_values[...] = jnp.zeros_like(grad_values)

    @pl.loop(0, tokens // rows)
    def _(i):
        block = chunk(i, rows)
        visible = (place_row[...] >= start[block, :]) & (place_row[...] <= place[block, :])
        visible = jnp.concatenate([visible] * group, axis=0)
        for half in range(halves):
            own = span(half, HEAD_DIM)
            heads = range(half * group, (half + 1) * group)
            query = jnp.concatenate([queries[block, span(h, HEAD_DIM)] for h in heads], axis=0)
            grad = jnp.concatenate([grad_mixed[block, span(h, HEAD_DIM)] for h in heads], axis=0)
            log_total = jnp.concatenate([spread[block, h : h + 1] for h in heads], axis=0)
            scores = dot_cols(query, keys[:, own]) * SCALE
            scores = jnp.where(visible, scores, -1e30)
            probs = jnp.exp(scores - log_total)
            grad_probs = dot_cols(grad, values[:, own])
            weighted = jnp.sum(probs * grad_probs, axis=-1, keepdims=True)
            grad_scores = (probs * (grad_probs - weighted)).astype(low)
            grad_query = dot(grad_scores, keys[:, own]) * SCALE
            for g, head in enumerate(heads):
                grad_queries[block, span(head, HEAD_DIM)] = grad_query[span(g, rows)]
            grad_keys[:, own] += dot_rows(grad_scores, query) * SCALE
            grad_values[:, own] += dot_rows(probs.astype(low), grad)

    total_query = jnp.zeros((1, HEAD_DIM), f32)
    total_key = jnp.zeros((1, HEAD_DIM), f32)
    for half in range(halves):
        base = half * step
        own = span(half, HEAD_DIM)
        for g in range(group + 1):
            at = slice(base + g * HEAD_DIM, base + (g + 1) * HEAD_DIM)
            if g < group:
                grad, gain = grad_queries[:, span(half * group + g, HEAD_DIM)], query_gain[...]
            else:
                grad, gain = grad_keys[:, own], key_gain[...]
            grad = turn_back(grad, cosine[...], sine[...])
            grad, grad_gain = rms_back(raw[:, at], gain, grad)
            grad_raw[:, at] = grad.astype(low)
            if g < group:
                total_query += grad_gain
            else:
                total_key += grad_gain
        at = base + (group + 1) * HEAD_DIM
        grad_raw[:, at : at + HEAD_DIM] = grad_values[:, own].astype(low)
    grad_query_gain[...] = total_query
    grad_key_gain[...] = total_key
    for z in range(depth):
        total = None
        for half, weight in enumerate((own_weight, far_weight)):
            for j, at in enumerate((0, part + GAIN_ROWS)):
                grad = grad_raw[:, span(2 * half + j, LANES)]
                term = dot_cols(grad, weight[z, at : at + part, :])
                total = term if total is None else total + term
        if dealt:
            total = dot(chosen[...], total.astype(low))
        deal_out(parts, span(z, part), total)


def weight_grads_kernel(part, strided, index, left, grads, inner, branch, own, far, *refs):
    *rows_out, turned = refs
    depth = own.shape[0]
    chunks = grads.shape[1] // (2 * LANES)
    size = inner.shape[1] // 2
    for z in range(depth):
        turned[span(z, part), :] = left[:, span(z, part)].T
    for half, target in enumerate((own, far)):
        for j in range(chunks):
            total = dot(turned[...], grads[:, span(half * chunks + j, LANES)])
            for z in range(depth):
                target[z, span(j, part), :] = total[span(z, part)].astype(target.dtype)
    for half in range(2):
        rows = inner[:, span(half, size)].T
        for j in range(branch.shape[1] // LANES):
            total = dot(rows, branch[:, span(j, LANES)])
            if strided:
                share = size // (depth // 2)
                carried = share // 2
                at = slice(chunks * part + j * carried, chunks * part + (j + 1) * carried)
                for i in range(depth // 2):
                    z = (index[1] ^ half) * (depth // 2) + i
                    block = total[span(i, share)]
                    one, two = block[:carried], block[carried:]
                    own[z, at, :] = jnp.where(index[1] == 0, one, two)
                    far[z, at, :] = jnp.where(index[1] == 0, two, one).astype(far.dtype)
            else:
                target = rows_out[half]
                count = target.shape[0]
                share = size // count
                for k in range(count):
                    target[k, span(j, share), :] = total[span(k, share)].astype(target.dtype)


def sum_kernel(own, recv, total):
    total[...] = (own[...] + recv[...].astype(f32)).astype(low)


def meet_kernel(index, own, recv, own_rows, recv_rows, total, *rows):
    total[...] = (own[...] + recv[...].astype(f32)).astype(low)
    for k, row in enumerate(rows):
        at = index[0] ^ k
        row[...] = (own_rows[at] + recv_rows[at].astype(f32)).astype(low)


def layout_kernel(index, total, gains, far_gains, *refs):
    *rows, out = refs
    at = total.shape[1]
    end = at + rows[0].shape[0]
    out[:, :at, :] = total[...]
    for k, row in enumerate(rows):
        out[index[0] ^ k, at:end, :] = row[...]
    out[:, end:, :] = (gains[...] + far_gains[...]).astype(low)


def shards(
    stream_in,
    lengths,
    dealing,
    attention_gain,
    query_weight,
    key_weight,
    value_weight,
    query_gain,
    key_gain,
    out_weight,
    mlp_gain,
    gate_weight,
    up_weight,
    down_weight,
):
    core = lax.axis_index("section")
    piece = lax.axis_index("ctx")
    count = lax.axis_size("ctx")
    depth = lax.axis_size("fsdp")
    rows, width = stream_in.shape[3], stream_in.shape[4]
    tokens = rows * count
    first = core == 0
    query_half = query_weight.shape[2] // (2 * count)
    key_half = key_weight.shape[2] // (2 * count)
    hidden_half = gate_weight.shape[2] // (2 * count)
    part = query_weight.shape[1]
    aligned = depth == count == 4
    out_share, down_share = query_half // count, hidden_half // count
    index = jnp.stack([piece, core]).astype(jnp.int32)
    chunks = width // LANES
    qkv_rows = 2 * part + GAIN_ROWS
    lift_rows = 2 * hidden_half // LANES * part

    own = lax.dynamic_index_in_dim(stream_in[0, 0], core, 0, keepdims=False)
    other = swap(lax.dynamic_index_in_dim(stream_in[0, 0], 1 - core, 0, keepdims=False))
    entering = jnp.where(first, own, other)
    cotangent = jnp.where(first, other, own)

    where = jnp.stack([piece, core]).astype(jnp.int32)

    def cut(kernel, weights, constants, size, after=()):
        def half(i, where):
            return jnp.where(i == 0, 1 - where[1], where[1])

        def columns(i, where):
            return 0, 0, where[0] * 2 + half(i, where)

        def shares(i, where):
            return 0, half(i, where) * count + where[0], 0

        def even(i, where):
            return 0, 0, half(i, where) * 2

        def odd(i, where):
            return 0, 0, half(i, where) * 2 + 1

        def carried(i, where):
            return 0, where[0] * 2 + half(i, where), 0

        maps = {"columns": columns, "shares": shares, "even": even, "odd": odd, "carried": carried}
        in_specs = [
            pl.BlockSpec((1, height, breadth), maps[which]) for _, height, breadth, which in weights
        ]
        in_specs += [pl.BlockSpec(v.shape, lambda i, where: (0, 0)) for v in constants]
        in_specs += [pl.BlockSpec(memory_space=pl.ANY)] * len(after)

        def body(where, *refs):
            kernel(where, *refs[: len(refs) - 1 - len(after)], refs[-1])

        return pl.pallas_call(
            body,
            grid_spec=pltpu.PrefetchScalarGridSpec(
                num_scalar_prefetch=1,
                grid=(2,),
                in_specs=in_specs,
                out_specs=pl.BlockSpec((1, size, LANES), lambda i, where: (i, 0, 0)),
            ),
            out_shape=jax.ShapeDtypeStruct((2, size, LANES), low),
            compiler_params=pltpu.CompilerParams(vmem_limit_bytes=VMEM_LIMIT),
            cost_estimate=pl.CostEstimate(
                flops=int(3 * FLOPS_PER_US), bytes_accessed=12 * size * LANES, transcendentals=0
            ),
        )(where, *[weight for weight, *_ in weights], *constants, *after)

    def place_shares(weight, out, at):
        share = weight.shape[1]
        for j in range(chunks):
            out[0, at + j * share : at + (j + 1) * share, :] = weight[0, :, span(j, LANES)].astype(low)

    def qkv_cut_kernel(where, query, key, value, *refs):
        *rest, gains, out = refs
        out[0, :part, :] = query[0].astype(low)
        out[0, part : part + GAIN_ROWS, :] = gains[...]
        at = slice(part + GAIN_ROWS, qkv_rows)
        out[0, at, :key_half] = key[0].astype(low)
        out[0, at, key_half:] = value[0].astype(low)
        if aligned:
            place_shares(rest[0], out, qkv_rows)

    def mlp_cut_kernel(where, gate, up, out):
        both = jnp.concatenate([gate[0].astype(low), up[0].astype(low)], axis=1)
        for j in range(2 * hidden_half // LANES):
            out[0, span(j, part), :] = both[:, span(j, LANES)]

    def strided_cut_kernel(where, gate, gate_next, up, up_next, down, out):
        share = hidden_half // 2

        for c in range(count):

            @pl.when(where[0] == c)
            def _(c=c):
                sides = [window(v[0], c * share, share) for v in (gate, gate_next, up, up_next)]
                both = [side_by_side(*sides[:2], share), side_by_side(*sides[2:], share)]
                both = jnp.concatenate(both, axis=1).astype(low)
                for j in range(2 * hidden_half // LANES):
                    out[0, span(j, part), :] = both[:, span(j, LANES)]

        place_shares(down, out, lift_rows)

    gains = (attention_gain[0], mlp_gain[0], query_gain[0], key_gain[0])
    sizes = [gain.shape[0] for gain in gains]
    gain_block = jnp.concatenate(gains).astype(low)
    gain_block = jnp.pad(gain_block, (0, GAIN_ROWS * LANES - gain_block.shape[0]))
    gain_block = gain_block.reshape(GAIN_ROWS, LANES)

    def by_layer(cuts):
        mine, other = cuts[1], swap(cuts[0])
        return jnp.where(first, mine, other), jnp.where(first, other, mine)

    weights = [(query_weight, part, query_half, "columns"), (key_weight, part, key_half, "columns")]
    weights += [(value_weight, part, key_half, "columns")]
    weights += [(out_weight, out_share, width, "shares")] if aligned else []
    size = qkv_rows + (chunks * out_share if aligned else 0)
    cuts = cut(qkv_cut_kernel, weights, [gain_block], size)
    attention_blocks = by_layer(cuts)
    line = jnp.arange(size, dtype=jnp.int32)[:, None]
    gain_rows = (line >= part) & (line < part + GAIN_ROWS)
    attention_blocks = jnp.where(gain_rows, cuts[1], attention_blocks[0]), attention_blocks[1]
    point = mark(attention_blocks[0])
    if aligned:
        block = 2 * hidden_half
        weights = [(gate_weight, part, block, "even"), (gate_weight, part, block, "odd")]
        weights += [(up_weight, part, block, "even"), (up_weight, part, block, "odd")]
        weights += [(down_weight, down_share, width, "carried")]
        size = lift_rows + chunks * down_share
        mlp_blocks = by_layer(cut(strided_cut_kernel, weights, [], size, [point]))
    else:
        weights = [(gate_weight, part, hidden_half, "columns"), (up_weight, part, hidden_half, "columns")]
        mlp_blocks = by_layer(cut(mlp_cut_kernel, weights, [], lift_rows))

    def gathered(block):
        return lax.all_gather(block, "fsdp", axis=0, tiled=False)

    def whole_rows(weight, size):
        full = lax.all_gather(weight[0].astype(low), "fsdp", axis=0, tiled=True)
        full = lax.dynamic_slice_in_dim(full, piece * 2 * size, 2 * size, 0)
        other = swap(full)
        layers = jnp.where(first, full, other), jnp.where(first, other, full)
        own = [lax.dynamic_slice_in_dim(v, core * size, size, 0) for v in layers]
        far = [lax.dynamic_slice_in_dim(v, (1 - core) * size, size, 0) for v in layers]
        return [jnp.concatenate(pair, axis=0) for pair in zip(own, far)]

    def picked_rows(own, first_row):
        size = own.shape[1] - first_row
        kernel = functools.partial(pick_kernel, first_row)
        return call(kernel, [own], [((size, LANES), low)] * count, 1, scalars=[index])

    def split_gains(own):
        found, at = [], 0
        flat = own[:, part : part + GAIN_ROWS].reshape(depth, -1)
        for size in sizes:
            found.append(flat[:, at : at + size].reshape(1, -1).astype(f32))
            at += size
        return found

    lens = lax.dynamic_index_in_dim(lengths[0], core, 0, keepdims=False)
    slots = lax.dynamic_index_in_dim(dealing[0], core, 0, keepdims=False)
    order = jnp.arange(tokens, dtype=jnp.int32)
    natural = ((order // rows) ^ piece) * rows + order % rows
    bounds = jnp.cumsum(lens)
    passed = (bounds[None, :] <= natural[:, None]).astype(jnp.int32)
    start = jnp.sum(passed * lens[None, :], axis=1)
    position = natural - start
    rates = jnp.power(rope_base, jnp.arange(HEAD_DIM // 2, dtype=f32) * (-2.0 / HEAD_DIM))
    phase = position.astype(f32)[:, None] * rates
    cosine, sine = jnp.cos(phase), jnp.sin(phase)
    cosine = jnp.concatenate([cosine, cosine], axis=-1)
    sine = jnp.concatenate([-sine, sine], axis=-1)
    places = [start[:, None], natural[:, None], natural[None, :]]

    wanted = slots.reshape(count, rows)
    wanted = jnp.concatenate(xored([wanted[j] for j in range(count)], piece))
    wanted = ((wanted // rows) ^ piece) * rows + wanted % rows
    chosen = (wanted[:, None] == order[None, :]).astype(low)

    wide, half_wide = (rows, width), (tokens, width)
    heads_wide, hidden_wide = 2 * query_half, 2 * hidden_half

    def add(parts, residual, gain, rounded, sends_rows=False, after=()):
        kernel = functools.partial(add_kernel, count, rounded, sends_rows)
        outputs = [(wide, f32), (wide, low)]
        return call(kernel, [*parts, residual, gain], outputs, 2, after=after)

    def add_back(parts, upstream, middle, gain, rounded, gains=(), after=()):
        packs = aligned and len(gains) > 0
        kernel = functools.partial(add_back_kernel, count, rounded, packs)
        outputs = [(wide, f32), (wide, low), ((1, width), f32)]
        outputs += [((depth, GAIN_ROWS, LANES), f32)] if packs else []
        operands = [*parts, upstream, middle, gain] + (list(gains) if packs else [])
        return call(kernel, operands, outputs, 2, after=after)

    def attention_forward(pieces, weights, found, raw_rows, after=()):
        kernel = functools.partial(attention_forward_kernel, count, part, raw_rows)
        outputs = [(half_wide, low), ((tokens, 2 * (query_half + 2 * key_half)), f32)]
        outputs += [((tokens, heads_wide), low), ((tokens, 2 * key_half), low)]
        outputs += [((tokens, heads_wide), low), ((tokens, heads_wide // HEAD_DIM), f32)]
        operands = [*pieces] + ([found[0], chosen] if raw_rows else [])
        outputs += [(wide, low)] if raw_rows else []
        operands += [*weights, cosine, sine, found[2], found[3], *places]
        return call(kernel, operands, outputs, 6.0, [((tokens, 2 * key_half), low)], after=after)

    def rows_product(form, left, given, dealt=False, after=()):
        kernel = functools.partial(rows_kernel, count, form, dealt)
        outputs = [(wide, low)] * count + [((left.shape[1], width), low)]
        operands = [left] + ([chosen] if dealt else []) + [*given]
        *parts, whole = call(kernel, operands, outputs, 8, scalars=[index], after=after)
        return parts, whole

    def lift_forward(pieces, weights, gain=None, after=()):
        kernel = functools.partial(lift_kernel, count, part, gain is not None)
        outputs = [(half_wide, low)] + [((tokens, hidden_wide), f32)] * 2
        outputs += [((tokens, hidden_wide), low)]
        operands = [*pieces]
        if gain is not None:
            operands += [gain, chosen]
            outputs += [(wide, low)]
        return call(kernel, [*operands, *weights], outputs, 0.6, after=after)

    def mlp_forward(pieces, weights, form, down):
        kernel = functools.partial(mlp_forward_kernel, count, part, form)
        outputs = [(half_wide, low)] + [((tokens, hidden_wide), f32)] * 2
        outputs += [((tokens, hidden_wide), low)] + [(wide, low)] * count
        outputs += [((hidden_wide, width), low)]
        operands = [*pieces, *weights] + ([] if form == "strided" else [down])
        *results, whole = call(kernel, operands, outputs, 8, scalars=[index])
        return results[:4], results[4:], whole

    def mlp_backward(pieces, weights, form, down, kept, after=()):
        kernel = functools.partial(mlp_backward_kernel, count, part, form)
        outputs = [(wide, low)] * count + [(half_wide, low), ((tokens, 2 * hidden_wide), low)]
        outputs += [((hidden_wide, width), low)]
        operands = [*pieces, *weights, kept[1], kept[2]] + ([] if form == "strided" else [down])
        results = call(kernel, operands, outputs, 3.0, scalars=[index], after=after)
        parts, (branch, both, whole) = results[:count], results[count:]
        return parts, branch, both, whole

    def attention_backward(pieces, weights, out, found, kept, dealt=False, after=()):
        kernel = functools.partial(attention_backward_kernel, count, part, dealt)
        normed, raw, queries, keys, mixed, spread = kept
        outputs = [(wide, low)] * count + [(half_wide, low), (raw.shape, low)]
        outputs += [((1, HEAD_DIM), f32)] * 2
        outputs += [(wide, low)] if dealt else []
        scratch = [(queries.shape, low), (keys.shape, low), (queries.shape, f32)]
        scratch += [(keys.shape, f32)] * 2
        operands = [*pieces] + ([chosen] if dealt else [])
        operands += [*weights, out, cosine, sine, found[2], found[3], *places]
        operands += [raw, queries, keys, spread]
        results = call(
            kernel, operands, outputs, 18, scratch, after=after
        )
        parts, (branch, grad_raw, query, key, *rest) = results[:count], results[count:]
        return (parts, branch, grad_raw, (query, key), *rest)

    def weight_grads(left, grads, inner, branch, strided=False, after=()):
        kernel = functools.partial(weight_grads_kernel, part, strided)
        size = grads.shape[1] // (2 * LANES) * part
        row_shape = (count, inner.shape[1] // (2 * count) * chunks, LANES)
        if strided:
            size += row_shape[1]
        outputs = [((depth, size, LANES), f32), ((depth, size, LANES), low)]
        outputs += [] if strided else [(row_shape, f32), (row_shape, low)]
        operands = [left, grads, inner, branch]
        scratch = [((width, tokens), low)]
        return call(kernel, operands, outputs, 3.0, scratch, scalars=[index], after=after)

    if not aligned:
        outs, downs = whole_rows(out_weight, query_half), whole_rows(down_weight, hidden_half)

    def arrived(value, after):
        own = tie(value, after)
        return [own, swap(own)]

    def moving_rows(weights, first_row, whole):
        return met(picked_rows(weights[0], first_row)) if aligned else [whole]

    def with_far(shares):
        return [*shares, *map(swap, shares)] if aligned else shares

    out_form, down_form = ("shares", "strided") if aligned else ("whole", "whole")
    pieces = hops(tie(entering, point))
    cotangents = hops(tie(cotangent, point))
    early = pieces, cotangents, mlp_blocks, attention_blocks[1], chosen, cosine, sine, places
    if aligned:
        pack = lax.axis_index("fsdp")
        out_rows = tie(attention_blocks[0][qkv_rows:], point)
        out_rows = [out_rows] + [
            lax.ppermute(out_rows, "fsdp", [(i, i ^ k) for i in range(depth)]) for k in range(1, depth)
        ]
        out_rows = xored(out_rows, piece ^ pack)
        early = *early, out_rows
        shares = met(out_rows)
    else:
        shares = [outs[0]]
    qkv_first = arrived(gathered(attention_blocks[0][:qkv_rows]), early)
    found_own, found_far = split_gains(qkv_first[0]), split_gains(qkv_first[1])
    found_first = [jnp.where(first, own, far) for own, far in zip(found_own, found_far)]
    found_last = [jnp.where(first, far, own) for own, far in zip(found_own, found_far)]
    kept_attention_first = attention_forward(pieces, qkv_first, found_first, True)
    kept_attention_first, shares = beside(kept_attention_first, shares)
    *kept_attention_first, dealt_entering = kept_attention_first
    parts, out_first = rows_product(out_form, kept_attention_first[4], with_far(shares))
    middle_first, normed = add(met(parts), entering, found_first[1], False)
    pieces = hops(normed)
    lift_first = arrived(gathered(mlp_blocks[0]), pieces)
    kept_mlp_first, parts, down_first = mlp_forward(
        pieces, lift_first, down_form, None if aligned else downs[0]
    )

    hidden_last, normed = add(met(parts), middle_first, found_last[0], True)
    pieces = hops(normed)
    qkv_last = arrived(gathered(attention_blocks[1]), pieces)
    shares = moving_rows(qkv_last, qkv_rows, None if aligned else outs[1])
    kept_attention_last = attention_forward(pieces, qkv_last, found_last, False)
    kept_attention_last, shares = beside(kept_attention_last, shares)
    parts, out_last = rows_product(out_form, kept_attention_last[4], with_far(shares))
    middle_last, sent = add(met(parts), hidden_last, found_last[1], False, True)
    pieces = hops(sent)
    lift_last = arrived(gathered(mlp_blocks[1]), pieces)
    *kept_mlp_last, dealt_middle = lift_forward(pieces, lift_last, found_last[1])

    def meet(grads, swapped):
        own, far, own_rows, far_rows = grads
        if not aligned:
            total = (own + swapped[0].astype(f32)).astype(low)
            return total, [own_rows + swapped[1].astype(f32)]
        outputs = [(own.shape, low)] + [(own_rows.shape[1:], low)] * count
        operands = [own, swapped[0], own_rows, swapped[1]]
        total, *rows_by = call(meet_kernel, operands, outputs, 4, scalars=[index])
        return total, rows_by

    def laid_out(total, rows_by, packed):
        if not aligned:
            return total
        size = total.shape[1] + rows_by[0].shape[0] + GAIN_ROWS
        outputs = [((depth, size, LANES), low)]
        operands = [total, packed[0], swap(packed[0]), *rows_by]
        return call(layout_kernel, operands, outputs, 0.9, scalars=[index])[0]

    def gains_reduced(from_first, from_last):
        def by_pack(gains):
            return jnp.concatenate([gain.reshape(depth, -1) for gain in gains], axis=1)

        one, two = by_pack(from_first), by_pack(from_last)
        total = jnp.where(first, one, two) + swap(jnp.where(first, two, one))
        pack = lax.axis_index("fsdp")
        summed = lax.dynamic_index_in_dim(total, pack, 0)
        for k in range(1, depth):
            sent = lax.dynamic_index_in_dim(total, pack ^ k, 0)
            summed = summed + lax.ppermute(sent, "fsdp", [(i, i ^ k) for i in range(depth)])
        return sum(hops(summed))

    def scattered(operand):
        return lax.psum_scatter(operand, "fsdp", scatter_dimension=0, tiled=False)

    def met_rows(rows_by):
        return met(rows_by) if aligned else rows_by

    def rows_fallback(rest):
        (rest,) = rest
        share = rest.shape[1] // chunks
        rest = rest.reshape(count, chunks, share, LANES).swapaxes(1, 2).reshape(-1, width)
        full = jnp.zeros((2 * count * rest.shape[0], width), low)
        at = (piece * 2 + core) * rest.shape[0]
        full = lax.dynamic_update_slice_in_dim(full, rest.astype(low), at, 0)
        return lax.psum(lax.psum_scatter(full, "fsdp", scatter_dimension=0, tiled=True), "ctx")

    def returned(pieces, layer):
        own = jnp.stack(pieces)
        return own, lax.ppermute(own, "section", [(1 - layer, layer)])

    def mlp_meet(grads, swapped):
        if aligned:
            return call(sum_kernel, [grads[0], swapped[0]], [(grads[0].shape, low)], 2)
        return meet(grads, swapped)

    down_whole = None if aligned else downs[1]
    parts, branch, both, whole = mlp_backward(cotangents, lift_last, down_form, down_whole, kept_mlp_last)
    mlp_grads = weight_grads(kept_mlp_last[0], both, kept_mlp_last[3], branch, aligned)
    last_parts, unused = rows_product("whole", kept_mlp_last[3], [whole], True, after=[both])
    (mlp_grads, last_parts), parts = beside((mlp_grads, last_parts), met(parts))
    swapped = [swap(v) for v in mlp_grads[1::2]]
    grad, sent, mlp_gain = add_back(parts, cotangent, middle_last, found_last[1], False)
    (total, *down_rows), pieces = beside(mlp_meet(mlp_grads, swapped), hops(sent))
    mlp_last = scattered(total)

    results = attention_backward(
        pieces, qkv_last, out_last, found_last, kept_attention_last, after=[mark(total)]
    )
    results, last_parts = beside(results, met(tie(last_parts, pieces[1])))
    parts, branch, grad_raw, head_gains = results
    last = dealt_middle.astype(f32)
    for value in last_parts:
        last = last + value.astype(f32)
    last = last.astype(low)
    attention_grads = weight_grads(kept_attention_last[0], grad_raw, kept_attention_last[4], branch)
    attention_grads, parts = beside(attention_grads, met(parts))
    swapped = swap(attention_grads[1]), swap(attention_grads[3])
    grad, sent, gain, *packed = add_back(
        parts, grad, hidden_last, found_last[0], True, (mlp_gain, *head_gains)
    )
    gains_last = (gain, mlp_gain, *head_gains)
    down_grad_last = None if aligned else rows_fallback(*down_rows)
    total, out_rows = meet(attention_grads, swapped)
    moved, pieces = beside(met_rows(out_rows), hops(sent))
    operand, mlp_last = beside(laid_out(total, moved, packed), mlp_last)
    attention_last = scattered(operand)

    near = [hop(mlp_last, k) for k in range(1, count - 1)]
    results = mlp_backward(
        pieces, lift_first, "whole", down_first, kept_mlp_first, after=[mark(operand, mlp_last)]
    )
    parts, branch, both, unused = results
    mlp_grads = weight_grads(kept_mlp_first[0], both, kept_mlp_first[3], branch, aligned)
    mlp_grads, parts = beside(mlp_grads, met(parts))
    out_grad_last = None if aligned else rows_fallback(out_rows)
    swapped = [swap(v) for v in mlp_grads[1::2]]
    grad, sent, mlp_gain = add_back(parts, grad, middle_first, found_first[1], False)
    (total, *down_rows), pieces = beside(mlp_meet(mlp_grads, swapped), hops(sent))
    total, attention_last = beside(total, attention_last)
    mlp_first = scattered(total)

    attention_last = tie(attention_last, pieces[1])
    near_last = [hop(attention_last, k) for k in range(1, count - 1)]
    results = attention_backward(
        pieces,
        qkv_first,
        out_first,
        found_first,
        kept_attention_first,
        True,
        after=[mark(total, attention_last)],
    )
    results, near, near_last = lax.optimization_barrier((results, near, near_last))
    parts, branch, grad_raw, head_gains, dealt_branch = results
    grads = weight_grads(kept_attention_first[0], grad_raw, kept_attention_first[4], branch)
    swapped = swap(grads[1]), swap(grads[3])
    grads, parts = beside(grads, met(parts))
    held = grads[0], grads[2]
    unused, grad, gain, *packed = add_back(
        parts, dealt_branch, dealt_entering, found_first[0], True, (mlp_gain, *head_gains)
    )
    down_grad_first = None if aligned else rows_fallback(*down_rows)
    total, out_rows = meet((held[0], grads[1], held[1], grads[3]), swapped)
    moved, mlp_first = beside(met_rows(out_rows), mlp_first)
    operand = laid_out(total, moved, packed)
    out_grad_first = None if aligned else rows_fallback(out_rows)
    gains_first = (gain, mlp_gain, *head_gains)
    attention_first = scattered(operand)
    point = mark(operand)
    sums = None if aligned else gains_reduced(gains_first, gains_last)
    mlp_last = [mlp_last, *near, hop(tie(mlp_last, parts), count - 1)]
    attention_last = [attention_last, *near_last, hop(tie(attention_last, point), count - 1)]
    mlp_first = hops(tie(mlp_first, point))
    mlp_last, attention_last = returned(mlp_last, 1), returned(attention_last, 1)
    attention_first = hops(tie(attention_first, mlp_first))
    mlp_first = returned(mlp_first, 0)
    own = jnp.where(first, grad, last)
    other = swap(jnp.where(first, last, grad))
    boundary = jnp.where(first, jnp.stack([own, other]), jnp.stack([other, own]))

    def settle(kernel, from_first, from_last, outputs, at_once=1, after=()):
        size = from_first[0].shape[1]

        def block_of(layer):
            def at(i, where):
                return jnp.where(where[1] == layer, i ^ (where[0] // at_once), 0), 0, 0

            return pl.BlockSpec((at_once, size, LANES), at)

        def body(where, *refs):
            kernel(where, *refs[:4], *refs[4 + len(after) :])

        return pl.pallas_call(
            body,
            grid_spec=pltpu.PrefetchScalarGridSpec(
                num_scalar_prefetch=1,
                grid=(count // at_once,),
                in_specs=[block_of(0), block_of(0), block_of(1), block_of(1)]
                + [pl.BlockSpec(memory_space=pl.ANY)] * len(after),
                out_specs=[
                    pl.BlockSpec(block, functools.partial(lambda at, i, where: at(i), at))
                    for _, block, at in outputs
                ],
            ),
            out_shape=[jax.ShapeDtypeStruct(shape, f32) for shape, _, _ in outputs],
            compiler_params=pltpu.CompilerParams(vmem_limit_bytes=VMEM_LIMIT),
            cost_estimate=pl.CostEstimate(
                flops=0, bytes_accessed=12 * count * size * LANES, transcendentals=0
            ),
        )(where, *from_first, *from_last, *after)

    def halves_of(where, blocks, body):
        @pl.when(where[1] == 0)
        def _():
            body(0, blocks[0])
            body(1, blocks[1])

        @pl.when(where[1] == 1)
        def _():
            body(1, blocks[2])
            body(0, blocks[3])

    def place_rows(block, at, half, out):
        share = out.shape[1]
        for j in range(chunks):
            out[half, :, span(j, LANES)] = block[0, at + j * share : at + (j + 1) * share, :].astype(f32)

    def mlp_settle_kernel(where, *refs):
        blocks, (gate, up) = refs[:4], refs[4:]

        def body(half, block):
            both = [block[0, span(j, part), :].astype(f32) for j in range(2 * hidden_half // LANES)]
            both = jnp.concatenate(both, axis=1)
            gate[:, span(half, hidden_half)] = both[:, :hidden_half]
            up[:, span(half, hidden_half)] = both[:, hidden_half:]

        halves_of(where, blocks, body)

    def strided_settle_kernel(where, *refs):
        blocks, (gate, up, down) = refs[:4], refs[4:]
        share = hidden_half // 2
        step = pl.program_id(0)

        def body(half, block):
            pair = []
            for side in range(2):
                at = (where[0] % 2) ^ side
                both = [block[at, span(j, part), :].astype(f32) for j in range(2 * hidden_half // LANES)]
                pair.append(jnp.concatenate(both, axis=1))
                for j in range(chunks):
                    rows_at = slice(lift_rows + j * down_share, lift_rows + (j + 1) * down_share)
                    down[2 * side + half, :, span(j, LANES)] = block[at, rows_at, :].astype(f32)
            for target, start in ((gate, 0), (up, hidden_half)):
                for i in range(2):
                    sides = [window(v[:, start : start + hidden_half], i * share, share) for v in pair]
                    to = (2 * half + i) * 2 * hidden_half + step * hidden_half
                    to = pl.ds(pl.multiple_of(to, 128), hidden_half)
                    target[:, to] = side_by_side(*sides, share)

        halves_of(where, blocks, body)

    def attention_settle_kernel(where, *refs):
        blocks, (query, key, value, *out) = refs[:4], refs[4:]
        if aligned:

            @pl.when(pl.program_id(0) == 0)
            def _():
                out[1][...] = jnp.zeros_like(out[1])

        def body(half, block):
            query[:, span(half, query_half)] = block[0, :part, :].astype(f32)
            both = block[0, part : 2 * part, :].astype(f32)
            key[:, span(half, key_half)] = both[:, :key_half]
            value[:, span(half, key_half)] = both[:, key_half:]
            if aligned:
                place_rows(block, 2 * part, half, out[0])
                if half == 0:
                    out[1][...] += block[0, 2 * part + chunks * out_share :, :].astype(f32)

        halves_of(where, blocks, body)

    def column_output(size):
        return ((part, 2 * count * size), (part, 2 * size), lambda i: (0, i))

    def row_output(size):
        return ((2, size, width), (2, size // count, width), lambda i: (0, i, 0))

    if aligned:
        whole_columns = (part, 2 * count * hidden_half)
        outputs = [(whole_columns, whole_columns, lambda i: (0, 0))] * 2
        outputs += [((2 * count, down_share, width), (count, down_share, width), lambda i: (i, 0, 0))]
        settled = settle(strided_settle_kernel, mlp_first, mlp_last, outputs, 2, [other])
    else:
        settled = settle(mlp_settle_kernel, mlp_first, mlp_last, [column_output(hidden_half)] * 2)
    (grad_gate, grad_up, *grad_down), attention_first = beside(settled, attention_first)
    outputs = [column_output(query_half)] + [column_output(key_half)] * 2
    if aligned:
        outputs += [row_output(query_half)]
        outputs += [((GAIN_ROWS, LANES), (GAIN_ROWS, LANES), lambda i: (0, 0))]
    grad_query, grad_key, grad_value, *grad_out = settle(
        attention_settle_kernel, returned(attention_first, 0), attention_last, outputs
    )
    if aligned:
        sums = grad_out[1]
        at = lax.axis_index("fsdp") * sizes[2]
        head_sums = [lax.dynamic_slice_in_dim(sums[2:3], at + k * HEAD_DIM, sizes[2], 1) for k in range(2)]
        split = [sums[0:1], sums[1:2], *head_sums]
    else:
        split, at = [], 0
        for size in sizes:
            split.append(sums[:, at : at + size])
            at += size

    if aligned:
        grad_out, grad_down = grad_out[0].reshape(-1, width), grad_down[0].reshape(-1, width)
    else:
        pair = []
        for one, two in ((out_grad_first, out_grad_last), (down_grad_first, down_grad_last)):
            own = jnp.where(first, one, two).astype(f32)
            pair.append(own + swap(jnp.where(first, two, one)).astype(f32))
        grad_out, grad_down = pair
    return (
        boundary[None, None],
        split[0],
        grad_query[None],
        grad_key[None],
        grad_value[None],
        split[2],
        split[3],
        grad_out[None],
        split[1],
        grad_gate[None],
        grad_up[None],
        grad_down[None],
    )


def solution(mesh):
    weight, gain, row = P("section", "fsdp", None), P("section", "fsdp"), P("fsdp", None, None)
    stream = P("section", "fsdp", None, "ctx", None)
    masters = (gain, weight, weight, weight, gain, gain, weight, gain, weight, weight, weight)
    return jax.shard_map(
        shards,
        mesh=mesh,
        in_specs=(stream, row, row) + masters,
        out_specs=(stream,) + masters,
        check_vma=False,
    )
```
